128 devices in a mesh: dp: 32 (over y, x, core), expert: 4 (over z).
Axes of the slice: x: 4, y: 4, z: 4, core: 2. Of those that a mesh axis runs over, the one named last changes fastest.
Arguments:
- tokens: bfloat16 [32768, 1024], P(('dp', 'expert')), may hold values from -6 to 6
- out_grad: bfloat16 [32768, 1024], P(('dp', 'expert')), may hold values from -6 to 6
- gate: float32 [32768], P(('dp', 'expert')), may hold values from 0.2 to 1
- region: int32 [32768, 1], P(('dp', 'expert')), may hold values from 0 to 3; in each aligned block of 256 rows (0 to 255, 256 to 511, ...) at most 128 rows name the same one
- w_in: bfloat16 [4, 4096, 1024], P('expert'), may hold values from -0.1875 to 0.1875
- w_out: bfloat16 [4, 4096, 1024], P('expert'), may hold values from -0.09375 to 0.09375
Outputs:
- token_grad: bfloat16 [32768, 1024], P(('dp', 'expert'))
- w_in_grad: float32 [4, 4096, 1024], P('expert', 'dp')
- w_out_grad: float32 [4, 4096, 1024], P('expert', 'dp')
The draws below stay inside these ranges and needn't reach their ends.
Inputs may be any that keep to these rules, and one draw needn't show every extreme that they name: `region`: of the 256 rows of one device, at most 128 name the same expert, and in every draw some device has exactly 128 rows for some expert.
All inputs are finite; a program needn't handle non-finite values.
Results may differ from the reference program's by a relative error of at most 0.02.
Values may be sent and summed in bfloat16 or wider, within the bound.
No kernel may reach another device: no remote copies, remote signals or barrier semaphores. Data moves between devices by JAX's collectives and lax.ppermute only.
A program may use at most 128 MiB of HBM per device.

```python
import math
import jax
import jax.numpy as jnp
import numpy as np
from jax import lax

D = 1024
FF = 4096
TOK_DEV = 256
EXPERTS = 4
CAP = 128
TOKENS = 32768
N_DP = 32
N_EXPERT = 4


def level_of(key, shape, cuts, smallest, high):
    loudness, own = 1.0, jax.random.fold_in(key, 6)
    for axis_at, shards_of in cuts:
        draws = jnp.exp(jax.random.uniform(jax.random.fold_in(own, axis_at), (shards_of,), jnp.float32, smallest / len(cuts), high / len(cuts)))
        loudness = loudness * jnp.repeat(draws, shape[axis_at] // shards_of).reshape([-1 if axis == axis_at else 1 for axis in range(len(shape))])
    return loudness


def routed_block(rng, own, number, rows, amount, top, reach, slope):
    order = jax.random.permutation(rng, amount)
    heavy_load, usual = shares(amount, rows * top, reach, slope, True), shares(amount, rows * top, reach, slope, False)
    places = jnp.arange(amount)

    def named(tallies, offset_by):
        used = int((tallies > 0).sum())
        fixed = max(1, used // 4)
        passed = fixed + (places - fixed + offset_by * (used - fixed)) % max(1, amount - fixed)
        return jnp.zeros((amount,), jnp.int32).at[order[jnp.where(places < fixed, places, passed)]].set(jnp.asarray(tallies, jnp.int32))

    tallies = jnp.where(number % 4 == 0, named(heavy_load, number // 4), named(usual, number - number // 4 - 1))
    mixed = jax.random.permutation(jax.random.fold_in(own, 3), amount)
    giver, sink = mixed[0:amount // 2 * 2:2], mixed[1:amount // 2 * 2:2]
    margin = jnp.minimum(tallies[giver] - 1, reach - tallies[sink]) // 2
    margin = jnp.where((giver == order[0]) | (sink == order[0]) | (tallies[sink] == 0), 0, jnp.maximum(margin, 0))
    passed = jax.random.randint(jax.random.fold_in(own, 4), (amount // 2,), 0, 1 << 20) % (margin + 1)
    tallies = tallies.at[giver].add(-passed).at[sink].add(passed)
    items = jnp.searchsorted(jnp.cumsum(tallies), jnp.arange(rows * top), side="right").astype(jnp.int32)
    table = items.reshape(top, rows).T
    table = table[jax.random.permutation(jax.random.fold_in(own, 1), rows)]
    offset_by = jax.random.randint(jax.random.fold_in(own, 2), (rows, 1), 0, top)
    return jnp.take_along_axis(table, (jnp.arange(top)[None, :] + offset_by) % top, axis=1)


def shares(amount, total, most, lean, full):
    portions = [(1 << 20) // math.isqrt(standing ** lean) + 1 for standing in range(1, amount + 1)]
    largest = most if full else min(most, max(-(-total // amount), total * portions[0] // sum(portions)))
    least = 1 if total - largest >= amount - 1 else 0
    counts, rest = [largest] + [least] * (amount - 1), total - largest - least * (amount - 1)
    while rest > 0:
        free = [i for i in range(1, amount) if counts[i] < largest] or [i for i in range(1, amount) if counts[i] < most]
        whole, left = sum([portions[i] for i in free]), rest
        for i in free:
            extra = min(most - counts[i], max(1, left * portions[i] // whole), rest)
            counts[i] = counts[i] + extra
            rest = rest - extra
    return np.array(counts)


def normal_values(rng, dims, spread, most, split=(), kind=jnp.bfloat16):
    entries = spread * jax.random.normal(rng, dims, jnp.float32)
    if split:
        entries = entries * level_of(rng, dims, split, -0.22, 0.18)
    return jnp.clip(entries, -most, most).astype(kind)


def setup_inputs(seed: int = 0) -> dict:
    arg_keys = jax.random.split(jax.random.key(seed), 7)
    tokens = normal_values(arg_keys[0], (TOKENS, D), 1.0, 6.0, ((0, 128),))
    out_grad = normal_values(arg_keys[1], (TOKENS, D), 1.0, 6.0, ((0, 128),))
    gate = jnp.clip(0.2 + 0.8 * jax.random.uniform(arg_keys[2], (TOKENS,), jnp.float32) ** level_of(arg_keys[2], (TOKENS,), ((0, 128),), -0.2, 0.2), 0.2, 1.0)
    region_keys = jax.random.split(jax.random.fold_in(arg_keys[3], 1), TOKENS // TOK_DEV)
    region_turns = jax.random.permutation(jax.random.fold_in(arg_keys[3], 3), TOKENS // TOK_DEV)
    region = jax.vmap(lambda own, number: routed_block(jax.random.fold_in(arg_keys[3], 2), own, number, TOK_DEV, EXPERTS, 1, CAP, 2))(region_keys, region_turns).reshape((TOKENS, 1))
    w_in = normal_values(arg_keys[4], (EXPERTS, FF, D), D ** -0.5, 0.1875, ((0, 4),))
    w_out = normal_values(arg_keys[5], (EXPERTS, FF, D), FF ** -0.5, 0.09375, ((0, 4),))
    return {"tokens": tokens, "out_grad": out_grad, "gate": gate, "region": region, "w_in": w_in, "w_out": w_out}


def gelu_parts(pre_act):
    root_two_pi = 0.7978845608028654
    cubic = pre_act * pre_act * pre_act
    tanh_val = jnp.tanh(root_two_pi * (pre_act + 0.044715 * cubic))
    halved = 0.5 * (1.0 + tanh_val)
    gelu_value = pre_act * halved
    gelu_slope = halved + 0.5 * pre_act * (1.0 - tanh_val * tanh_val) * root_two_pi * (1.0 + 3.0 * 0.044715 * pre_act * pre_act)
    return (gelu_value, gelu_slope)

def reference(tokens, out_grad, gate, region, w_in, w_out):
    scaled = (gate[:, None] * out_grad.astype(jnp.float32)).astype(jnp.bfloat16)
    region_ids = region[:, 0].astype(jnp.int32)
    block_len = N_EXPERT * TOK_DEV
    window_rows = N_EXPERT * CAP
    grad_scale = 1.0 / math.sqrt(float(TOKENS // EXPERTS))

    def one_expert(running, expert_id):
        weight_in = w_in[expert_id]
        weight_out = w_out[expert_id]

        def one_group(carry, group_id):
            tok_acc, acc_in, acc_out = carry
            base = (group_id * block_len).astype(jnp.int32)
            block_ids = lax.dynamic_slice(region_ids, (base,), (block_len,))
            local_order = jnp.argsort(block_ids, stable=True).astype(jnp.int32)
            count = jnp.sum((block_ids == expert_id).astype(jnp.int32)).astype(jnp.int32)
            start = jnp.sum((block_ids < expert_id).astype(jnp.int32)).astype(jnp.int32)
            order_pad = jnp.concatenate([local_order, jnp.zeros((window_rows,), jnp.int32)]).astype(jnp.int32)
            picked = (lax.dynamic_slice(order_pad, (start,), (window_rows,)) + base).astype(jnp.int32)
            is_kept = (jnp.arange(window_rows, dtype=jnp.int32) < count)[:, None]
            inputs_win = jnp.where(is_kept, tokens[picked], jnp.zeros((), tokens.dtype))
            grads_win = jnp.where(is_kept, scaled[picked], jnp.zeros((), scaled.dtype))
            pre_act = lax.dot_general(inputs_win, weight_in, (((1,), (1,)), ((), ())), preferred_element_type=jnp.float32)
            gelu_value, gelu_slope = gelu_parts(pre_act)
            activation = gelu_value.astype(jnp.bfloat16)
            act_grad = lax.dot_general(grads_win, weight_out, (((1,), (1,)), ((), ())), preferred_element_type=jnp.float32)
            pre_grad = (act_grad * gelu_slope).astype(jnp.bfloat16)
            row_grads = jnp.dot(pre_grad, weight_in, preferred_element_type=jnp.float32).astype(jnp.bfloat16)
            part_in = lax.dot_general(pre_grad, inputs_win, (((0,), (0,)), ((), ())), preferred_element_type=jnp.float32).astype(jnp.bfloat16)
            part_out = lax.dot_general(activation, grads_win, (((0,), (0,)), ((), ())), preferred_element_type=jnp.float32).astype(jnp.bfloat16)
            tok_acc = tok_acc.at[picked].add(jnp.where(is_kept, row_grads, jnp.zeros((), row_grads.dtype)))
            acc_in = acc_in + part_in.astype(jnp.float32)
            acc_out = acc_out + part_out.astype(jnp.float32)
            return ((tok_acc, acc_in, acc_out), None)
        zeros_grad = jnp.zeros((FF, D), jnp.float32)
        (running, acc_in, acc_out), unused = lax.scan(one_group, (running, zeros_grad, zeros_grad), jnp.arange(N_DP, dtype=jnp.int32))
        return (running, (acc_in * grad_scale, acc_out * grad_scale))
    token_grad, (w_in_grad, w_out_grad) = lax.scan(one_expert, jnp.zeros(tokens.shape, jnp.bfloat16), jnp.arange(EXPERTS, dtype=jnp.int32))
    return (token_grad, w_in_grad, w_out_grad)
```

```python
import math

import jax
import jax.numpy as jnp
from jax import lax
from jax.experimental import pallas as pl
from jax.experimental.pallas import tpu as pltpu
from jax.sharding import Mesh, PartitionSpec as P

BF16 = jnp.bfloat16
F32 = jnp.float32
VMEM_LIMIT = 44 * 1024 * 1024
ORDER = (2, 1, 3, 0)
INVERSE = (3, 1, 0, 2)


def ring(step):
    return [(i, (i + step) % 4) for i in range(4)]


def swap_core(array):
    return lax.ppermute(array, "core", [(0, 1), (1, 0)])


def params():
    return pltpu.CompilerParams(vmem_limit_bytes=VMEM_LIMIT)


def cost(nbytes=1024):
    return pl.CostEstimate(flops=0, bytes_accessed=int(nbytes), transcendentals=0)


def shape(rows, cols, dtype=BF16):
    return jax.ShapeDtypeStruct((rows, cols), dtype)


def dot_nt(a, b):
    return lax.dot_general(a, b, (((1,), (1,)), ((), ())), preferred_element_type=F32)


def dot_nn(a, b):
    return lax.dot_general(a, b, (((1,), (0,)), ((), ())), preferred_element_type=F32)


def dot_tn(a, b):
    return lax.dot_general(a, b, (((0,), (0,)), ((), ())), preferred_element_type=F32)


def gelu_parts(pre_act):
    root_two_pi = 0.7978845608028654
    square = pre_act * pre_act
    inner = pre_act * (root_two_pi + root_two_pi * 0.044715 * square)
    halved = 0.5 + 0.5 * jnp.tanh(inner)
    value = pre_act * halved
    slope_of_inner = 2.0 * root_two_pi + 6.0 * root_two_pi * 0.044715 * square
    return value, halved + value * (1.0 - halved) * slope_of_inner


VMEM = pl.BlockSpec(memory_space=pltpu.VMEM)
ANY = pl.BlockSpec(memory_space=pl.ANY)


def dispatch_tokens(region, tokens):
    n, width = tokens.shape

    def body(region_ref, tok_ref, place_ref, out_ref):
        dest = region_ref[...]
        onehot = (dest == lax.broadcasted_iota(jnp.int32, (8, n), 0)).astype(F32)
        upper = (
            lax.broadcasted_iota(jnp.int32, (n, n), 0) < lax.broadcasted_iota(jnp.int32, (n, n), 1)
        ).astype(F32)
        before = dot_nn(onehot.astype(BF16), upper.astype(BF16))
        rank = jnp.sum(before * onehot, axis=0, keepdims=True).astype(jnp.int32)
        slot = dest * 128 + rank
        place = (slot == lax.broadcasted_iota(jnp.int32, (512, n), 0)).astype(F32).astype(BF16)
        place_ref[...] = place
        out_ref[...] = dot_nn(place, tok_ref[...]).astype(BF16)

    return pl.pallas_call(
        body,
        out_shape=[shape(512, n), shape(512, width)],
        in_specs=[VMEM] * 2,
        out_specs=[VMEM] * 2,
        compiler_params=params(),
        cost_estimate=cost(4 * n * width * 2),
    )(region, tokens)


def dispatch_grads(place, gate, grads):
    n, width = grads.shape

    def body(place_ref, gate_ref, grad_ref, out_ref):
        column = jnp.transpose(jnp.broadcast_to(gate_ref[...], (128, n)))[:, :1]
        scaled = (column * grad_ref[...].astype(F32)).astype(BF16)
        out_ref[...] = dot_nn(place_ref[...], scaled).astype(BF16)

    return pl.pallas_call(
        body,
        out_shape=shape(512, width),
        in_specs=[VMEM] * 3,
        out_specs=VMEM,
        compiler_params=params(),
        cost_estimate=cost(4 * n * width * 2),
    )(place, gate, grads)


HBM = pl.BlockSpec(memory_space=pltpu.HBM)


def weight_scratch(width, count):
    return [pltpu.VMEM((512 * count, width), BF16), pltpu.SemaphoreType.DMA((4 * count,))]


def weight_group(table_ref, weight_ref, w_buf, sems, offset, count):
    step = pl.program_id(0)

    def fetch(k):
        block = pl.multiple_of(table_ref[offset + k] * 128, 128)
        place = pl.multiple_of(k * 128, 128)
        return pltpu.make_async_copy(
            weight_ref.at[pl.ds(block, 128), :], w_buf.at[pl.ds(place, 128), :], sems.at[k]
        )

    @pl.when(step == 0)
    def _():
        for k in range(4 * count):
            fetch(k).start()

    for q in range(4):
        fetch(4 * step + q).wait()
    return w_buf.at[pl.ds(pl.multiple_of(step * 512, 512), 512), :]


def after(array, *others):
    def body(*refs):
        del refs

    return pl.pallas_call(
        body,
        in_specs=[ANY] * (1 + len(others)),
        out_specs=ANY,
        out_shape=jax.ShapeDtypeStruct(array.shape, array.dtype),
        input_output_aliases={0: 0},
        compiler_params=params(),
        cost_estimate=cost(),
    )(array, *others)


def columns(halves, c):
    return halves[c // 2][(c % 2) * 256 : (c % 2 + 1) * 256, :]


def forward(table, halves, weight):
    width = weight.shape[1]
    tok = 1024

    def body(table_ref, own_ref, other_ref, weight_ref, first_ref, act_ref, slope_ref, mark_ref, w_buf, sems):
        mark_ref[...] = jnp.zeros_like(mark_ref)
        w_ref = weight_group(table_ref, weight_ref, w_buf, sems, 0, 4)
        for c in range(4):
            cols = slice(c * 256, (c + 1) * 256)
            act, slope = gelu_parts(dot_nt(w_ref[...], columns((own_ref, other_ref), c)))
            slope_ref[:, cols] = slope.astype(BF16)
            act = act.astype(BF16)

            @pl.when(pl.program_id(0) == 0)
            def _():
                first_ref[:, cols] = act

            @pl.when(pl.program_id(0) > 0)
            def _():
                act_ref[:, cols] = act


    return pl.pallas_call(
        body,
        grid_spec=pltpu.PrefetchScalarGridSpec(
            num_scalar_prefetch=1,
            grid=(4,),
            in_specs=[VMEM] * 2 + [HBM],
            out_specs=[
                pl.BlockSpec((512, tok), lambda i, *_: (0, 0)),
                pl.BlockSpec((512, tok), lambda i, *_: (jnp.maximum(i - 1, 0), 0)),
                pl.BlockSpec((512, tok), lambda i, *_: (i, 0)),
            ]
            + [pl.BlockSpec((8, 128), lambda i, *_: (0, 0))],
            scratch_shapes=weight_scratch(width, 4),
        ),
        out_shape=[shape(512, tok), shape(1536, tok), shape(2048, tok), shape(8, 128, F32)],
        compiler_params=params(),
        cost_estimate=cost(2**24),
    )(table, *halves, weight)


def outer(left, halves):
    return dot_nn(left[:, :512], halves[0][...]) + dot_nn(left[:, 512:], halves[1][...])


def outer_products(act, halves, first, count, deps):
    width = halves[0].shape[1]
    split = act.shape[0] == 512

    def body(act_ref, own_ref, other_ref, *refs):
        outs = refs[len(deps) :]
        span = 512 // len(outs)
        for k, out in enumerate(outs):
            out[...] = outer(act_ref[k * span : (k + 1) * span, :], (own_ref, other_ref)).astype(BF16)

    return pl.pallas_call(
        body,
        grid=(count,),
        in_specs=[pl.BlockSpec((512, 1024), lambda i: (i + first, 0))] + [VMEM] * 2 + [ANY] * len(deps),
        out_specs=[pl.BlockSpec((256, width), lambda i: (0, 0))] * 2
        if split
        else pl.BlockSpec((512, width), lambda i: (i, 0)),
        out_shape=[shape(256, width)] * 2 if split else shape(512 * count, width),
        compiler_params=params(),
        cost_estimate=cost(2**20 * (2 + 2 * count)),
    )(act, *halves, *deps)


def backward(table, grads, rows, slope, weight, groups, deps):
    first, count = groups
    width = weight.shape[1]
    tok = 1024
    split = first == 0

    def body(table_ref, d_own, d_other, x_own, x_other, slope_ref, weight_ref, *refs):
        pre_ref, *outs, w_buf, sems, s_buf = refs[len(deps) :]
        step = pl.program_id(0)
        w_ref = weight_group(table_ref, weight_ref, w_buf, sems, 16 + 4 * first, count)
        for q in range(4):
            block = pl.multiple_of(table_ref[32 + 4 * (step + first) + q] * 128, 128)
            s_buf[q * 128 : (q + 1) * 128, :] = slope_ref[pl.ds(block, 128), :]
        for c in range(4):
            cols = slice(c * 256, (c + 1) * 256)
            act_grad = dot_nt(w_ref[...], columns((d_own, d_other), c))
            pre_ref[:, cols] = (act_grad * s_buf[:, cols].astype(F32)).astype(BF16)
        span = 512 // len(outs)
        for k, out in enumerate(outs):
            out[...] = outer(pre_ref[k * span : (k + 1) * span, :], (x_own, x_other)).astype(BF16)

    return pl.pallas_call(
        body,
        grid_spec=pltpu.PrefetchScalarGridSpec(
            num_scalar_prefetch=1,
            grid=(count,),
            in_specs=[VMEM] * 5 + [HBM] + [ANY] * len(deps),
            out_specs=[pl.BlockSpec((512, tok), lambda i, *_: (i, 0))]
            + (
                [pl.BlockSpec((256, width), lambda i, *_: (0, 0))] * 2
                if split
                else [pl.BlockSpec((512, width), lambda i, *_: (i, 0))]
            ),
            scratch_shapes=weight_scratch(width, count) + [pltpu.VMEM((512, tok), BF16)],
        ),
        out_shape=[shape(512 * count, tok)]
        + ([shape(256, width)] * 2 if split else [shape(512 * count, width)]),
        compiler_params=params(),
        cost_estimate=cost(2**20 * (2 + 4 * count)),
    )(table, *grads, *rows, slope, weight, *deps)


def row_gradients(table, pre, weight, deps):
    width = weight.shape[1]
    rows = 512

    def body(table_ref, a_ref, b_ref, c_ref, weight_ref, *refs):
        out_ref, w_buf, sems, total = refs[len(deps) :]
        step = pl.program_id(0)
        w_ref = weight_group(table_ref, weight_ref, w_buf, sems, 16, 4)

        @pl.when(step == 0)
        def _():
            total[...] = dot_tn(a_ref[...], w_ref[...])

        @pl.when(jnp.logical_and(step > 0, step < 3))
        def _():
            begin = pl.multiple_of((step - 1) * 512, 512)
            total[...] += dot_tn(b_ref[pl.ds(begin, 512), :], w_ref[...])

        @pl.when(step == 3)
        def _():
            final = (total[...] + dot_tn(c_ref[...], w_ref[...])).astype(BF16)
            own = table_ref[48]
            out_ref[pl.ds(pl.multiple_of(own * rows, rows), rows), :] = final[:rows]
            out_ref[pl.ds(pl.multiple_of((1 - own) * rows, rows), rows), :] = final[rows:]

    return pl.pallas_call(
        body,
        grid_spec=pltpu.PrefetchScalarGridSpec(
            num_scalar_prefetch=1,
            grid=(4,),
            in_specs=[VMEM] * 3 + [HBM] + [ANY] * len(deps),
            out_specs=pl.BlockSpec((2 * rows, width), lambda i, *_: (0, 0)),
            scratch_shapes=weight_scratch(width, 4) + [pltpu.VMEM((2 * rows, width), F32)],
        ),
        out_shape=shape(2 * rows, width),
        compiler_params=params(),
        cost_estimate=cost(2**23 + 2**22),
    )(table, *pre, weight, *deps)


def restore_order(place, rows):
    n, width = place.shape[1], rows.shape[1]

    def body(place_ref, rows_ref, out_ref):
        out_ref[...] = dot_tn(place_ref[...], rows_ref[...]).astype(BF16)

    return pl.pallas_call(
        body,
        out_shape=shape(n, width),
        in_specs=[VMEM] * 2,
        out_specs=VMEM,
        compiler_params=params(),
        cost_estimate=cost(2**21),
    )(place, rows)


def add(*terms):
    total = terms[0].astype(F32)
    for term in terms[1:]:
        total = total + term.astype(F32)
    return total


def small(array):
    return array[:8, :128]


def both(pair):
    return pair[0][-8:, :128], pair[1][:8, :128]


def first_hop(low, high, axis):
    return lax.ppermute(low, axis, ring(3)), lax.ppermute(high, axis, ring(1))


def join(arrived, following, previous):
    h = following.shape[0] // 2
    from_next, from_prev = arrived
    up = jnp.concatenate([following[:h], add(following[h:], from_prev).astype(BF16)], axis=0)
    down = jnp.concatenate([add(previous[:h], from_next).astype(BF16), previous[h:]], axis=0)
    return up, down


def second_hop(up, down, axis):
    return lax.ppermute(up, axis, ring(1)), lax.ppermute(down, axis, ring(3))


def within(group, axis):
    n = group.shape[0] // 4
    own, following, opposite, previous = (group[k * n : (k + 1) * n] for k in range(4))
    arrived = first_hop(opposite[: n // 2], opposite[n // 2 :], axis)
    return own, *join(arrived, following, previous)


def sum_cores(terms):
    terms = lax.all_to_all(terms, "core", split_axis=0, concat_axis=0, tiled=True)
    n = terms.shape[0] // 2
    return add(terms[:n], terms[n:]).astype(BF16)


def once(index, work, like):
    trips = 1 + jnp.minimum(index, 0)
    return lax.fori_loop(0, trips, lambda _, start: work(start), jnp.zeros_like(like))


def local(tokens, out_grad, gate, region, w_in, w_out):
    x, y, core = (lax.axis_index(a).astype(jnp.int32) for a in ("x", "y", "core"))
    scale = 1.0 / math.sqrt(float(tokens.shape[0] * lax.axis_size(("y", "x", "core"))))
    order = jnp.array(ORDER, jnp.int32)
    every = jnp.arange(4, dtype=jnp.int32)
    by_x = ((((y + every[None, :]) % 4) * 4 + (x + order[:, None]) % 4) * 2 + core).reshape(16)
    by_y = ((((y + order[:, None]) % 4) * 4 + (x + every[None, :]) % 4) * 2 + core).reshape(16)
    same = jnp.array([INVERSE[q] * 4 + ORDER[p] for p in range(4) for q in range(4)], jnp.int32)
    table = jnp.concatenate([by_x, by_y, same, core[None]])
    weight_in, weight_out = w_in[0], w_out[0]

    def exchange(array):
        return lax.all_to_all(array, "expert", split_axis=0, concat_axis=0, tiled=True)

    place, send_x = dispatch_tokens(region.reshape(1, -1), tokens)
    send_d = dispatch_grads(place, gate.reshape(1, -1), out_grad)
    own_x = exchange(send_x)
    own_d = exchange(send_d)
    rows_x = (own_x, swap_core(own_x))
    act_first, act_rest, slope, mark = forward(table, rows_x, weight_in)
    own_d = after(own_d, mark)
    rows_d = (own_d, swap_core(own_d))

    out_low, out_high = outer_products(act_first, rows_d, 0, 1, ())
    out_hop = first_hop(out_low, out_high, "x")
    pre_a, in_low, in_high = backward(
        table, rows_d, rows_x, slope, weight_out, (0, 1), (small(out_high),)
    )
    in_hop = first_hop(in_low, in_high, "y")
    out_sides = outer_products(act_rest, rows_d, 0, 2, (small(in_high),))
    out_join = join(out_hop, out_sides[:512], out_sides[512:])
    out_parts = second_hop(*out_join, "x")
    pre_b, in_sides = backward(table, rows_d, rows_x, slope, weight_out, (1, 2), both(out_join))
    in_join = join(in_hop, in_sides[:512], in_sides[512:])
    in_parts = second_hop(*in_join, "y")
    pre_c, in_own = backward(table, rows_d, rows_x, slope, weight_out, (3, 1), both(in_join))
    out_own = outer_products(act_rest, rows_d, 2, 1, (small(in_own),))
    own = once(
        x,
        lambda start: sum_cores(
            row_gradients(table, (pre_a, pre_b, pre_c), weight_in, (small(start),))
        ),
        rows_x[0],
    )
    back = exchange(own)

    group = add(after(out_own, small(own)), *out_parts).astype(BF16)
    last = within(group, "y")
    grad_out = add(last[0], *second_hop(*last[1:], "y")) * scale
    group = add(after(in_own, *both(last[1:])), *in_parts).astype(BF16)
    last = within(group, "x")
    grad_in = add(last[0], *second_hop(*last[1:], "x")) * scale
    token_grad = restore_order(place, back)
    return token_grad, grad_in[None], grad_out[None]


def solution(mesh):
    chips = Mesh(mesh.devices.reshape(4, 4, 2, 4), ("y", "x", "core", "expert"))
    rows = ("y", "x", "core", "expert")
    plane = ("y", "x", "core")
    return jax.shard_map(
        local,
        mesh=chips,
        in_specs=(
            P(rows, None),
            P(rows, None),
            P(rows),
            P(rows, None),
            P("expert", None, None),
            P("expert", None, None),
        ),
        out_specs=(P(rows, None), P("expert", plane, None), P("expert", plane, None)),
        check_vma=False,
    )
```

```python
import math

import jax
import jax.numpy as jnp
from jax import lax
from jax.experimental import pallas as pl
from jax.experimental.pallas import tpu as pltpu
from jax.sharding import Mesh, PartitionSpec as P

BF16 = jnp.bfloat16
F32 = jnp.float32
VMEM_LIMIT = 28 * 1024 * 1024
ORDER = (2, 1, 3, 0)
INVERSE = (3, 1, 0, 2)


def ring(step):
    return [(i, (i + step) % 4) for i in range(4)]


def swap_core(array):
    return lax.ppermute(array, "core", [(0, 1), (1, 0)])


def params():
    return pltpu.CompilerParams(vmem_limit_bytes=VMEM_LIMIT)


def cost(nbytes=1024):
    return pl.CostEstimate(flops=0, bytes_accessed=int(nbytes), transcendentals=0)


def shape(rows, cols, dtype=BF16):
    return jax.ShapeDtypeStruct((rows, cols), dtype)


def dot_nt(a, b):
    return lax.dot_general(a, b, (((1,), (1,)), ((), ())), preferred_element_type=F32)


def dot_nn(a, b):
    return lax.dot_general(a, b, (((1,), (0,)), ((), ())), preferred_element_type=F32)


def dot_tn(a, b):
    return lax.dot_general(a, b, (((0,), (0,)), ((), ())), preferred_element_type=F32)


def gelu_parts(pre_act):
    root_two_pi = 0.7978845608028654
    square = pre_act * pre_act
    inner = pre_act * (root_two_pi + root_two_pi * 0.044715 * square)
    halved = 0.5 + 0.5 * jnp.tanh(inner)
    value = pre_act * halved
    slope_of_inner = 2.0 * root_two_pi + 6.0 * root_two_pi * 0.044715 * square
    return value, halved + value * (1.0 - halved) * slope_of_inner


VMEM = pl.BlockSpec(memory_space=pltpu.VMEM)
ANY = pl.BlockSpec(memory_space=pl.ANY)


def dispatch_tokens(where, region, tokens):
    n, width = tokens.shape

    def body(where_ref, region_ref, tok_ref, place_ref, *outs):
        dest = jnp.bitwise_and(region_ref[...] - where_ref[0] + 4, 3)
        onehot = (dest == lax.broadcasted_iota(jnp.int32, (8, n), 0)).astype(F32)
        upper = (
            lax.broadcasted_iota(jnp.int32, (n, n), 0) < lax.broadcasted_iota(jnp.int32, (n, n), 1)
        ).astype(F32)
        before = dot_nn(onehot.astype(BF16), upper.astype(BF16))
        rank = jnp.sum(before * onehot, axis=0, keepdims=True).astype(jnp.int32)
        slot = dest * 128 + rank
        place = (slot == lax.broadcasted_iota(jnp.int32, (512, n), 0)).astype(F32).astype(BF16)
        place_ref[...] = place
        for r, out in enumerate(outs):
            out[...] = dot_nn(place[r * 128 : (r + 1) * 128], tok_ref[...]).astype(BF16)

    return pl.pallas_call(
        body,
        out_shape=[shape(512, n)] + [shape(128, width)] * 4,
        in_specs=[pl.BlockSpec(memory_space=pltpu.SMEM)] + [VMEM] * 2,
        out_specs=[VMEM] * 5,
        compiler_params=params(),
        cost_estimate=cost(4 * n * width * 2),
    )(where, region, tokens)


def dispatch_grads(place, gate, grads):
    n, width = grads.shape

    def body(place_ref, gate_ref, grad_ref, *outs):
        column = jnp.transpose(jnp.broadcast_to(gate_ref[...], (128, n)))[:, :1]
        scaled = (column * grad_ref[...].astype(F32)).astype(BF16)
        for r, out in enumerate(outs):
            out[...] = dot_nn(place_ref[r * 128 : (r + 1) * 128, :], scaled).astype(BF16)

    return pl.pallas_call(
        body,
        out_shape=[shape(128, width)] * 4,
        in_specs=[VMEM] * 3,
        out_specs=[VMEM] * 4,
        compiler_params=params(),
        cost_estimate=cost(4 * n * width * 2),
    )(place, gate, grads)


HBM = pl.BlockSpec(memory_space=pltpu.HBM)


def block_scratch(width, count):
    return [pltpu.VMEM((512 * count, width), BF16), pltpu.SemaphoreType.DMA((4 * count,))]


def block_group(table_ref, weight_ref, w_buf, sems, offset, count):
    step = pl.program_id(0)

    def fetch(k):
        block = pl.multiple_of(table_ref[offset + k] * 128, 128)
        place = pl.multiple_of(k * 128, 128)
        return pltpu.make_async_copy(
            weight_ref.at[pl.ds(block, 128), :], w_buf.at[pl.ds(place, 128), :], sems.at[k]
        )

    @pl.when(step == 0)
    def _():
        for k in range(4 * count):
            fetch(k).start()

    for q in range(4):
        fetch(4 * step + q).wait()
    return w_buf.at[pl.ds(pl.multiple_of(step * 512, 512), 512), :]


def after(array, *others):
    def body(*refs):
        del refs

    return pl.pallas_call(
        body,
        in_specs=[ANY] * (1 + len(others)),
        out_specs=ANY,
        out_shape=jax.ShapeDtypeStruct(array.shape, array.dtype),
        input_output_aliases={0: 0},
        compiler_params=params(),
        cost_estimate=cost(),
    )(array, *others)


MARK = jax.ShapeDtypeStruct((8, 128), F32)
MARK_SPEC = pl.BlockSpec((8, 128), lambda i, *_: (0, 0))


def fixed(rows, cols):
    return pl.BlockSpec((rows, cols), lambda i, *_: (0, 0))


def merge(table_ref, part_refs, all_ref):
    for k, ref in enumerate(part_refs):
        begin = pl.multiple_of(k // 4 * 512 + table_ref[48 + k % 4] * 128, 128)
        all_ref[pl.ds(begin, 128), :] = ref[...]


def forward(table, parts, weight):
    width = weight.shape[1]
    tok = 128 * len(parts)

    def body(table_ref, *refs):
        part_refs, weight_ref = refs[: len(parts)], refs[len(parts)]
        act_ref, slope_ref, all_ref, mark_ref, w_buf, sems = refs[len(parts) + 1 :]

        @pl.when(pl.program_id(0) == 0)
        def _():
            mark_ref[...] = jnp.zeros_like(mark_ref)
            merge(table_ref, part_refs, all_ref)

        w_ref = block_group(table_ref, weight_ref, w_buf, sems, 0, 4)
        for c in range(tok // 256):
            cols = slice(c * 256, (c + 1) * 256)
            act, slope = gelu_parts(dot_nt(w_ref[...], all_ref[cols, :]))
            act_ref[:, cols] = act.astype(BF16)
            slope_ref[:, cols] = slope.astype(BF16)

    return pl.pallas_call(
        body,
        grid_spec=pltpu.PrefetchScalarGridSpec(
            num_scalar_prefetch=1,
            grid=(4,),
            in_specs=[VMEM] * len(parts) + [HBM],
            out_specs=[pl.BlockSpec((512, tok), lambda i, *_: (i, 0))] * 2
            + [fixed(tok, width), MARK_SPEC],
            scratch_shapes=block_scratch(width, 4),
        ),
        out_shape=[pltpu.HBM((2048, tok), BF16)] * 2 + [shape(tok, width), MARK],
        compiler_params=params(),
        cost_estimate=cost(2**24),
    )(table, *parts, weight)


def outer_first(table, act, parts):
    width = parts[0].shape[1]
    tok = 128 * len(parts)

    def body(table_ref, act_ref, *refs):
        part_refs, (low_ref, high_ref, all_ref, mark_ref) = refs[: len(parts)], refs[len(parts) :]
        mark_ref[...] = jnp.zeros_like(mark_ref)
        merge(table_ref, part_refs, all_ref)
        low_ref[...] = dot_nn(act_ref[:256, :], all_ref[...]).astype(BF16)
        high_ref[...] = dot_nn(act_ref[256:, :], all_ref[...]).astype(BF16)

    return pl.pallas_call(
        body,
        grid_spec=pltpu.PrefetchScalarGridSpec(
            num_scalar_prefetch=1,
            grid=(1,),
            in_specs=[fixed(512, tok)] + [VMEM] * len(parts),
            out_specs=[fixed(256, width)] * 2 + [fixed(tok, width), MARK_SPEC],
        ),
        out_shape=[shape(256, width)] * 2 + [shape(tok, width), MARK],
        compiler_params=params(),
        cost_estimate=cost(2**22),
    )(table, act, *parts)


def outer_rest(act, rows, first, count, deps):
    tok, width = rows.shape

    def body(act_ref, rows_ref, *refs):
        out_ref = refs[len(deps)]
        out_ref[...] = dot_nn(act_ref[...], rows_ref[...]).astype(BF16)

    return pl.pallas_call(
        body,
        grid=(count,),
        in_specs=[pl.BlockSpec((512, tok), lambda i: (i + first, 0)), VMEM] + [ANY] * len(deps),
        out_specs=pl.BlockSpec((512, width), lambda i: (i, 0)),
        out_shape=shape(512 * count, width),
        compiler_params=params(),
        cost_estimate=cost(2**20 * (2 + 2 * count)),
    )(act, rows, *deps)


def backward(table, grads, rows, slope, weight, first, count, deps):
    tok, width = rows.shape
    split = first == 0

    def body(table_ref, grads_ref, rows_ref, slope_ref, weight_ref, *refs):
        pre_ref, *outs, mark_ref, w_buf, w_sems, s_buf, s_sems = refs[len(deps) :]
        mark_ref[...] = jnp.zeros_like(mark_ref)
        w_ref = block_group(table_ref, weight_ref, w_buf, w_sems, 16 + 4 * first, count)
        s_ref = block_group(table_ref, slope_ref, s_buf, s_sems, 32 + 4 * first, count)
        for c in range(tok // 256):
            cols = slice(c * 256, (c + 1) * 256)
            act_grad = dot_nt(w_ref[...], grads_ref[cols, :])
            pre_ref[:, cols] = (act_grad * s_ref[:, cols].astype(F32)).astype(BF16)
        span = 512 // len(outs)
        for k, out in enumerate(outs):
            out[...] = dot_nn(pre_ref[k * span : (k + 1) * span, :], rows_ref[...]).astype(BF16)

    def groups(cols):
        return pl.BlockSpec((512, cols), lambda i, *_: (i, 0))

    return pl.pallas_call(
        body,
        grid_spec=pltpu.PrefetchScalarGridSpec(
            num_scalar_prefetch=1,
            grid=(count,),
            in_specs=[VMEM] * 2 + [HBM] * 2 + [ANY] * len(deps),
            out_specs=[groups(tok)]
            + ([fixed(256, width)] * 2 if split else [groups(width)])
            + [MARK_SPEC],
            scratch_shapes=block_scratch(width, count) + block_scratch(tok, count),
        ),
        out_shape=[shape(512 * count, tok)]
        + ([shape(256, width)] * 2 if split else [shape(512 * count, width)])
        + [MARK],
        compiler_params=params(),
        cost_estimate=cost(2**20 * (2 + 4 * count)),
    )(table, grads, rows, slope, weight, *deps)


def row_gradients(table, pre, weight, deps):
    width = weight.shape[1]
    rows = 512

    def body(table_ref, a_ref, b_ref, c_ref, weight_ref, *refs):
        own_ref, other_ref, w_buf, sems, total = refs[len(deps) :]
        step = pl.program_id(0)
        w_ref = block_group(table_ref, weight_ref, w_buf, sems, 16, 4)

        @pl.when(step == 0)
        def _():
            total[...] = dot_tn(a_ref[...], w_ref[...])

        @pl.when(jnp.logical_and(step > 0, step < 3))
        def _():
            begin = pl.multiple_of((step - 1) * 512, 512)
            total[...] += dot_tn(b_ref[pl.ds(begin, 512), :], w_ref[...])

        @pl.when(step == 3)
        def _():
            final = (total[...] + dot_tn(c_ref[...], w_ref[...])).astype(BF16)
            own_ref[...] = final[:rows]
            other_ref[...] = final[rows:]

    return pl.pallas_call(
        body,
        grid_spec=pltpu.PrefetchScalarGridSpec(
            num_scalar_prefetch=1,
            grid=(4,),
            in_specs=[VMEM] * 3 + [HBM] + [ANY] * len(deps),
            out_specs=[fixed(rows, width)] * 2,
            scratch_shapes=block_scratch(width, 4) + [pltpu.VMEM((2 * rows, width), F32)],
        ),
        out_shape=[shape(rows, width)] * 2,
        compiler_params=params(),
        cost_estimate=cost(2**23 + 2**22),
    )(table, *pre, weight, *deps)


def join(sides, arrived):
    n, width = sides.shape
    h = n // 4

    def body(sides_ref, from_next, from_prev, up_ref, down_ref, mark_ref):
        mark_ref[...] = jnp.zeros_like(mark_ref)
        up_ref[:h, :] = sides_ref[:h, :]
        up_ref[h:, :] = add(sides_ref[h : 2 * h, :], from_prev[...]).astype(BF16)
        down_ref[:h, :] = add(sides_ref[2 * h : 3 * h, :], from_next[...]).astype(BF16)
        down_ref[h:, :] = sides_ref[3 * h :, :]

    return pl.pallas_call(
        body,
        out_shape=[shape(2 * h, width)] * 2 + [MARK],
        in_specs=[VMEM] * 3,
        out_specs=[VMEM] * 3,
        compiler_params=params(),
        cost_estimate=cost(4 * n * width),
    )(sides, *arrived)


def restore_order(where, place, rows):
    n, width = place.shape[1], rows.shape[1]

    def body(where_ref, place_ref, rows_ref, out_ref):
        total = jnp.zeros((n, width), F32)
        for e in range(4):
            bucket = pl.multiple_of(jnp.bitwise_and(e - where_ref[0] + 4, 3) * 128, 128)
            total += dot_tn(place_ref[pl.ds(bucket, 128), :], rows_ref[e * 128 : (e + 1) * 128, :])
        out_ref[...] = total.astype(BF16)

    return pl.pallas_call(
        body,
        out_shape=shape(n, width),
        in_specs=[pl.BlockSpec(memory_space=pltpu.SMEM)] + [VMEM] * 2,
        out_specs=VMEM,
        compiler_params=params(),
        cost_estimate=cost(2**21),
    )(where, place, rows)


def add(*terms):
    total = terms[0].astype(F32)
    for term in terms[1:]:
        total = total + term.astype(F32)
    return total


def first_hop(low, high, axis):
    return lax.ppermute(low, axis, ring(3)), lax.ppermute(high, axis, ring(1))


def second_hop(up, down, axis):
    return lax.ppermute(up, axis, ring(1)), lax.ppermute(down, axis, ring(3))


def combine(own, received):
    n, width = own.shape
    q = n // 4

    def body(own_ref, left, right, keep_ref, sides_ref, low_ref, high_ref, mark_ref):
        mark_ref[...] = jnp.zeros_like(mark_ref)

        def total(begin, end):
            span = slice(begin, end)
            return add(own_ref[span, :], left[span, :], right[span, :]).astype(BF16)

        low_ref[...] = total(2 * q, 2 * q + q // 2)
        high_ref[...] = total(2 * q + q // 2, 3 * q)
        keep_ref[...] = total(0, q)
        sides_ref[:q, :] = total(q, 2 * q)
        sides_ref[q:, :] = total(3 * q, n)

    return pl.pallas_call(
        body,
        out_shape=[shape(q, width), shape(2 * q, width), shape(q // 2, width), shape(q // 2, width), MARK],
        in_specs=[VMEM] * 3,
        out_specs=[VMEM] * 5,
        compiler_params=params(),
        cost_estimate=cost(8 * n * width),
    )(own, *received)


def in_hbm(array):
    return pltpu.with_memory_space_constraint(array, pltpu.HBM)


def sum_cores(own, other):
    return add(own, swap_core(other)).astype(BF16)


def once(index, work, start):
    trips = 1 + jnp.minimum(index, 0)
    return lax.fori_loop(0, trips, lambda _, array: work(array), start)


def local(tokens, out_grad, gate, region, w_in, w_out):
    expert = lax.axis_index("expert").astype(jnp.int32)
    x, y, core = (lax.axis_index(a).astype(jnp.int32) for a in ("x", "y", "core"))
    scale = 1.0 / math.sqrt(float(tokens.shape[0] * lax.axis_size(("y", "x", "core"))))
    order = jnp.array(ORDER, jnp.int32)
    every = jnp.arange(4, dtype=jnp.int32)
    by_x = ((((y + every[None, :]) % 4) * 4 + (x + order[:, None]) % 4) * 2 + core).reshape(16)
    by_y = ((((y + order[:, None]) % 4) * 4 + (x + every[None, :]) % 4) * 2 + core).reshape(16)
    same = jnp.array([INVERSE[q] * 4 + ORDER[p] for p in range(4) for q in range(4)], jnp.int32)
    table = jnp.concatenate([by_x, by_y, same, (expert - every) % 4])
    weight_in, weight_out = in_hbm(w_in[0]), in_hbm(w_out[0])

    place, *send_x = dispatch_tokens(expert[None], region.reshape(1, -1), tokens)
    send_d = dispatch_grads(place, gate.reshape(1, -1), out_grad)

    def to_owner(parts):
        return [parts[0]] + [lax.ppermute(parts[r], "expert", ring(r)) for r in (1, 2, 3)]

    own_x = to_owner(send_x)
    both_x = own_x + [swap_core(p) for p in own_x]
    own_d = to_owner(send_d)
    act, slope, rows_x, mark = forward(table, both_x, weight_in)
    act, slope = in_hbm(act), in_hbm(slope)
    own_d = [after(part, mark) for part in own_d]
    both_d = own_d + [swap_core(p) for p in own_d]

    out_low, out_high, rows_d, mark = outer_first(table, act, both_d)
    hop = first_hop(out_low, out_high, "x")
    pre_a, in_low, in_high, mark = backward(
        table, rows_d, rows_x, slope, weight_out, 0, 1, (mark,)
    )
    out_sides = outer_rest(act, rows_d, 1, 2, (mark,))
    *pair, mark = join(out_sides, hop)
    out_parts = second_hop(*pair, "x")
    hop = first_hop(in_low, in_high, "y")
    pre_b, in_sides, mark = backward(table, rows_d, rows_x, slope, weight_out, 1, 2, (mark,))
    *pair, mark = join(in_sides, hop)
    in_parts = second_hop(*pair, "y")
    pre_c, in_own, mark = backward(table, rows_d, rows_x, slope, weight_out, 3, 1, (mark,))
    out_own = outer_rest(act, rows_d, 3, 1, (mark,))
    own = once(
        x,
        lambda start: sum_cores(
            *row_gradients(table, (pre_a, pre_b, pre_c), weight_in, (start,))
        ),
        out_own,
    )
    back = lax.all_to_all(own, "expert", split_axis=0, concat_axis=0, tiled=True)

    keep, sides, low, high, mark = combine(out_own, out_parts)
    *pair, mark = join(sides, first_hop(low, high, "y"))
    grad_out = add(keep, *second_hop(*pair, "y")) * scale
    keep, sides, low, high, _ = combine(after(in_own, mark), in_parts)
    *pair, _ = join(sides, first_hop(low, high, "x"))
    grad_in = add(keep, *second_hop(*pair, "x")) * scale
    token_grad = restore_order(expert[None], place, back)
    return token_grad, grad_in[None], grad_out[None]


def solution(mesh):
    chips = Mesh(mesh.devices.reshape(4, 4, 2, 4), ("y", "x", "core", "expert"))
    rows = ("y", "x", "core", "expert")
    plane = ("y", "x", "core")
    return jax.shard_map(
        local,
        mesh=chips,
        in_specs=(
            P(rows, None),
            P(rows, None),
            P(rows),
            P(rows, None),
            P("expert", None, None),
            P("expert", None, None),
        ),
        out_specs=(P(rows, None), P("expert", plane, None), P("expert", plane, None)),
        check_vma=False,
    )
```

```python
import math

import jax
import jax.numpy as jnp
from jax import lax
from jax.experimental import pallas as pl
from jax.experimental.pallas import tpu as pltpu
from jax.sharding import Mesh, PartitionSpec as P

BF16 = jnp.bfloat16
F32 = jnp.float32
VMEM_LIMIT = 28 * 1024 * 1024
ORDER = (2, 1, 3, 0)
INVERSE = (3, 1, 0, 2)


def ring(step):
    return [(i, (i + step) % 4) for i in range(4)]


def swap_core(array):
    return lax.ppermute(array, "core", [(0, 1), (1, 0)])


def params():
    return pltpu.CompilerParams(vmem_limit_bytes=VMEM_LIMIT)


def cost(nbytes=1024):
    return pl.CostEstimate(flops=0, bytes_accessed=int(nbytes), transcendentals=0)


def shape(rows, cols, dtype=BF16):
    return jax.ShapeDtypeStruct((rows, cols), dtype)


def dot_nt(a, b):
    return lax.dot_general(a, b, (((1,), (1,)), ((), ())), preferred_element_type=F32)


def dot_nn(a, b):
    return lax.dot_general(a, b, (((1,), (0,)), ((), ())), preferred_element_type=F32)


def dot_tn(a, b):
    return lax.dot_general(a, b, (((0,), (0,)), ((), ())), preferred_element_type=F32)


def gelu_parts(pre_act):
    root_two_pi = 0.7978845608028654
    square = pre_act * pre_act
    inner = pre_act * (root_two_pi + root_two_pi * 0.044715 * square)
    halved = 0.5 + 0.5 * jnp.tanh(inner)
    value = pre_act * halved
    slope_of_inner = 2.0 * root_two_pi + 6.0 * root_two_pi * 0.044715 * square
    return value, halved + value * (1.0 - halved) * slope_of_inner


VMEM = pl.BlockSpec(memory_space=pltpu.VMEM)
ANY = pl.BlockSpec(memory_space=pl.ANY)


def dispatch_tokens(where, region, tokens):
    n, width = tokens.shape

    def body(where_ref, region_ref, tok_ref, place_ref, *outs):
        dest = jnp.bitwise_and(region_ref[...] - where_ref[0] + 4, 3)
        onehot = (dest == lax.broadcasted_iota(jnp.int32, (8, n), 0)).astype(F32)
        upper = (
            lax.broadcasted_iota(jnp.int32, (n, n), 0) < lax.broadcasted_iota(jnp.int32, (n, n), 1)
        ).astype(F32)
        before = dot_nn(onehot.astype(BF16), upper.astype(BF16))
        rank = jnp.sum(before * onehot, axis=0, keepdims=True).astype(jnp.int32)
        slot = dest * 128 + rank
        place = (slot == lax.broadcasted_iota(jnp.int32, (512, n), 0)).astype(F32).astype(BF16)
        place_ref[...] = place
        for r, out in enumerate(outs):
            out[...] = dot_nn(place[r * 128 : (r + 1) * 128], tok_ref[...]).astype(BF16)

    return pl.pallas_call(
        body,
        out_shape=[shape(512, n)] + [shape(128, width)] * 4,
        in_specs=[pl.BlockSpec(memory_space=pltpu.SMEM)] + [VMEM] * 2,
        out_specs=[VMEM] * 5,
        compiler_params=params(),
        cost_estimate=cost(4 * n * width * 2),
    )(where, region, tokens)


def dispatch_grads(place, gate, grads):
    n, width = grads.shape

    def body(place_ref, gate_ref, grad_ref, *outs):
        column = jnp.transpose(jnp.broadcast_to(gate_ref[...], (128, n)))[:, :1]
        scaled = (column * grad_ref[...].astype(F32)).astype(BF16)
        for r, out in enumerate(outs):
            out[...] = dot_nn(place_ref[r * 128 : (r + 1) * 128, :], scaled).astype(BF16)

    return pl.pallas_call(
        body,
        out_shape=[shape(128, width)] * 4,
        in_specs=[VMEM] * 3,
        out_specs=[VMEM] * 4,
        compiler_params=params(),
        cost_estimate=cost(4 * n * width * 2),
    )(place, gate, grads)


HBM = pl.BlockSpec(memory_space=pltpu.HBM)


def block_scratch(width, count):
    return [pltpu.VMEM((512 * count, width), BF16), pltpu.SemaphoreType.DMA((4 * count,))]


def block_group(table_ref, weight_ref, w_buf, sems, offset, count):
    step = pl.program_id(0)

    def fetch(k):
        block = pl.multiple_of(table_ref[offset + k] * 128, 128)
        place = pl.multiple_of(k * 128, 128)
        return pltpu.make_async_copy(
            weight_ref.at[pl.ds(block, 128), :], w_buf.at[pl.ds(place, 128), :], sems.at[k]
        )

    @pl.when(step == 0)
    def _():
        for k in range(4 * count):
            fetch(k).start()

    for q in range(4):
        fetch(4 * step + q).wait()
    return w_buf.at[pl.ds(pl.multiple_of(step * 512, 512), 512), :]


def after(array, *others):
    def body(*refs):
        del refs

    return pl.pallas_call(
        body,
        in_specs=[ANY] * (1 + len(others)),
        out_specs=ANY,
        out_shape=jax.ShapeDtypeStruct(array.shape, array.dtype),
        input_output_aliases={0: 0},
        compiler_params=params(),
        cost_estimate=cost(),
    )(array, *others)


MARK = jax.ShapeDtypeStruct((8, 128), F32)
MARK_SPEC = pl.BlockSpec((8, 128), lambda i, *_: (0, 0))


def fixed(rows, cols):
    return pl.BlockSpec((rows, cols), lambda i, *_: (0, 0))


def merge(table_ref, part_refs, all_ref):
    for k, ref in enumerate(part_refs):
        begin = pl.multiple_of(k // 4 * 512 + table_ref[48 + k % 4] * 128, 128)
        all_ref[pl.ds(begin, 128), :] = ref[...]


def forward(table, parts, weight):
    width = weight.shape[1]
    tok = 128 * len(parts)

    def body(table_ref, *refs):
        part_refs, weight_ref = refs[: len(parts)], refs[len(parts)]
        act_ref, slope_ref, all_ref, mark_ref, w_buf, sems = refs[len(parts) + 1 :]

        @pl.when(pl.program_id(0) == 0)
        def _():
            mark_ref[...] = jnp.zeros_like(mark_ref)
            merge(table_ref, part_refs, all_ref)

        w_ref = block_group(table_ref, weight_ref, w_buf, sems, 0, 4)
        for c in range(tok // 256):
            cols = slice(c * 256, (c + 1) * 256)
            act, slope = gelu_parts(dot_nt(w_ref[...], all_ref[cols, :]))
            act_ref[:, cols] = act.astype(BF16)
            slope_ref[:, cols] = slope.astype(BF16)

    return pl.pallas_call(
        body,
        grid_spec=pltpu.PrefetchScalarGridSpec(
            num_scalar_prefetch=1,
            grid=(4,),
            in_specs=[VMEM] * len(parts) + [HBM],
            out_specs=[pl.BlockSpec((512, tok), lambda i, *_: (i, 0))] * 2
            + [fixed(tok, width), MARK_SPEC],
            scratch_shapes=block_scratch(width, 4),
        ),
        out_shape=[pltpu.HBM((2048, tok), BF16)] * 2 + [shape(tok, width), MARK],
        compiler_params=params(),
        cost_estimate=cost(2**24),
    )(table, *parts, weight)


def outer_first(table, act, parts):
    width = parts[0].shape[1]
    tok = 128 * len(parts)

    def body(table_ref, act_ref, *refs):
        part_refs, (low_ref, high_ref, all_ref, mark_ref) = refs[: len(parts)], refs[len(parts) :]
        mark_ref[...] = jnp.zeros_like(mark_ref)
        merge(table_ref, part_refs, all_ref)
        low_ref[...] = dot_nn(act_ref[:256, :], all_ref[...]).astype(BF16)
        high_ref[...] = dot_nn(act_ref[256:, :], all_ref[...]).astype(BF16)

    return pl.pallas_call(
        body,
        grid_spec=pltpu.PrefetchScalarGridSpec(
            num_scalar_prefetch=1,
            grid=(1,),
            in_specs=[fixed(512, tok)] + [VMEM] * len(parts),
            out_specs=[fixed(256, width)] * 2 + [fixed(tok, width), MARK_SPEC],
        ),
        out_shape=[shape(256, width)] * 2 + [shape(tok, width), MARK],
        compiler_params=params(),
        cost_estimate=cost(2**22),
    )(table, act, *parts)


def outer_rest(act, rows, first, count, deps):
    tok, width = rows.shape

    def body(act_ref, rows_ref, *refs):
        out_ref = refs[len(deps)]
        out_ref[...] = dot_nn(act_ref[...], rows_ref[...]).astype(BF16)

    return pl.pallas_call(
        body,
        grid=(count,),
        in_specs=[pl.BlockSpec((512, tok), lambda i: (i + first, 0)), VMEM] + [ANY] * len(deps),
        out_specs=pl.BlockSpec((512, width), lambda i: (i, 0)),
        out_shape=shape(512 * count, width),
        compiler_params=params(),
        cost_estimate=cost(2**20 * (2 + 2 * count)),
    )(act, rows, *deps)


def backward(table, grads, rows, slope, weight, first, count, deps):
    tok, width = rows.shape
    split = first == 0

    def body(table_ref, grads_ref, rows_ref, slope_ref, weight_ref, *refs):
        pre_ref, *outs, mark_ref, w_buf, w_sems, s_buf, s_sems = refs[len(deps) :]
        mark_ref[...] = jnp.zeros_like(mark_ref)
        w_ref = block_group(table_ref, weight_ref, w_buf, w_sems, 16 + 4 * first, count)
        s_ref = block_group(table_ref, slope_ref, s_buf, s_sems, 32 + 4 * first, count)
        for c in range(tok // 256):
            cols = slice(c * 256, (c + 1) * 256)
            act_grad = dot_nt(w_ref[...], grads_ref[cols, :])
            pre_ref[:, cols] = (act_grad * s_ref[:, cols].astype(F32)).astype(BF16)
        span = 512 // len(outs)
        for k, out in enumerate(outs):
            out[...] = dot_nn(pre_ref[k * span : (k + 1) * span, :], rows_ref[...]).astype(BF16)

    def groups(cols):
        return pl.BlockSpec((512, cols), lambda i, *_: (i, 0))

    return pl.pallas_call(
        body,
        grid_spec=pltpu.PrefetchScalarGridSpec(
            num_scalar_prefetch=1,
            grid=(count,),
            in_specs=[VMEM] * 2 + [HBM] * 2 + [ANY] * len(deps),
            out_specs=[groups(tok)]
            + ([fixed(256, width)] * 2 if split else [groups(width)])
            + [MARK_SPEC],
            scratch_shapes=block_scratch(width, count) + block_scratch(tok, count),
        ),
        out_shape=[shape(512 * count, tok)]
        + ([shape(256, width)] * 2 if split else [shape(512 * count, width)])
        + [MARK],
        compiler_params=params(),
        cost_estimate=cost(2**20 * (2 + 4 * count)),
    )(table, grads, rows, slope, weight, *deps)


def row_gradients(table, pre, weight, deps):
    width = weight.shape[1]
    rows = 512

    def body(table_ref, a_ref, b_ref, c_ref, weight_ref, *refs):
        out_ref, w_buf, sems, total = refs[len(deps) :]
        step = pl.program_id(0)
        w_ref = block_group(table_ref, weight_ref, w_buf, sems, 16, 4)

        @pl.when(step == 0)
        def _():
            total[...] = dot_tn(a_ref[...], w_ref[...])

        @pl.when(jnp.logical_and(step > 0, step < 3))
        def _():
            begin = pl.multiple_of((step - 1) * 512, 512)
            total[...] += dot_tn(b_ref[pl.ds(begin, 512), :], w_ref[...])

        @pl.when(step == 3)
        def _():
            final = (total[...] + dot_tn(c_ref[...], w_ref[...])).astype(BF16)
            own = table_ref[52]
            out_ref[pl.ds(pl.multiple_of(own * rows, rows), rows), :] = final[:rows]
            out_ref[pl.ds(pl.multiple_of((1 - own) * rows, rows), rows), :] = final[rows:]

    return pl.pallas_call(
        body,
        grid_spec=pltpu.PrefetchScalarGridSpec(
            num_scalar_prefetch=1,
            grid=(4,),
            in_specs=[VMEM] * 3 + [HBM] + [ANY] * len(deps),
            out_specs=fixed(2 * rows, width),
            scratch_shapes=block_scratch(width, 4) + [pltpu.VMEM((2 * rows, width), F32)],
        ),
        out_shape=shape(2 * rows, width),
        compiler_params=params(),
        cost_estimate=cost(2**23 + 2**22),
    )(table, *pre, weight, *deps)


def join(sides, arrived):
    n, width = sides.shape
    h = n // 4

    def body(sides_ref, from_next, from_prev, up_ref, down_ref, mark_ref):
        mark_ref[...] = jnp.zeros_like(mark_ref)
        up_ref[:h, :] = sides_ref[:h, :]
        up_ref[h:, :] = add(sides_ref[h : 2 * h, :], from_prev[...]).astype(BF16)
        down_ref[:h, :] = add(sides_ref[2 * h : 3 * h, :], from_next[...]).astype(BF16)
        down_ref[h:, :] = sides_ref[3 * h :, :]

    return pl.pallas_call(
        body,
        out_shape=[shape(2 * h, width)] * 2 + [MARK],
        in_specs=[VMEM] * 3,
        out_specs=[VMEM] * 3,
        compiler_params=params(),
        cost_estimate=cost(4 * n * width),
    )(sides, *arrived)


def restore_order(where, place, rows):
    n, width = place.shape[1], rows.shape[1]

    def body(where_ref, place_ref, rows_ref, out_ref):
        total = jnp.zeros((n, width), F32)
        for e in range(4):
            bucket = pl.multiple_of(jnp.bitwise_and(e - where_ref[0] + 4, 3) * 128, 128)
            total += dot_tn(place_ref[pl.ds(bucket, 128), :], rows_ref[e * 128 : (e + 1) * 128, :])
        out_ref[...] = total.astype(BF16)

    return pl.pallas_call(
        body,
        out_shape=shape(n, width),
        in_specs=[pl.BlockSpec(memory_space=pltpu.SMEM)] + [VMEM] * 2,
        out_specs=VMEM,
        compiler_params=params(),
        cost_estimate=cost(2**21),
    )(where, place, rows)


def add(*terms):
    total = terms[0].astype(F32)
    for term in terms[1:]:
        total = total + term.astype(F32)
    return total


def first_hop(low, high, axis):
    return lax.ppermute(low, axis, ring(3)), lax.ppermute(high, axis, ring(1))


def second_hop(up, down, axis):
    return lax.ppermute(up, axis, ring(1)), lax.ppermute(down, axis, ring(3))


def combine(own, received):
    n, width = own.shape
    q = n // 4

    def body(own_ref, left, right, keep_ref, sides_ref, low_ref, high_ref, mark_ref):
        mark_ref[...] = jnp.zeros_like(mark_ref)

        def total(begin, end):
            span = slice(begin, end)
            return add(own_ref[span, :], left[span, :], right[span, :]).astype(BF16)

        low_ref[...] = total(2 * q, 2 * q + q // 2)
        high_ref[...] = total(2 * q + q // 2, 3 * q)
        keep_ref[...] = total(0, q)
        sides_ref[:q, :] = total(q, 2 * q)
        sides_ref[q:, :] = total(3 * q, n)

    return pl.pallas_call(
        body,
        out_shape=[shape(q, width), shape(2 * q, width), shape(q // 2, width), shape(q // 2, width), MARK],
        in_specs=[VMEM] * 3,
        out_specs=[VMEM] * 5,
        compiler_params=params(),
        cost_estimate=cost(8 * n * width),
    )(own, *received)


def in_hbm(array):
    return pltpu.with_memory_space_constraint(array, pltpu.HBM)


def sum_cores(terms):
    terms = lax.all_to_all(terms, "core", split_axis=0, concat_axis=0, tiled=True)
    n = terms.shape[0] // 2
    return add(terms[:n], terms[n:]).astype(BF16)


def local(tokens, out_grad, gate, region, w_in, w_out):
    expert = lax.axis_index("expert").astype(jnp.int32)
    x, y, core = (lax.axis_index(a).astype(jnp.int32) for a in ("x", "y", "core"))
    scale = 1.0 / math.sqrt(float(tokens.shape[0] * lax.axis_size(("y", "x", "core"))))
    order = jnp.array(ORDER, jnp.int32)
    every = jnp.arange(4, dtype=jnp.int32)
    by_x = ((((y + every[None, :]) % 4) * 4 + (x + order[:, None]) % 4) * 2 + core).reshape(16)
    by_y = ((((y + order[:, None]) % 4) * 4 + (x + every[None, :]) % 4) * 2 + core).reshape(16)
    same = jnp.array([INVERSE[q] * 4 + ORDER[p] for p in range(4) for q in range(4)], jnp.int32)
    table = jnp.concatenate([by_x, by_y, same, (expert - every) % 4, core[None]])
    weight_in, weight_out = in_hbm(w_in[0]), in_hbm(w_out[0])

    place, *send_x = dispatch_tokens(expert[None], region.reshape(1, -1), tokens)
    send_d = dispatch_grads(place, gate.reshape(1, -1), out_grad)

    def to_owner(parts):
        return [parts[0]] + [lax.ppermute(parts[r], "expert", ring(r)) for r in (1, 2, 3)]

    own_x = to_owner(send_x)
    both_x = own_x + [swap_core(p) for p in own_x]
    own_d = to_owner(send_d)
    act, slope, rows_x, mark = forward(table, both_x, weight_in)
    act, slope = in_hbm(act), in_hbm(slope)
    own_d = [after(part, mark) for part in own_d]
    both_d = own_d + [swap_core(p) for p in own_d]

    out_low, out_high, rows_d, mark = outer_first(table, act, both_d)
    hop = first_hop(out_low, out_high, "x")
    pre_a, in_low, in_high, mark = backward(
        table, rows_d, rows_x, slope, weight_out, 0, 1, (mark,)
    )
    out_sides = outer_rest(act, rows_d, 1, 2, (mark,))
    *pair, mark = join(out_sides, hop)
    out_parts = second_hop(*pair, "x")
    hop = first_hop(in_low, in_high, "y")
    pre_b, in_sides, mark = backward(table, rows_d, rows_x, slope, weight_out, 1, 2, (mark,))
    *pair, mark = join(in_sides, hop)
    in_parts = second_hop(*pair, "y")
    pre_c, in_own, mark = backward(table, rows_d, rows_x, slope, weight_out, 3, 1, (mark,))
    out_own = outer_rest(act, rows_d, 3, 1, (mark,))
    own = sum_cores(row_gradients(table, (pre_a, pre_b, pre_c), weight_in, ()))
    back = lax.all_to_all(own, "expert", split_axis=0, concat_axis=0, tiled=True)

    keep, sides, low, high, mark = combine(out_own, out_parts)
    *pair, mark = join(sides, first_hop(low, high, "y"))
    grad_out = add(keep, *second_hop(*pair, "y")) * scale
    keep, sides, low, high, _ = combine(after(in_own, mark), in_parts)
    *pair, _ = join(sides, first_hop(low, high, "x"))
    grad_in = add(keep, *second_hop(*pair, "x")) * scale
    token_grad = restore_order(expert[None], place, back)
    return token_grad, grad_in[None], grad_out[None]


def solution(mesh):
    chips = Mesh(mesh.devices.reshape(4, 4, 2, 4), ("y", "x", "core", "expert"))
    rows = ("y", "x", "core", "expert")
    plane = ("y", "x", "core")
    return jax.shard_map(
        local,
        mesh=chips,
        in_specs=(
            P(rows, None),
            P(rows, None),
            P(rows),
            P(rows, None),
            P("expert", None, None),
            P("expert", None, None),
        ),
        out_specs=(P(rows, None), P("expert", plane, None), P("expert", plane, None)),
        check_vma=False,
    )
```

```python
import math

import jax
import jax.numpy as jnp
from jax import lax
from jax.experimental import pallas as pl
from jax.experimental.pallas import tpu as pltpu
from jax.sharding import Mesh, PartitionSpec as P

BF16 = jnp.bfloat16
F32 = jnp.float32
VMEM_LIMIT = 28 * 1024 * 1024
ORDER = (2, 1, 3, 0)
INVERSE = (3, 1, 0, 2)


def ring(step):
    return [(i, (i + step) % 4) for i in range(4)]


def swap_core(array):
    return lax.ppermute(array, "core", [(0, 1), (1, 0)])


def params():
    return pltpu.CompilerParams(vmem_limit_bytes=VMEM_LIMIT)


def cost(nbytes=1024):
    return pl.CostEstimate(flops=0, bytes_accessed=int(nbytes), transcendentals=0)


def shape(rows, cols, dtype=BF16):
    return jax.ShapeDtypeStruct((rows, cols), dtype)


def dot_nt(a, b):
    return lax.dot_general(a, b, (((1,), (1,)), ((), ())), preferred_element_type=F32)


def dot_nn(a, b):
    return lax.dot_general(a, b, (((1,), (0,)), ((), ())), preferred_element_type=F32)


def dot_tn(a, b):
    return lax.dot_general(a, b, (((0,), (0,)), ((), ())), preferred_element_type=F32)


def gelu_parts(pre_act):
    root_two_pi = 0.7978845608028654
    square = pre_act * pre_act
    inner = pre_act * (root_two_pi + root_two_pi * 0.044715 * square)
    halved = 0.5 + 0.5 * jnp.tanh(inner)
    value = pre_act * halved
    slope_of_inner = 2.0 * root_two_pi + 6.0 * root_two_pi * 0.044715 * square
    return value, halved + value * (1.0 - halved) * slope_of_inner


VMEM = pl.BlockSpec(memory_space=pltpu.VMEM)
ANY = pl.BlockSpec(memory_space=pl.ANY)


def bucket(where_ref, r):
    return pl.ds(pl.multiple_of(jnp.bitwise_and(where_ref[0] + r, 3) * 128, 128), 128)


def dispatch_tokens(where, region, tokens):
    n, width = tokens.shape

    def body(where_ref, region_hbm, tok_hbm, place_ref, *refs):
        outs, (region_ref, tok_ref, sems) = refs[:4], refs[4:]
        copies = [
            pltpu.make_async_copy(region_hbm, region_ref, sems.at[0]),
            pltpu.make_async_copy(tok_hbm, tok_ref, sems.at[1]),
        ]
        for copy in copies:
            copy.start()
        upper = (
            lax.broadcasted_iota(jnp.int32, (n, n), 0) < lax.broadcasted_iota(jnp.int32, (n, n), 1)
        ).astype(F32)
        copies[0].wait()
        dest = region_ref[...]
        onehot = (dest == lax.broadcasted_iota(jnp.int32, (8, n), 0)).astype(F32)
        before = dot_nn(onehot.astype(BF16), upper.astype(BF16))
        rank = jnp.sum(before * onehot, axis=0, keepdims=True).astype(jnp.int32)
        slot = dest * 128 + rank
        place = (slot == lax.broadcasted_iota(jnp.int32, (512, n), 0)).astype(F32).astype(BF16)
        place_ref[...] = place
        copies[1].wait()
        for r, out in enumerate(outs):
            out[...] = dot_nn(place_ref[bucket(where_ref, r), :], tok_ref[...]).astype(BF16)

    return pl.pallas_call(
        body,
        out_shape=[shape(512, n)] + [shape(128, width)] * 4,
        in_specs=[pl.BlockSpec(memory_space=pltpu.SMEM)] + [HBM] * 2,
        out_specs=[VMEM] * 5,
        scratch_shapes=[
            pltpu.VMEM((1, n), jnp.int32),
            pltpu.VMEM((n, width), BF16),
            pltpu.SemaphoreType.DMA((2,)),
        ],
        compiler_params=params(),
        cost_estimate=cost(4 * n * width * 2),
    )(where, region, tokens)


def dispatch_grads(where, place, gate, grads):
    n, width = grads.shape

    def body(where_ref, place_ref, gate_ref, grad_ref, *outs):
        column = jnp.transpose(jnp.broadcast_to(gate_ref[...], (128, n)))[:, :1]
        scaled = (column * grad_ref[...].astype(F32)).astype(BF16)
        for r, out in enumerate(outs):
            out[...] = dot_nn(place_ref[bucket(where_ref, r), :], scaled).astype(BF16)

    return pl.pallas_call(
        body,
        out_shape=[shape(128, width)] * 4,
        in_specs=[pl.BlockSpec(memory_space=pltpu.SMEM)] + [VMEM] * 3,
        out_specs=[VMEM] * 4,
        compiler_params=params(),
        cost_estimate=cost(4 * n * width * 2),
    )(where, place, gate, grads)


HBM = pl.BlockSpec(memory_space=pltpu.HBM)


def block_scratch(width, count):
    return [pltpu.VMEM((512 * count, width), BF16), pltpu.SemaphoreType.DMA((4 * count,))]


def block_group(table_ref, weight_ref, w_buf, sems, offset, count):
    step = pl.program_id(0)

    def fetch(k):
        block = pl.multiple_of(table_ref[offset + k] * 128, 128)
        place = pl.multiple_of(k * 128, 128)
        return pltpu.make_async_copy(
            weight_ref.at[pl.ds(block, 128), :], w_buf.at[pl.ds(place, 128), :], sems.at[k]
        )

    @pl.when(step == 0)
    def _():
        for k in range(4 * count):
            fetch(k).start()

    for q in range(4):
        fetch(4 * step + q).wait()
    return w_buf.at[pl.ds(pl.multiple_of(step * 512, 512), 512), :]


def after(array, *others):
    def body(*refs):
        del refs

    return pl.pallas_call(
        body,
        in_specs=[ANY] * (1 + len(others)),
        out_specs=ANY,
        out_shape=jax.ShapeDtypeStruct(array.shape, array.dtype),
        input_output_aliases={0: 0},
        compiler_params=params(),
        cost_estimate=cost(),
    )(array, *others)


MARK = jax.ShapeDtypeStruct((8, 128), F32)
MARK_SPEC = pl.BlockSpec((8, 128), lambda i, *_: (0, 0))


def fixed(rows, cols):
    return pl.BlockSpec((rows, cols), lambda i, *_: (0, 0))


def merge(table_ref, part_refs, all_ref):
    for k, ref in enumerate(part_refs):
        begin = pl.multiple_of(k // 4 * 512 + table_ref[48 + k % 4] * 128, 128)
        all_ref[pl.ds(begin, 128), :] = ref[...]


def forward(table, parts, weight):
    width = weight.shape[1]
    tok = 128 * len(parts)

    def body(table_ref, *refs):
        part_refs, weight_ref = refs[: len(parts)], refs[len(parts)]
        act_ref, slope_ref, all_ref, mark_ref, w_buf, sems = refs[len(parts) + 1 :]

        @pl.when(pl.program_id(0) == 0)
        def _():
            mark_ref[...] = jnp.zeros_like(mark_ref)
            merge(table_ref, part_refs, all_ref)

        w_ref = block_group(table_ref, weight_ref, w_buf, sems, 0, 4)
        for c in range(tok // 256):
            cols = slice(c * 256, (c + 1) * 256)
            act, slope = gelu_parts(dot_nt(w_ref[...], all_ref[cols, :]))
            act_ref[:, cols] = act.astype(BF16)
            slope_ref[:, cols] = slope.astype(BF16)

    return pl.pallas_call(
        body,
        grid_spec=pltpu.PrefetchScalarGridSpec(
            num_scalar_prefetch=1,
            grid=(4,),
            in_specs=[VMEM] * len(parts) + [HBM],
            out_specs=[pl.BlockSpec((512, tok), lambda i, *_: (i, 0))] * 2
            + [fixed(tok, width), MARK_SPEC],
            scratch_shapes=block_scratch(width, 4),
        ),
        out_shape=[pltpu.HBM((2048, tok), BF16)] * 2 + [shape(tok, width), MARK],
        compiler_params=params(),
        cost_estimate=cost(2**24),
    )(table, *parts, weight)


def outer_first(table, act, parts):
    width = parts[0].shape[1]
    tok = 128 * len(parts)

    def body(table_ref, act_ref, *refs):
        part_refs, (low_ref, high_ref, all_ref, mark_ref) = refs[: len(parts)], refs[len(parts) :]
        mark_ref[...] = jnp.zeros_like(mark_ref)
        merge(table_ref, part_refs, all_ref)
        low_ref[...] = dot_nn(act_ref[:256, :], all_ref[...]).astype(BF16)
        high_ref[...] = dot_nn(act_ref[256:, :], all_ref[...]).astype(BF16)

    return pl.pallas_call(
        body,
        grid_spec=pltpu.PrefetchScalarGridSpec(
            num_scalar_prefetch=1,
            grid=(1,),
            in_specs=[fixed(512, tok)] + [VMEM] * len(parts),
            out_specs=[fixed(256, width)] * 2 + [fixed(tok, width), MARK_SPEC],
        ),
        out_shape=[shape(256, width)] * 2 + [shape(tok, width), MARK],
        compiler_params=params(),
        cost_estimate=cost(2**22),
    )(table, act, *parts)


def outer_rest(act, rows, first, count, deps):
    tok, width = rows.shape

    def body(act_ref, rows_ref, *refs):
        out_ref = refs[len(deps)]
        out_ref[...] = dot_nn(act_ref[...], rows_ref[...]).astype(BF16)

    return pl.pallas_call(
        body,
        grid=(count,),
        in_specs=[pl.BlockSpec((512, tok), lambda i: (i + first, 0)), VMEM] + [ANY] * len(deps),
        out_specs=pl.BlockSpec((512, width), lambda i: (i, 0)),
        out_shape=shape(512 * count, width),
        compiler_params=params(),
        cost_estimate=cost(2**20 * (2 + 2 * count)),
    )(act, rows, *deps)


def backward(table, grads, rows, slope, weight, first, count, deps):
    tok, width = rows.shape
    split = first == 0

    def body(table_ref, grads_ref, rows_ref, slope_ref, weight_ref, *refs):
        pre_ref, *outs, mark_ref, w_buf, w_sems, s_buf, s_sems = refs[len(deps) :]
        mark_ref[...] = jnp.zeros_like(mark_ref)
        w_ref = block_group(table_ref, weight_ref, w_buf, w_sems, 16 + 4 * first, count)
        s_ref = block_group(table_ref, slope_ref, s_buf, s_sems, 32 + 4 * first, count)
        for c in range(tok // 256):
            cols = slice(c * 256, (c + 1) * 256)
            act_grad = dot_nt(w_ref[...], grads_ref[cols, :])
            pre_ref[:, cols] = (act_grad * s_ref[:, cols].astype(F32)).astype(BF16)
        span = 512 // len(outs)
        for k, out in enumerate(outs):
            out[...] = dot_nn(pre_ref[k * span : (k + 1) * span, :], rows_ref[...]).astype(BF16)

    def groups(cols):
        return pl.BlockSpec((512, cols), lambda i, *_: (i, 0))

    return pl.pallas_call(
        body,
        grid_spec=pltpu.PrefetchScalarGridSpec(
            num_scalar_prefetch=1,
            grid=(count,),
            in_specs=[VMEM] * 2 + [HBM] * 2 + [ANY] * len(deps),
            out_specs=[groups(tok)]
            + ([fixed(256, width)] * 2 if split else [groups(width)])
            + [MARK_SPEC],
            scratch_shapes=block_scratch(width, count) + block_scratch(tok, count),
        ),
        out_shape=[shape(512 * count, tok)]
        + ([shape(256, width)] * 2 if split else [shape(512 * count, width)])
        + [MARK],
        compiler_params=params(),
        cost_estimate=cost(2**20 * (2 + 4 * count)),
    )(table, grads, rows, slope, weight, *deps)


def row_gradients(table, pre, weight, deps):
    width = weight.shape[1]
    rows = 512

    def body(table_ref, a_ref, b_ref, c_ref, weight_ref, *refs):
        out_ref, w_buf, sems, total = refs[len(deps) :]
        step = pl.program_id(0)
        w_ref = block_group(table_ref, weight_ref, w_buf, sems, 16, 4)

        @pl.when(step == 0)
        def _():
            total[...] = dot_tn(a_ref[...], w_ref[...])

        @pl.when(jnp.logical_and(step > 0, step < 3))
        def _():
            begin = pl.multiple_of((step - 1) * 512, 512)
            total[...] += dot_tn(b_ref[pl.ds(begin, 512), :], w_ref[...])

        @pl.when(step == 3)
        def _():
            final = (total[...] + dot_tn(c_ref[...], w_ref[...])).astype(BF16)
            own = table_ref[52]
            out_ref[pl.ds(pl.multiple_of(own * rows, rows), rows), :] = final[:rows]
            out_ref[pl.ds(pl.multiple_of((1 - own) * rows, rows), rows), :] = final[rows:]

    return pl.pallas_call(
        body,
        grid_spec=pltpu.PrefetchScalarGridSpec(
            num_scalar_prefetch=1,
            grid=(4,),
            in_specs=[VMEM] * 3 + [HBM] + [ANY] * len(deps),
            out_specs=fixed(2 * rows, width),
            scratch_shapes=block_scratch(width, 4) + [pltpu.VMEM((2 * rows, width), F32)],
        ),
        out_shape=shape(2 * rows, width),
        compiler_params=params(),
        cost_estimate=cost(2**23 + 2**22),
    )(table, *pre, weight, *deps)


def join(sides, arrived):
    n, width = sides.shape
    h = n // 4

    def body(sides_ref, from_next, from_prev, up_ref, down_ref, mark_ref):
        mark_ref[...] = jnp.zeros_like(mark_ref)
        up_ref[:h, :] = sides_ref[:h, :]
        up_ref[h:, :] = add(sides_ref[h : 2 * h, :], from_prev[...]).astype(BF16)
        down_ref[:h, :] = add(sides_ref[2 * h : 3 * h, :], from_next[...]).astype(BF16)
        down_ref[h:, :] = sides_ref[3 * h :, :]

    return pl.pallas_call(
        body,
        out_shape=[shape(2 * h, width)] * 2 + [MARK],
        in_specs=[VMEM] * 3,
        out_specs=[VMEM] * 3,
        compiler_params=params(),
        cost_estimate=cost(4 * n * width),
    )(sides, *arrived)


def restore_order(place, rows):
    n, width = place.shape[1], rows.shape[1]

    def body(place_ref, rows_ref, out_ref):
        out_ref[...] = dot_tn(place_ref[...], rows_ref[...]).astype(BF16)

    return pl.pallas_call(
        body,
        out_shape=shape(n, width),
        in_specs=[VMEM] * 2,
        out_specs=VMEM,
        compiler_params=params(),
        cost_estimate=cost(2**21),
    )(place, rows)


def add(*terms):
    total = terms[0].astype(F32)
    for term in terms[1:]:
        total = total + term.astype(F32)
    return total


def first_hop(low, high, axis):
    return lax.ppermute(low, axis, ring(3)), lax.ppermute(high, axis, ring(1))


def second_hop(up, down, axis):
    return lax.ppermute(up, axis, ring(1)), lax.ppermute(down, axis, ring(3))


def cut(total, refs):
    keep_ref, sides_ref, low_ref, high_ref, mark_ref = refs
    n = total.shape[0]
    q = n // 4
    mark_ref[...] = jnp.zeros_like(mark_ref)
    total = total.astype(BF16)
    keep_ref[...] = total[:q]
    sides_ref[:q, :] = total[q : 2 * q]
    low_ref[...] = total[2 * q : 2 * q + q // 2]
    high_ref[...] = total[2 * q + q // 2 : 3 * q]
    sides_ref[q:, :] = total[3 * q :]


def cut_shapes(n, width):
    return [shape(n // k, width) for k in (4, 2, 8, 8)] + [MARK]


def combine(own, received):
    n, width = own.shape

    def body(own_ref, left, right, *refs):
        cut(add(own_ref[...], left[...], right[...]), refs)

    return pl.pallas_call(
        body,
        out_shape=cut_shapes(n, width),
        in_specs=[VMEM] * 3,
        out_specs=[VMEM] * 5,
        compiler_params=params(),
        cost_estimate=cost(8 * n * width),
    )(own, *received)


def combine_product(act, rows, group, received):
    tok, width = rows.shape

    def body(act_ref, rows_ref, left, right, *refs):
        cut(dot_nn(act_ref[...], rows_ref[...]) + add(left[...], right[...]), refs)

    shapes = cut_shapes(512, width)
    return pl.pallas_call(
        body,
        grid=(1,),
        in_specs=[pl.BlockSpec((512, tok), lambda i: (group, 0))] + [VMEM] * 3,
        out_specs=[fixed(*out.shape) for out in shapes],
        out_shape=shapes,
        compiler_params=params(),
        cost_estimate=cost(10 * 512 * width),
    )(act, rows, *received)


def in_hbm(array):
    return pltpu.with_memory_space_constraint(array, pltpu.HBM)


def sum_cores(terms):
    terms = lax.all_to_all(terms, "core", split_axis=0, concat_axis=0, tiled=True)
    n = terms.shape[0] // 2
    return add(terms[:n], terms[n:]).astype(BF16)


def local(tokens, out_grad, gate, region, w_in, w_out):
    expert = lax.axis_index("expert").astype(jnp.int32)
    x, y, core = (lax.axis_index(a).astype(jnp.int32) for a in ("x", "y", "core"))
    scale = 1.0 / math.sqrt(float(tokens.shape[0] * lax.axis_size(("y", "x", "core"))))
    order = jnp.array(ORDER, jnp.int32)
    every = jnp.arange(4, dtype=jnp.int32)
    by_x = ((((y + every[None, :]) % 4) * 4 + (x + order[:, None]) % 4) * 2 + core).reshape(16)
    by_y = ((((y + order[:, None]) % 4) * 4 + (x + every[None, :]) % 4) * 2 + core).reshape(16)
    same = jnp.array([INVERSE[q] * 4 + ORDER[p] for p in range(4) for q in range(4)], jnp.int32)
    table = jnp.concatenate([by_x, by_y, same, (expert - every) % 4, core[None]])
    weight_in, weight_out = in_hbm(w_in[0]), in_hbm(w_out[0])

    place, *send_x = dispatch_tokens(
        expert[None], in_hbm(region.reshape(1, -1)), in_hbm(tokens)
    )
    send_d = dispatch_grads(expert[None], place, gate.reshape(1, -1), out_grad)

    def to_owner(parts):
        return [parts[0]] + [lax.ppermute(parts[r], "expert", ring(r)) for r in (1, 2, 3)]

    own_x = to_owner(send_x)
    both_x = own_x + [swap_core(p) for p in own_x]
    own_d = to_owner(send_d)
    act, slope, rows_x, mark = forward(table, both_x, weight_in)
    act, slope = in_hbm(act), in_hbm(slope)
    own_d = [after(part, mark) for part in own_d]
    both_d = own_d + [swap_core(p) for p in own_d]

    out_low, out_high, rows_d, mark = outer_first(table, act, both_d)
    hop = first_hop(out_low, out_high, "x")
    pre_a, in_low, in_high, mark = backward(
        table, rows_d, rows_x, slope, weight_out, 0, 1, (mark,)
    )
    out_sides = outer_rest(act, rows_d, 1, 2, (mark,))
    *pair, mark = join(out_sides, hop)
    out_parts = second_hop(*pair, "x")
    hop = first_hop(in_low, in_high, "y")
    pre_b, in_sides, mark = backward(table, rows_d, rows_x, slope, weight_out, 1, 2, (mark,))
    *pair, mark = join(in_sides, hop)
    in_parts = second_hop(*pair, "y")
    pre_c, in_own, mark = backward(table, rows_d, rows_x, slope, weight_out, 3, 1, (mark,))
    own = sum_cores(row_gradients(table, (pre_a, pre_b, pre_c), weight_in, ()))
    back = lax.all_to_all(own, "expert", split_axis=0, concat_axis=0, tiled=True)

    out_keep, out_sides, low, high, mark = combine_product(act, rows_d, 3, out_parts)
    out_hop = first_hop(low, high, "y")
    in_keep, in_sides, low, high, mark = combine(after(in_own, mark), in_parts)
    in_hop = first_hop(low, high, "x")
    *pair, mark = join(after(out_sides, mark), out_hop)
    out_parts = second_hop(*pair, "y")
    *pair, _ = join(after(in_sides, mark), in_hop)
    in_parts = second_hop(*pair, "x")
    grad_out = add(out_keep, *out_parts) * scale
    grad_in = add(in_keep, *in_parts) * scale
    token_grad = restore_order(place, back)
    return token_grad, grad_in[None], grad_out[None]


def solution(mesh):
    chips = Mesh(mesh.devices.reshape(4, 4, 2, 4), ("y", "x", "core", "expert"))
    rows = ("y", "x", "core", "expert")
    plane = ("y", "x", "core")
    return jax.shard_map(
        local,
        mesh=chips,
        in_specs=(
            P(rows, None),
            P(rows, None),
            P(rows),
            P(rows, None),
            P("expert", None, None),
            P("expert", None, None),
        ),
        out_specs=(P(rows, None), P("expert", plane, None), P("expert", plane, None)),
        check_vma=False,
    )
```

```python
import math

import jax
import jax.numpy as jnp
from jax import lax
from jax.experimental import pallas as pl
from jax.experimental.pallas import tpu as pltpu
from jax.sharding import Mesh, PartitionSpec as P

BF16 = jnp.bfloat16
F32 = jnp.float32
VMEM_LIMIT = 28 * 1024 * 1024
ORDER = (2, 1, 3, 0)
INVERSE = (3, 1, 0, 2)


def ring(step):
    return [(i, (i + step) % 4) for i in range(4)]


def swap_core(array):
    return lax.ppermute(array, "core", [(0, 1), (1, 0)])


def params():
    return pltpu.CompilerParams(vmem_limit_bytes=VMEM_LIMIT)


def cost(nbytes=1024):
    return pl.CostEstimate(flops=0, bytes_accessed=int(nbytes), transcendentals=0)


def shape(rows, cols, dtype=BF16):
    return jax.ShapeDtypeStruct((rows, cols), dtype)


def dot_nt(a, b):
    return lax.dot_general(a, b, (((1,), (1,)), ((), ())), preferred_element_type=F32)


def dot_nn(a, b):
    return lax.dot_general(a, b, (((1,), (0,)), ((), ())), preferred_element_type=F32)


def dot_tn(a, b):
    return lax.dot_general(a, b, (((0,), (0,)), ((), ())), preferred_element_type=F32)


def gelu_parts(pre_act):
    root_two_pi = 0.7978845608028654
    square = pre_act * pre_act
    inner = pre_act * (root_two_pi + root_two_pi * 0.044715 * square)
    halved = 0.5 + 0.5 * jnp.tanh(inner)
    value = pre_act * halved
    slope_of_inner = 2.0 * root_two_pi + 6.0 * root_two_pi * 0.044715 * square
    return value, halved + value * (1.0 - halved) * slope_of_inner


VMEM = pl.BlockSpec(memory_space=pltpu.VMEM)
ANY = pl.BlockSpec(memory_space=pl.ANY)


def bucket(where_ref, r):
    return pl.ds(pl.multiple_of(jnp.bitwise_and(where_ref[0] + r, 3) * 128, 128), 128)


def dispatch_tokens(where, region, tokens):
    n, width = tokens.shape

    def body(where_ref, region_hbm, tok_hbm, place_ref, *refs):
        outs, (region_ref, tok_ref, sems) = refs[:4], refs[4:]
        copies = [
            pltpu.make_async_copy(region_hbm, region_ref, sems.at[0]),
            pltpu.make_async_copy(tok_hbm, tok_ref, sems.at[1]),
        ]
        for copy in copies:
            copy.start()
        upper = (
            lax.broadcasted_iota(jnp.int32, (n, n), 0) < lax.broadcasted_iota(jnp.int32, (n, n), 1)
        ).astype(F32)
        copies[0].wait()
        dest = region_ref[...]
        onehot = (dest == lax.broadcasted_iota(jnp.int32, (8, n), 0)).astype(F32)
        before = dot_nn(onehot.astype(BF16), upper.astype(BF16))
        rank = jnp.sum(before * onehot, axis=0, keepdims=True).astype(jnp.int32)
        slot = dest * 128 + rank
        place = (slot == lax.broadcasted_iota(jnp.int32, (512, n), 0)).astype(F32).astype(BF16)
        place_ref[...] = place
        copies[1].wait()
        for r, out in enumerate(outs):
            out[...] = dot_nn(place_ref[bucket(where_ref, r), :], tok_ref[...]).astype(BF16)

    return pl.pallas_call(
        body,
        out_shape=[shape(512, n)] + [shape(128, width)] * 4,
        in_specs=[pl.BlockSpec(memory_space=pltpu.SMEM)] + [HBM] * 2,
        out_specs=[VMEM] * 5,
        scratch_shapes=[
            pltpu.VMEM((1, n), jnp.int32),
            pltpu.VMEM((n, width), BF16),
            pltpu.SemaphoreType.DMA((2,)),
        ],
        compiler_params=params(),
        cost_estimate=cost(4 * n * width * 2),
    )(where, region, tokens)


def dispatch_grads(where, place, gate, grads):
    n, width = grads.shape

    def body(where_ref, place_ref, gate_ref, grad_ref, *outs):
        column = jnp.transpose(jnp.broadcast_to(gate_ref[...], (128, n)))[:, :1]
        scaled = (column * grad_ref[...].astype(F32)).astype(BF16)
        for r, out in enumerate(outs):
            out[...] = dot_nn(place_ref[bucket(where_ref, r), :], scaled).astype(BF16)

    return pl.pallas_call(
        body,
        out_shape=[shape(128, width)] * 4,
        in_specs=[pl.BlockSpec(memory_space=pltpu.SMEM)] + [VMEM] * 3,
        out_specs=[VMEM] * 4,
        compiler_params=params(),
        cost_estimate=cost(4 * n * width * 2),
    )(where, place, gate, grads)


HBM = pl.BlockSpec(memory_space=pltpu.HBM)


def block_scratch(width, count):
    return [pltpu.VMEM((512 * count, width), BF16), pltpu.SemaphoreType.DMA((4 * count,))]


def block_group(table_ref, weight_ref, w_buf, sems, offset, count):
    step = pl.program_id(0)

    def fetch(k):
        block = pl.multiple_of(table_ref[offset + k] * 128, 128)
        place = pl.multiple_of(k * 128, 128)
        return pltpu.make_async_copy(
            weight_ref.at[pl.ds(block, 128), :], w_buf.at[pl.ds(place, 128), :], sems.at[k]
        )

    @pl.when(step == 0)
    def _():
        for k in range(4 * count):
            fetch(k).start()

    for q in range(4):
        fetch(4 * step + q).wait()
    return w_buf.at[pl.ds(pl.multiple_of(step * 512, 512), 512), :]


def after(array, *others):
    def body(*refs):
        del refs

    return pl.pallas_call(
        body,
        in_specs=[ANY] * (1 + len(others)),
        out_specs=ANY,
        out_shape=jax.ShapeDtypeStruct(array.shape, array.dtype),
        input_output_aliases={0: 0},
        compiler_params=params(),
        cost_estimate=cost(),
    )(array, *others)


MARK = jax.ShapeDtypeStruct((8, 128), F32)
MARK_SPEC = pl.BlockSpec((8, 128), lambda i, *_: (0, 0))


def fixed(rows, cols):
    return pl.BlockSpec((rows, cols), lambda i, *_: (0, 0))


def merge(table_ref, part_refs, all_ref):
    for k, ref in enumerate(part_refs):
        begin = pl.multiple_of(k // 4 * 512 + table_ref[48 + k % 4] * 128, 128)
        all_ref[pl.ds(begin, 128), :] = ref[...]


def forward(table, parts, weight):
    width = weight.shape[1]
    tok = 128 * len(parts)

    def body(table_ref, *refs):
        part_refs, weight_ref = refs[: len(parts)], refs[len(parts)]
        act_ref, slope_ref, all_ref, mark_ref, w_buf, sems = refs[len(parts) + 1 :]

        @pl.when(pl.program_id(0) == 0)
        def _():
            mark_ref[...] = jnp.zeros_like(mark_ref)
            merge(table_ref, part_refs, all_ref)

        w_ref = block_group(table_ref, weight_ref, w_buf, sems, 0, 4)
        pre_act = dot_nt(w_ref[...], all_ref[:256, :])
        for begin in range(0, tok, 256):
            cols = slice(begin, begin + 256)
            if begin + 256 < tok:
                following = dot_nt(w_ref[...], all_ref[begin + 256 : begin + 512, :])
            act, slope = gelu_parts(pre_act)
            act_ref[:, cols] = act.astype(BF16)
            slope_ref[:, cols] = slope.astype(BF16)
            pre_act = following

    return pl.pallas_call(
        body,
        grid_spec=pltpu.PrefetchScalarGridSpec(
            num_scalar_prefetch=1,
            grid=(4,),
            in_specs=[VMEM] * len(parts) + [HBM],
            out_specs=[pl.BlockSpec((512, tok), lambda i, *_: (i, 0))] * 2
            + [fixed(tok, width), MARK_SPEC],
            scratch_shapes=block_scratch(width, 4),
        ),
        out_shape=[pltpu.HBM((2048, tok), BF16)] * 2 + [shape(tok, width), MARK],
        compiler_params=params(),
        cost_estimate=cost(2**24),
    )(table, *parts, weight)


def outer_first(table, act, parts):
    width = parts[0].shape[1]
    tok = 128 * len(parts)

    def body(table_ref, act_ref, *refs):
        part_refs, (low_ref, high_ref, all_ref, mark_ref) = refs[: len(parts)], refs[len(parts) :]
        mark_ref[...] = jnp.zeros_like(mark_ref)
        merge(table_ref, part_refs, all_ref)
        low_ref[...] = dot_nn(act_ref[:256, :], all_ref[...]).astype(BF16)
        high_ref[...] = dot_nn(act_ref[256:, :], all_ref[...]).astype(BF16)

    return pl.pallas_call(
        body,
        grid_spec=pltpu.PrefetchScalarGridSpec(
            num_scalar_prefetch=1,
            grid=(1,),
            in_specs=[fixed(512, tok)] + [VMEM] * len(parts),
            out_specs=[fixed(256, width)] * 2 + [fixed(tok, width), MARK_SPEC],
        ),
        out_shape=[shape(256, width)] * 2 + [shape(tok, width), MARK],
        compiler_params=params(),
        cost_estimate=cost(2**22),
    )(table, act, *parts)


def outer_rest(act, rows, first, count, deps):
    tok, width = rows.shape

    def body(act_ref, rows_ref, *refs):
        out_ref = refs[len(deps)]
        out_ref[...] = dot_nn(act_ref[...], rows_ref[...]).astype(BF16)

    return pl.pallas_call(
        body,
        grid=(count,),
        in_specs=[pl.BlockSpec((512, tok), lambda i: (i + first, 0)), VMEM] + [ANY] * len(deps),
        out_specs=pl.BlockSpec((512, width), lambda i: (i, 0)),
        out_shape=shape(512 * count, width),
        compiler_params=params(),
        cost_estimate=cost(2**20 * (2 + 2 * count)),
    )(act, rows, *deps)


def backward(table, grads, rows, slope, weight, first, count, deps):
    tok, width = rows.shape
    split = first == 0

    def body(table_ref, grads_ref, rows_ref, slope_ref, weight_ref, *refs):
        pre_ref, *outs, mark_ref, w_buf, w_sems, s_buf, s_sems = refs[len(deps) :]
        mark_ref[...] = jnp.zeros_like(mark_ref)
        w_ref = block_group(table_ref, weight_ref, w_buf, w_sems, 16 + 4 * first, count)
        s_ref = block_group(table_ref, slope_ref, s_buf, s_sems, 32 + 4 * first, count)
        act_grad = dot_nt(w_ref[...], grads_ref[:256, :])
        for begin in range(0, tok, 256):
            cols = slice(begin, begin + 256)
            if begin + 256 < tok:
                following = dot_nt(w_ref[...], grads_ref[begin + 256 : begin + 512, :])
            pre_ref[:, cols] = (act_grad * s_ref[:, cols].astype(F32)).astype(BF16)
            act_grad = following
        span = 512 // len(outs)
        for k, out in enumerate(outs):
            out[...] = dot_nn(pre_ref[k * span : (k + 1) * span, :], rows_ref[...]).astype(BF16)

    def groups(cols):
        return pl.BlockSpec((512, cols), lambda i, *_: (i, 0))

    return pl.pallas_call(
        body,
        grid_spec=pltpu.PrefetchScalarGridSpec(
            num_scalar_prefetch=1,
            grid=(count,),
            in_specs=[VMEM] * 2 + [HBM] * 2 + [ANY] * len(deps),
            out_specs=[groups(tok)]
            + ([fixed(256, width)] * 2 if split else [groups(width)])
            + [MARK_SPEC],
            scratch_shapes=block_scratch(width, count) + block_scratch(tok, count),
        ),
        out_shape=[shape(512 * count, tok)]
        + ([shape(256, width)] * 2 if split else [shape(512 * count, width)])
        + [MARK],
        compiler_params=params(),
        cost_estimate=cost(2**20 * (2 + 4 * count)),
    )(table, grads, rows, slope, weight, *deps)


def row_gradients(table, pre, weight, deps):
    width = weight.shape[1]
    rows = 512

    def body(table_ref, a_ref, b_ref, c_ref, weight_ref, *refs):
        out_ref, w_buf, sems, total = refs[len(deps) :]
        step = pl.program_id(0)
        w_ref = block_group(table_ref, weight_ref, w_buf, sems, 16, 4)

        @pl.when(step == 0)
        def _():
            total[...] = dot_tn(a_ref[...], w_ref[...])

        @pl.when(jnp.logical_and(step > 0, step < 3))
        def _():
            begin = pl.multiple_of((step - 1) * 512, 512)
            total[...] += dot_tn(b_ref[pl.ds(begin, 512), :], w_ref[...])

        @pl.when(step == 3)
        def _():
            final = (total[...] + dot_tn(c_ref[...], w_ref[...])).astype(BF16)
            own = table_ref[52]
            out_ref[pl.ds(pl.multiple_of(own * rows, rows), rows), :] = final[:rows]
            out_ref[pl.ds(pl.multiple_of((1 - own) * rows, rows), rows), :] = final[rows:]

    return pl.pallas_call(
        body,
        grid_spec=pltpu.PrefetchScalarGridSpec(
            num_scalar_prefetch=1,
            grid=(4,),
            in_specs=[VMEM] * 3 + [HBM] + [ANY] * len(deps),
            out_specs=fixed(2 * rows, width),
            scratch_shapes=block_scratch(width, 4) + [pltpu.VMEM((2 * rows, width), F32)],
        ),
        out_shape=shape(2 * rows, width),
        compiler_params=params(),
        cost_estimate=cost(2**23 + 2**22),
    )(table, *pre, weight, *deps)


def join(*sums):
    n, width = sums[0][0].shape
    h = n // 4

    def body(*refs):
        ins, outs = refs[: 3 * len(sums)], refs[3 * len(sums) :]
        outs[-1][...] = jnp.zeros_like(outs[-1])
        for k in range(len(sums)):
            sides_ref, from_next, from_prev = ins[3 * k : 3 * k + 3]
            up_ref, down_ref = outs[2 * k : 2 * k + 2]
            up_ref[:h, :] = sides_ref[:h, :]
            up_ref[h:, :] = add(sides_ref[h : 2 * h, :], from_prev[...]).astype(BF16)
            down_ref[:h, :] = add(sides_ref[2 * h : 3 * h, :], from_next[...]).astype(BF16)
            down_ref[h:, :] = sides_ref[3 * h :, :]

    return pl.pallas_call(
        body,
        out_shape=[shape(2 * h, width)] * (2 * len(sums)) + [MARK],
        in_specs=[VMEM] * (3 * len(sums)),
        out_specs=[VMEM] * (2 * len(sums) + 1),
        compiler_params=params(),
        cost_estimate=cost(4 * n * width),
    )(*[array for sides, arrived in sums for array in (sides, *arrived)])


def restore_order(place, rows):
    n, width = place.shape[1], rows.shape[1]

    def body(place_ref, rows_ref, out_ref):
        out_ref[...] = dot_tn(place_ref[...], rows_ref[...]).astype(BF16)

    return pl.pallas_call(
        body,
        out_shape=shape(n, width),
        in_specs=[VMEM] * 2,
        out_specs=VMEM,
        compiler_params=params(),
        cost_estimate=cost(2**21),
    )(place, rows)


def add(*terms):
    total = terms[0].astype(F32)
    for term in terms[1:]:
        total = total + term.astype(F32)
    return total


def first_hop(low, high, axis):
    return lax.ppermute(low, axis, ring(3)), lax.ppermute(high, axis, ring(1))


def second_hop(up, down, axis):
    return lax.ppermute(up, axis, ring(1)), lax.ppermute(down, axis, ring(3))


def cut(total, refs):
    keep_ref, sides_ref, low_ref, high_ref, mark_ref = refs
    n = total.shape[0]
    q = n // 4
    mark_ref[...] = jnp.zeros_like(mark_ref)
    total = total.astype(BF16)
    keep_ref[...] = total[:q]
    sides_ref[:q, :] = total[q : 2 * q]
    low_ref[...] = total[2 * q : 2 * q + q // 2]
    high_ref[...] = total[2 * q + q // 2 : 3 * q]
    sides_ref[q:, :] = total[3 * q :]


def cut_shapes(n, width):
    return [shape(n // k, width) for k in (4, 2, 8, 8)] + [MARK]


def combine(own, received):
    n, width = own.shape

    def body(own_ref, left, right, *refs):
        cut(add(own_ref[...], left[...], right[...]), refs)

    return pl.pallas_call(
        body,
        out_shape=cut_shapes(n, width),
        in_specs=[VMEM] * 3,
        out_specs=[VMEM] * 5,
        compiler_params=params(),
        cost_estimate=cost(8 * n * width),
    )(own, *received)


def combine_product(act, rows, group, received):
    tok, width = rows.shape

    def body(act_ref, rows_ref, left, right, *refs):
        cut(dot_nn(act_ref[...], rows_ref[...]) + add(left[...], right[...]), refs)

    shapes = cut_shapes(512, width)
    return pl.pallas_call(
        body,
        grid=(1,),
        in_specs=[pl.BlockSpec((512, tok), lambda i: (group, 0))] + [VMEM] * 3,
        out_specs=[fixed(*out.shape) for out in shapes],
        out_shape=shapes,
        compiler_params=params(),
        cost_estimate=cost(10 * 512 * width),
    )(act, rows, *received)


def in_hbm(array):
    return pltpu.with_memory_space_constraint(array, pltpu.HBM)


def sum_cores(terms):
    terms = lax.all_to_all(terms, "core", split_axis=0, concat_axis=0, tiled=True)
    n = terms.shape[0] // 2
    return add(terms[:n], terms[n:]).astype(BF16)


def local(tokens, out_grad, gate, region, w_in, w_out):
    expert = lax.axis_index("expert").astype(jnp.int32)
    x, y, core = (lax.axis_index(a).astype(jnp.int32) for a in ("x", "y", "core"))
    scale = 1.0 / math.sqrt(float(tokens.shape[0] * lax.axis_size(("y", "x", "core"))))
    order = jnp.array(ORDER, jnp.int32)
    every = jnp.arange(4, dtype=jnp.int32)
    by_x = ((((y + every[None, :]) % 4) * 4 + (x + order[:, None]) % 4) * 2 + core).reshape(16)
    by_y = ((((y + order[:, None]) % 4) * 4 + (x + every[None, :]) % 4) * 2 + core).reshape(16)
    same = jnp.array([INVERSE[q] * 4 + ORDER[p] for p in range(4) for q in range(4)], jnp.int32)
    table = jnp.concatenate([by_x, by_y, same, (expert - every) % 4, core[None]])
    weight_in, weight_out = in_hbm(w_in[0]), in_hbm(w_out[0])

    place, *send_x = dispatch_tokens(
        expert[None], in_hbm(region.reshape(1, -1)), in_hbm(tokens)
    )
    send_d = dispatch_grads(expert[None], place, gate.reshape(1, -1), out_grad)

    def to_owner(parts):
        return [parts[0]] + [lax.ppermute(parts[r], "expert", ring(r)) for r in (1, 2, 3)]

    own_x = to_owner(send_x)
    both_x = own_x + [swap_core(p) for p in own_x]
    own_d = to_owner(send_d)
    act, slope, rows_x, mark = forward(table, both_x, weight_in)
    act, slope = in_hbm(act), in_hbm(slope)
    own_d = [after(part, mark) for part in own_d]
    both_d = own_d + [swap_core(p) for p in own_d]

    out_low, out_high, rows_d, mark = outer_first(table, act, both_d)
    hop = first_hop(out_low, out_high, "x")
    pre_a, in_low, in_high, mark = backward(
        table, rows_d, rows_x, slope, weight_out, 0, 1, (mark,)
    )
    out_sides = outer_rest(act, rows_d, 1, 2, (mark,))
    *pair, mark = join((out_sides, hop))
    out_parts = second_hop(*pair, "x")
    hop = first_hop(in_low, in_high, "y")
    pre_b, in_sides, mark = backward(table, rows_d, rows_x, slope, weight_out, 1, 2, (mark,))
    *pair, mark = join((in_sides, hop))
    in_parts = second_hop(*pair, "y")
    pre_c, in_own, mark = backward(table, rows_d, rows_x, slope, weight_out, 3, 1, (mark,))
    own = sum_cores(row_gradients(table, (pre_a, pre_b, pre_c), weight_in, ()))
    back = lax.all_to_all(own, "expert", split_axis=0, concat_axis=0, tiled=True)

    out_keep, out_sides, low, high, mark = combine_product(act, rows_d, 3, out_parts)
    out_hop = first_hop(low, high, "y")
    in_keep, in_sides, low, high, mark = combine(after(in_own, mark), in_parts)
    in_hop = first_hop(low, high, "x")
    *pairs, _ = join((out_sides, out_hop), (in_sides, in_hop))
    out_parts = second_hop(*pairs[:2], "y")
    in_parts = second_hop(*pairs[2:], "x")
    grad_out = add(out_keep, *out_parts) * scale
    grad_in = add(in_keep, *in_parts) * scale
    token_grad = restore_order(place, back)
    return token_grad, grad_in[None], grad_out[None]


def solution(mesh):
    chips = Mesh(mesh.devices.reshape(4, 4, 2, 4), ("y", "x", "core", "expert"))
    rows = ("y", "x", "core", "expert")
    plane = ("y", "x", "core")
    return jax.shard_map(
        local,
        mesh=chips,
        in_specs=(
            P(rows, None),
            P(rows, None),
            P(rows),
            P(rows, None),
            P("expert", None, None),
            P("expert", None, None),
        ),
        out_specs=(P(rows, None), P("expert", plane, None), P("expert", plane, None)),
        check_vma=False,
    )
```

```python
import math

import jax
import jax.numpy as jnp
from jax import lax
from jax.experimental import pallas as pl
from jax.experimental.pallas import tpu as pltpu
from jax.sharding import Mesh, PartitionSpec as P

BF16 = jnp.bfloat16
F32 = jnp.float32
VMEM_LIMIT = 18 * 1024 * 1024
ORDER = (2, 1, 3, 0)
INVERSE = (3, 1, 0, 2)


def ring(step):
    return [(i, (i + step) % 4) for i in range(4)]


def swap_core(array):
    return lax.ppermute(array, "core", [(0, 1), (1, 0)])


def params():
    return pltpu.CompilerParams(vmem_limit_bytes=VMEM_LIMIT)


def cost(nbytes=1024):
    return pl.CostEstimate(flops=0, bytes_accessed=int(nbytes), transcendentals=0)


def shape(rows, cols, dtype=BF16):
    return jax.ShapeDtypeStruct((rows, cols), dtype)


def dot_nt(a, b):
    return lax.dot_general(a, b, (((1,), (1,)), ((), ())), preferred_element_type=F32)


def dot_nn(a, b):
    return lax.dot_general(a, b, (((1,), (0,)), ((), ())), preferred_element_type=F32)


def dot_tn(a, b):
    return lax.dot_general(a, b, (((0,), (0,)), ((), ())), preferred_element_type=F32)


def gelu_parts(pre_act):
    root_two_pi = 0.7978845608028654
    square = pre_act * pre_act
    inner = pre_act * (root_two_pi + root_two_pi * 0.044715 * square)
    halved = 0.5 + 0.5 * jnp.tanh(inner)
    value = pre_act * halved
    slope_of_inner = 2.0 * root_two_pi + 6.0 * root_two_pi * 0.044715 * square
    return value, halved + value * (1.0 - halved) * slope_of_inner


VMEM = pl.BlockSpec(memory_space=pltpu.VMEM)
SMEM = pl.BlockSpec(memory_space=pltpu.SMEM)
ANY = pl.BlockSpec(memory_space=pl.ANY)


def bucket(where_ref, r):
    return pl.ds(pl.multiple_of(jnp.bitwise_and(where_ref[0] + r, 3) * 128, 128), 128)


def dispatch_tokens(where, region, tokens):
    n, width = tokens.shape

    def body(where_ref, region_hbm, tok_hbm, place_ref, *refs):
        outs, (region_ref, tok_ref, sems) = refs[:4], refs[4:]
        copies = [
            pltpu.make_async_copy(region_hbm, region_ref, sems.at[0]),
            pltpu.make_async_copy(tok_hbm, tok_ref, sems.at[1]),
        ]
        for copy in copies:
            copy.start()
        upper = (
            lax.broadcasted_iota(jnp.int32, (n, n), 0) < lax.broadcasted_iota(jnp.int32, (n, n), 1)
        ).astype(F32)
        copies[0].wait()
        dest = region_ref[...]
        onehot = (dest == lax.broadcasted_iota(jnp.int32, (8, n), 0)).astype(F32)
        before = dot_nn(onehot.astype(BF16), upper.astype(BF16))
        rank = jnp.sum(before * onehot, axis=0, keepdims=True).astype(jnp.int32)
        slot = dest * 128 + rank
        place = (slot == lax.broadcasted_iota(jnp.int32, (512, n), 0)).astype(F32).astype(BF16)
        place_ref[...] = place
        copies[1].wait()
        for r, out in enumerate(outs):
            out[...] = dot_nn(place_ref[bucket(where_ref, r), :], tok_ref[...]).astype(BF16)

    return pl.pallas_call(
        body,
        out_shape=[shape(512, n)] + [shape(128, width)] * 4,
        in_specs=[SMEM] + [HBM] * 2,
        out_specs=[VMEM] * 5,
        scratch_shapes=[
            pltpu.VMEM((1, n), jnp.int32),
            pltpu.VMEM((n, width), BF16),
            pltpu.SemaphoreType.DMA((2,)),
        ],
        compiler_params=params(),
        cost_estimate=cost(4 * n * width * 2),
    )(where, region, tokens)


def dispatch_grads(where, place, gate, grads, deps):
    n, width = grads.shape

    def body(where_ref, place_ref, gate_ref, grad_ref, *refs):
        outs = refs[len(deps) :]
        column = jnp.transpose(jnp.broadcast_to(gate_ref[...], (128, n)))[:, :1]
        scaled = (column * grad_ref[...].astype(F32)).astype(BF16)
        for r, out in enumerate(outs):
            out[...] = dot_nn(place_ref[bucket(where_ref, r), :], scaled).astype(BF16)

    return pl.pallas_call(
        body,
        out_shape=[shape(128, width)] * 4,
        in_specs=[SMEM] + [VMEM] * 3 + [ANY] * len(deps),
        out_specs=[VMEM] * 4,
        compiler_params=params(),
        cost_estimate=cost(4 * n * width * 2),
    )(where, place, gate, grads, *deps)


HBM = pl.BlockSpec(memory_space=pltpu.HBM)


def fetch_weights(table, w_in, w_out):
    count, width = 16, w_in.shape[1]

    def body(table_ref, in_hbm_ref, out_hbm_ref, in_ref, out_ref, mark_ref, sems):
        mark_ref[...] = jnp.zeros_like(mark_ref)
        copies = []
        for k in range(count):
            for side, (source, target) in enumerate(((in_hbm_ref, in_ref), (out_hbm_ref, out_ref))):
                block = pl.multiple_of(table_ref[count * side + k] * 128, 128)
                copies.append(
                    pltpu.make_async_copy(
                        source.at[pl.ds(block, 128), :],
                        target.at[pl.ds(k * 128, 128), :],
                        sems.at[side, k],
                    )
                )
        for copy in copies:
            copy.start()
        for copy in copies:
            copy.wait()

    return pl.pallas_call(
        body,
        out_shape=[pltpu.VMEM((count * 128, width), BF16)] * 2 + [MARK],
        in_specs=[SMEM] + [HBM] * 2,
        out_specs=[VMEM] * 3,
        scratch_shapes=[pltpu.SemaphoreType.DMA((2, count))],
        compiler_params=params(),
        cost_estimate=cost(2**24),
    )(table, w_in, w_out)


def group_rows(index):
    return pl.ds(pl.multiple_of(index * 512, 512), 512)


def after(array, *others):
    def body(*refs):
        del refs

    return pl.pallas_call(
        body,
        in_specs=[ANY] * (1 + len(others)),
        out_specs=ANY,
        out_shape=jax.ShapeDtypeStruct(array.shape, array.dtype),
        input_output_aliases={0: 0},
        compiler_params=params(),
        cost_estimate=cost(),
    )(array, *others)


MARK = jax.ShapeDtypeStruct((8, 128), F32)


def merge(table_ref, part_refs, all_ref):
    for k, ref in enumerate(part_refs):
        begin = pl.multiple_of(k // 4 * 512 + table_ref[48 + k % 4] * 128, 128)
        all_ref[pl.ds(begin, 128), :] = ref[...]


def forward(table, parts, weight):
    width = weight.shape[1]
    tok = 128 * len(parts)

    def body(table_ref, *refs):
        part_refs, weight_ref = refs[: len(parts)], refs[len(parts)]
        act_ref, slope_ref, all_ref, mark_ref = refs[len(parts) + 1 :]
        step = pl.program_id(0)

        @pl.when(step == 0)
        def _():
            mark_ref[...] = jnp.zeros_like(mark_ref)
            merge(table_ref, part_refs, all_ref)

        group = group_rows(step)
        for begin in range(0, tok, 256):
            cols = slice(begin, begin + 256)
            act, slope = gelu_parts(dot_nt(weight_ref[group, :], all_ref[cols, :]))
            act_ref[group, cols] = act.astype(BF16)
            slope_ref[group, cols] = slope.astype(BF16)

    return pl.pallas_call(
        body,
        grid=(4,),
        in_specs=[SMEM] + [VMEM] * (len(parts) + 1),
        out_specs=[VMEM] * 4,
        out_shape=[pltpu.VMEM((2048, tok), BF16)] * 2 + [shape(tok, width), MARK],
        compiler_params=params(),
        cost_estimate=cost(2**24),
    )(table, *parts, weight)


def outer_first(table, act, parts):
    width = parts[0].shape[1]
    tok = 128 * len(parts)

    def body(table_ref, act_ref, *refs):
        part_refs, (low_ref, high_ref, all_ref, mark_ref) = refs[: len(parts)], refs[len(parts) :]
        mark_ref[...] = jnp.zeros_like(mark_ref)
        merge(table_ref, part_refs, all_ref)
        low_ref[...] = dot_nn(act_ref[:256, :], all_ref[...]).astype(BF16)
        high_ref[...] = dot_nn(act_ref[256:512, :], all_ref[...]).astype(BF16)

    return pl.pallas_call(
        body,
        in_specs=[SMEM] + [VMEM] * (len(parts) + 1),
        out_specs=[VMEM] * 4,
        out_shape=[shape(256, width)] * 2 + [shape(tok, width), MARK],
        compiler_params=params(),
        cost_estimate=cost(2**22),
    )(table, act, *parts)


def outer_rest(act, rows, first, count, deps):
    width = rows.shape[1]

    def body(act_ref, rows_ref, *refs):
        step = pl.program_id(0)
        product = dot_nn(act_ref[group_rows(step + first), :], rows_ref[...])
        refs[len(deps)][group_rows(step), :] = product.astype(BF16)

    return pl.pallas_call(
        body,
        grid=(count,),
        in_specs=[VMEM] * 2 + [ANY] * len(deps),
        out_specs=VMEM,
        out_shape=shape(512 * count, width),
        compiler_params=params(),
        cost_estimate=cost(2**20 * (2 + 2 * count)),
    )(act, rows, *deps)


def backward(table, grads, rows, slope, weight, first, count, deps):
    tok, width = rows.shape
    split = first == 0

    def body(table_ref, grads_ref, rows_ref, slope_ref, weight_ref, *refs):
        pre_ref, *outs, mark_ref = refs[len(deps) :]
        mark_ref[...] = jnp.zeros_like(mark_ref)
        step = pl.program_id(0)
        group = group_rows(step + first)
        for begin in range(0, tok, 256):
            cols = slice(begin, begin + 256)
            act_grad = dot_nt(weight_ref[group, :], grads_ref[cols, :])
            for q in range(4):
                block = pl.multiple_of(table_ref[32 + 4 * (step + first) + q] * 128, 128)
                place = pl.multiple_of(step * 512 + q * 128, 128)
                part = act_grad[q * 128 : (q + 1) * 128] * slope_ref[pl.ds(block, 128), cols].astype(F32)
                pre_ref[pl.ds(place, 128), cols] = part.astype(BF16)
        if split:
            for k, out in enumerate(outs):
                out[...] = dot_nn(pre_ref[k * 256 : (k + 1) * 256, :], rows_ref[...]).astype(BF16)
        else:
            product = dot_nn(pre_ref[group_rows(step), :], rows_ref[...])
            outs[0][group_rows(step), :] = product.astype(BF16)

    return pl.pallas_call(
        body,
        grid=(count,),
        in_specs=[SMEM] + [VMEM] * 4 + [ANY] * len(deps),
        out_specs=[VMEM] * (4 if split else 3),
        out_shape=[shape(512 * count, tok)]
        + ([shape(256, width)] * 2 if split else [shape(512 * count, width)])
        + [MARK],
        compiler_params=params(),
        cost_estimate=cost(2**20 * (2 + 4 * count)),
    )(table, grads, rows, slope, weight, *deps)


def row_gradients(table, pre, weight):
    width = weight.shape[1]
    rows = 512

    def body(table_ref, a_ref, b_ref, c_ref, weight_ref, out_ref, w_ref, total):
        step = pl.program_id(0)
        for q in range(4):
            block = pl.multiple_of(table_ref[32 + 4 * step + q] * 128, 128)
            w_ref[q * 128 : (q + 1) * 128, :] = weight_ref[pl.ds(block, 128), :]

        @pl.when(step == 0)
        def _():
            total[...] = dot_tn(a_ref[...], w_ref[...])

        @pl.when(jnp.logical_and(step > 0, step < 3))
        def _():
            total[...] += dot_tn(b_ref[group_rows(step - 1), :], w_ref[...])

        @pl.when(step == 3)
        def _():
            final = (total[...] + dot_tn(c_ref[...], w_ref[...])).astype(BF16)
            own = table_ref[52]
            out_ref[group_rows(own), :] = final[:rows]
            out_ref[group_rows(1 - own), :] = final[rows:]

    return pl.pallas_call(
        body,
        grid=(4,),
        in_specs=[SMEM] + [VMEM] * 4,
        out_specs=VMEM,
        out_shape=shape(2 * rows, width),
        scratch_shapes=[pltpu.VMEM((512, width), BF16), pltpu.VMEM((2 * rows, width), F32)],
        compiler_params=params(),
        cost_estimate=cost(2**23 + 2**22),
    )(table, *pre, weight)


def join(*sums):
    n, width = sums[0][0].shape
    h = n // 4

    def body(*refs):
        ins, outs = refs[: 3 * len(sums)], refs[3 * len(sums) :]
        outs[-1][...] = jnp.zeros_like(outs[-1])
        for k in range(len(sums)):
            sides_ref, from_next, from_prev = ins[3 * k : 3 * k + 3]
            up_ref, down_ref = outs[2 * k : 2 * k + 2]
            up_ref[:h, :] = sides_ref[:h, :]
            up_ref[h:, :] = add(sides_ref[h : 2 * h, :], from_prev[...]).astype(BF16)
            down_ref[:h, :] = add(sides_ref[2 * h : 3 * h, :], from_next[...]).astype(BF16)
            down_ref[h:, :] = sides_ref[3 * h :, :]

    return pl.pallas_call(
        body,
        out_shape=[shape(2 * h, width)] * (2 * len(sums)) + [MARK],
        in_specs=[VMEM] * (3 * len(sums)),
        out_specs=[VMEM] * (2 * len(sums) + 1),
        compiler_params=params(),
        cost_estimate=cost(4 * n * width),
    )(*[array for sides, arrived in sums for array in (sides, *arrived)])


def restore_order(place, rows):
    n, width = place.shape[1], rows.shape[1]

    def body(place_ref, rows_ref, out_ref):
        out_ref[...] = dot_tn(place_ref[...], rows_ref[...]).astype(BF16)

    return pl.pallas_call(
        body,
        out_shape=shape(n, width),
        in_specs=[VMEM] * 2,
        out_specs=VMEM,
        compiler_params=params(),
        cost_estimate=cost(2**21),
    )(place, rows)


def add(*terms):
    total = terms[0].astype(F32)
    for term in terms[1:]:
        total = total + term.astype(F32)
    return total


def first_hop(low, high, axis):
    return lax.ppermute(low, axis, ring(3)), lax.ppermute(high, axis, ring(1))


def second_hop(up, down, axis):
    return lax.ppermute(up, axis, ring(1)), lax.ppermute(down, axis, ring(3))


def cut(total, refs):
    keep_ref, sides_ref, low_ref, high_ref, mark_ref = refs
    n = total.shape[0]
    q = n // 4
    mark_ref[...] = jnp.zeros_like(mark_ref)
    total = total.astype(BF16)
    keep_ref[...] = total[:q]
    sides_ref[:q, :] = total[q : 2 * q]
    low_ref[...] = total[2 * q : 2 * q + q // 2]
    high_ref[...] = total[2 * q + q // 2 : 3 * q]
    sides_ref[q:, :] = total[3 * q :]


def cut_shapes(n, width):
    return [shape(n // k, width) for k in (4, 2, 8, 8)] + [MARK]


def combine(own, received):
    n, width = own.shape

    def body(own_ref, left, right, *refs):
        cut(add(own_ref[...], left[...], right[...]), refs)

    return pl.pallas_call(
        body,
        out_shape=cut_shapes(n, width),
        in_specs=[VMEM] * 3,
        out_specs=[VMEM] * 5,
        compiler_params=params(),
        cost_estimate=cost(8 * n * width),
    )(own, *received)


def combine_product(act, rows, group, received):
    tok, width = rows.shape

    def body(act_ref, rows_ref, left, right, *refs):
        act_part = act_ref[group * 512 : (group + 1) * 512, :]
        cut(dot_nn(act_part, rows_ref[...]) + add(left[...], right[...]), refs)

    return pl.pallas_call(
        body,
        in_specs=[VMEM] * 4,
        out_specs=[VMEM] * 5,
        out_shape=cut_shapes(512, width),
        compiler_params=params(),
        cost_estimate=cost(10 * 512 * width),
    )(act, rows, *received)


def in_hbm(array):
    return pltpu.with_memory_space_constraint(array, pltpu.HBM)


def sum_cores(terms):
    terms = lax.all_to_all(terms, "core", split_axis=0, concat_axis=0, tiled=True)
    n = terms.shape[0] // 2
    return add(terms[:n], terms[n:]).astype(BF16)


def local(tokens, out_grad, gate, region, w_in, w_out):
    expert = lax.axis_index("expert").astype(jnp.int32)
    x, y, core = (lax.axis_index(a).astype(jnp.int32) for a in ("x", "y", "core"))
    scale = 1.0 / math.sqrt(float(tokens.shape[0] * lax.axis_size(("y", "x", "core"))))
    order = jnp.array(ORDER, jnp.int32)
    every = jnp.arange(4, dtype=jnp.int32)
    by_x = ((((y + every[None, :]) % 4) * 4 + (x + order[:, None]) % 4) * 2 + core).reshape(16)
    by_y = ((((y + order[:, None]) % 4) * 4 + (x + every[None, :]) % 4) * 2 + core).reshape(16)
    same = jnp.array([INVERSE[q] * 4 + ORDER[p] for p in range(4) for q in range(4)], jnp.int32)
    table = jnp.concatenate([by_x, by_y, same, (expert - every) % 4, core[None]])
    weight_in, weight_out, mark = fetch_weights(table, in_hbm(w_in[0]), in_hbm(w_out[0]))

    place, *send_x = dispatch_tokens(
        expert[None], in_hbm(region.reshape(1, -1)), in_hbm(tokens)
    )
    send_d = dispatch_grads(expert[None], place, gate.reshape(1, -1), out_grad, ())

    def to_owner(parts):
        return [parts[0]] + [lax.ppermute(parts[r], "expert", ring(r)) for r in (1, 2, 3)]

    own_x = to_owner(send_x)
    own_d = to_owner(send_d)
    own_x[0] = after(own_x[0], mark, send_d[0])
    own_x[2] = after(own_x[2], own_d[1])
    both_x = own_x + [swap_core(p) for p in own_x]
    act, slope, rows_x, mark = forward(table, both_x, weight_in)
    own_d = [after(part, mark) for part in own_d]
    both_d = own_d + [swap_core(p) for p in own_d]

    out_low, out_high, rows_d, mark = outer_first(table, act, both_d)
    hop = first_hop(out_low, out_high, "x")
    pre_a, in_low, in_high, mark = backward(
        table, rows_d, rows_x, slope, weight_out, 0, 1, (mark,)
    )
    out_sides = outer_rest(act, rows_d, 1, 2, (mark,))
    *pair, mark = join((out_sides, hop))
    out_parts = second_hop(*pair, "x")
    hop = first_hop(in_low, in_high, "y")
    pre_b, in_sides, mark = backward(table, rows_d, rows_x, slope, weight_out, 1, 2, (mark,))
    *pair, mark = join((in_sides, hop))
    in_parts = second_hop(*pair, "y")
    pre_c, in_own, mark = backward(table, rows_d, rows_x, slope, weight_out, 3, 1, (mark,))
    own = sum_cores(row_gradients(table, (pre_a, pre_b, pre_c), weight_in))
    back = lax.all_to_all(own, "expert", split_axis=0, concat_axis=0, tiled=True)

    out_keep, out_sides, low, high, mark = combine_product(act, rows_d, 3, out_parts)
    out_hop = first_hop(low, high, "y")
    in_keep, in_sides, low, high, mark = combine(after(in_own, mark), in_parts)
    in_hop = first_hop(low, high, "x")
    *pairs, _ = join((out_sides, out_hop), (in_sides, in_hop))
    out_parts = second_hop(*pairs[:2], "y")
    in_parts = second_hop(*pairs[2:], "x")
    grad_out = add(out_keep, *out_parts) * scale
    grad_in = add(in_keep, *in_parts) * scale
    token_grad = restore_order(place, back)
    return token_grad, grad_in[None], grad_out[None]


def solution(mesh):
    chips = Mesh(mesh.devices.reshape(4, 4, 2, 4), ("y", "x", "core", "expert"))
    rows = ("y", "x", "core", "expert")
    plane = ("y", "x", "core")
    return jax.shard_map(
        local,
        mesh=chips,
        in_specs=(
            P(rows, None),
            P(rows, None),
            P(rows),
            P(rows, None),
            P("expert", None, None),
            P("expert", None, None),
        ),
        out_specs=(P(rows, None), P("expert", plane, None), P("expert", plane, None)),
        check_vma=False,
    )
```

```python
import math

import jax
import jax.numpy as jnp
from jax import lax
from jax.experimental import pallas as pl
from jax.experimental.pallas import tpu as pltpu
from jax.sharding import Mesh, PartitionSpec as P

BF16 = jnp.bfloat16
F32 = jnp.float32
VMEM_LIMIT = 18 * 1024 * 1024
ORDER = (2, 1, 3, 0)
INVERSE = (3, 1, 0, 2)


def ring(step):
    return [(i, (i + step) % 4) for i in range(4)]


def swap_core(array):
    return lax.ppermute(array, "core", [(0, 1), (1, 0)])


def params():
    return pltpu.CompilerParams(vmem_limit_bytes=VMEM_LIMIT)


def cost(nbytes=1024):
    return pl.CostEstimate(flops=0, bytes_accessed=int(nbytes), transcendentals=0)


def shape(rows, cols, dtype=BF16):
    return jax.ShapeDtypeStruct((rows, cols), dtype)


def dot_nt(a, b):
    return lax.dot_general(a, b, (((1,), (1,)), ((), ())), preferred_element_type=F32)


def dot_nn(a, b):
    return lax.dot_general(a, b, (((1,), (0,)), ((), ())), preferred_element_type=F32)


def dot_tn(a, b):
    return lax.dot_general(a, b, (((0,), (0,)), ((), ())), preferred_element_type=F32)


def gelu_parts(pre_act):
    root_two_pi = 0.7978845608028654
    square = pre_act * pre_act
    inner = pre_act * (root_two_pi + root_two_pi * 0.044715 * square)
    halved = 0.5 + 0.5 * jnp.tanh(inner)
    value = pre_act * halved
    slope_of_inner = 2.0 * root_two_pi + 6.0 * root_two_pi * 0.044715 * square
    return value, halved + value * (1.0 - halved) * slope_of_inner


VMEM = pl.BlockSpec(memory_space=pltpu.VMEM)
SMEM = pl.BlockSpec(memory_space=pltpu.SMEM)
ANY = pl.BlockSpec(memory_space=pl.ANY)


def bucket(where_ref, r):
    return pl.ds(pl.multiple_of(jnp.bitwise_and(where_ref[0] + r, 3) * 128, 128), 128)


def dispatch_tokens(where, region, tokens):
    n, width = tokens.shape

    def body(where_ref, region_hbm, tok_hbm, place_ref, *refs):
        outs, (region_ref, tok_ref, sems) = refs[:4], refs[4:]
        copies = [
            pltpu.make_async_copy(region_hbm, region_ref, sems.at[0]),
            pltpu.make_async_copy(tok_hbm, tok_ref, sems.at[1]),
        ]
        for copy in copies:
            copy.start()
        upper = (
            lax.broadcasted_iota(jnp.int32, (n, n), 0) < lax.broadcasted_iota(jnp.int32, (n, n), 1)
        ).astype(F32)
        copies[0].wait()
        dest = region_ref[...]
        onehot = (dest == lax.broadcasted_iota(jnp.int32, (8, n), 0)).astype(F32)
        before = dot_nn(onehot.astype(BF16), upper.astype(BF16))
        rank = jnp.sum(before * onehot, axis=0, keepdims=True).astype(jnp.int32)
        slot = dest * 128 + rank
        place = (slot == lax.broadcasted_iota(jnp.int32, (512, n), 0)).astype(F32).astype(BF16)
        place_ref[...] = place
        copies[1].wait()
        for r, out in enumerate(outs):
            out[...] = dot_nn(place_ref[bucket(where_ref, r), :], tok_ref[...]).astype(BF16)

    return pl.pallas_call(
        body,
        out_shape=[shape(512, n)] + [shape(128, width)] * 4,
        in_specs=[SMEM] + [HBM] * 2,
        out_specs=[VMEM] * 5,
        scratch_shapes=[
            pltpu.VMEM((1, n), jnp.int32),
            pltpu.VMEM((n, width), BF16),
            pltpu.SemaphoreType.DMA((2,)),
        ],
        compiler_params=params(),
        cost_estimate=cost(4 * n * width * 2),
    )(where, region, tokens)


def dispatch_grads(where, place, gate, grads, deps):
    n, width = grads.shape

    def body(where_ref, place_ref, gate_ref, grad_ref, *refs):
        outs = refs[len(deps) :]
        column = jnp.transpose(jnp.broadcast_to(gate_ref[...], (128, n)))[:, :1]
        scaled = (column * grad_ref[...].astype(F32)).astype(BF16)
        for r, out in enumerate(outs):
            out[...] = dot_nn(place_ref[bucket(where_ref, r), :], scaled).astype(BF16)

    return pl.pallas_call(
        body,
        out_shape=[shape(128, width)] * 4,
        in_specs=[SMEM] + [VMEM] * 3 + [ANY] * len(deps),
        out_specs=[VMEM] * 4,
        compiler_params=params(),
        cost_estimate=cost(4 * n * width * 2),
    )(where, place, gate, grads, *deps)


HBM = pl.BlockSpec(memory_space=pltpu.HBM)


def fetch_weights(table, w_in, w_out):
    count, width = 16, w_in.shape[1]

    def body(table_ref, in_hbm_ref, out_hbm_ref, in_ref, out_ref, mark_ref, sems):
        mark_ref[...] = jnp.zeros_like(mark_ref)
        copies = []
        for k in range(count):
            for side, (source, target) in enumerate(((in_hbm_ref, in_ref), (out_hbm_ref, out_ref))):
                block = pl.multiple_of(table_ref[count * side + k] * 128, 128)
                copies.append(
                    pltpu.make_async_copy(
                        source.at[pl.ds(block, 128), :],
                        target.at[pl.ds(k * 128, 128), :],
                        sems.at[side, k],
                    )
                )
        for copy in copies:
            copy.start()
        for copy in copies:
            copy.wait()

    return pl.pallas_call(
        body,
        out_shape=[pltpu.VMEM((count * 128, width), BF16)] * 2 + [MARK],
        in_specs=[SMEM] + [HBM] * 2,
        out_specs=[VMEM] * 3,
        scratch_shapes=[pltpu.SemaphoreType.DMA((2, count))],
        compiler_params=params(),
        cost_estimate=cost(2**24),
    )(table, w_in, w_out)


def group_rows(index):
    return pl.ds(pl.multiple_of(index * 512, 512), 512)


def after(array, *others):
    def body(*refs):
        del refs

    return pl.pallas_call(
        body,
        in_specs=[ANY] * (1 + len(others)),
        out_specs=ANY,
        out_shape=jax.ShapeDtypeStruct(array.shape, array.dtype),
        input_output_aliases={0: 0},
        compiler_params=params(),
        cost_estimate=cost(),
    )(array, *others)


MARK = jax.ShapeDtypeStruct((8, 128), F32)


def merge(table_ref, part_refs, all_ref):
    for k, ref in enumerate(part_refs):
        begin = pl.multiple_of(k // 4 * 512 + table_ref[48 + k % 4] * 128, 128)
        all_ref[pl.ds(begin, 128), :] = ref[...]


def forward(table, parts, weight):
    width = weight.shape[1]
    tok = 128 * len(parts)

    def body(table_ref, *refs):
        part_refs, weight_ref = refs[: len(parts)], refs[len(parts)]
        act_ref, slope_ref, all_ref, mark_ref = refs[len(parts) + 1 :]
        step = pl.program_id(0)

        @pl.when(step == 0)
        def _():
            mark_ref[...] = jnp.zeros_like(mark_ref)
            merge(table_ref, part_refs, all_ref)

        group = group_rows(step)
        for begin in range(0, tok, 256):
            cols = slice(begin, begin + 256)
            act, slope = gelu_parts(dot_nt(weight_ref[group, :], all_ref[cols, :]))
            act_ref[group, cols] = act.astype(BF16)
            slope_ref[group, cols] = slope.astype(BF16)

    return pl.pallas_call(
        body,
        grid=(4,),
        in_specs=[SMEM] + [VMEM] * (len(parts) + 1),
        out_specs=[VMEM] * 4,
        out_shape=[pltpu.VMEM((2048, tok), BF16)] * 2 + [shape(tok, width), MARK],
        compiler_params=params(),
        cost_estimate=cost(2**24),
    )(table, *parts, weight)


def outer_first(table, act, parts):
    width = parts[0].shape[1]
    tok = 128 * len(parts)

    def body(table_ref, act_ref, *refs):
        part_refs, (low_ref, high_ref, all_ref, mark_ref) = refs[: len(parts)], refs[len(parts) :]
        mark_ref[...] = jnp.zeros_like(mark_ref)
        merge(table_ref, part_refs, all_ref)
        low_ref[...] = dot_nn(act_ref[:256, :], all_ref[...]).astype(BF16)
        high_ref[...] = dot_nn(act_ref[256:512, :], all_ref[...]).astype(BF16)

    return pl.pallas_call(
        body,
        in_specs=[SMEM] + [VMEM] * (len(parts) + 1),
        out_specs=[VMEM] * 4,
        out_shape=[shape(256, width)] * 2 + [shape(tok, width), MARK],
        compiler_params=params(),
        cost_estimate=cost(2**22),
    )(table, act, *parts)


def outer_rest(act, rows, deps):
    width = rows.shape[1]

    def body(act_ref, rows_ref, *refs):
        sides_ref, own_ref, mark_ref = refs[len(deps) :]
        mark_ref[...] = jnp.zeros_like(mark_ref)
        for k, out in enumerate((sides_ref.at[:512], sides_ref.at[512:], own_ref)):
            group = act_ref[(k + 1) * 512 : (k + 2) * 512, :]
            out[...] = dot_nn(group, rows_ref[...]).astype(BF16)

    return pl.pallas_call(
        body,
        in_specs=[VMEM] * 2 + [ANY] * len(deps),
        out_specs=[VMEM] * 3,
        out_shape=[shape(1024, width), shape(512, width), MARK],
        compiler_params=params(),
        cost_estimate=cost(2**23),
    )(act, rows, *deps)


def backward(table, grads, rows, slope, weight, first, count, deps):
    tok, width = rows.shape
    split = first == 0

    def body(table_ref, grads_ref, rows_ref, slope_ref, weight_ref, *refs):
        pre_ref, *outs, mark_ref = refs[len(deps) :]
        mark_ref[...] = jnp.zeros_like(mark_ref)
        step = pl.program_id(0)
        group = group_rows(step + first)
        for begin in range(0, tok, 256):
            cols = slice(begin, begin + 256)
            act_grad = dot_nt(weight_ref[group, :], grads_ref[cols, :])
            for q in range(4):
                block = pl.multiple_of(table_ref[32 + 4 * (step + first) + q] * 128, 128)
                place = pl.multiple_of(step * 512 + q * 128, 128)
                part = act_grad[q * 128 : (q + 1) * 128] * slope_ref[pl.ds(block, 128), cols].astype(F32)
                pre_ref[pl.ds(place, 128), cols] = part.astype(BF16)
        if split:
            for k, out in enumerate(outs):
                out[...] = dot_nn(pre_ref[k * 256 : (k + 1) * 256, :], rows_ref[...]).astype(BF16)
        else:
            product = dot_nn(pre_ref[group_rows(step), :], rows_ref[...])
            outs[0][group_rows(step), :] = product.astype(BF16)

    return pl.pallas_call(
        body,
        grid=(count,),
        in_specs=[SMEM] + [VMEM] * 4 + [ANY] * len(deps),
        out_specs=[VMEM] * (4 if split else 3),
        out_shape=[shape(512 * count, tok)]
        + ([shape(256, width)] * 2 if split else [shape(512 * count, width)])
        + [MARK],
        compiler_params=params(),
        cost_estimate=cost(2**20 * (2 + 4 * count)),
    )(table, grads, rows, slope, weight, *deps)


def row_gradients(table, pre, weight):
    width = weight.shape[1]
    rows = 512

    def body(table_ref, a_ref, b_ref, c_ref, weight_ref, out_ref, w_ref, total):
        step = pl.program_id(0)
        for q in range(4):
            block = pl.multiple_of(table_ref[32 + 4 * step + q] * 128, 128)
            w_ref[q * 128 : (q + 1) * 128, :] = weight_ref[pl.ds(block, 128), :]

        @pl.when(step == 0)
        def _():
            total[...] = dot_tn(a_ref[...], w_ref[...])

        @pl.when(jnp.logical_and(step > 0, step < 3))
        def _():
            total[...] += dot_tn(b_ref[group_rows(step - 1), :], w_ref[...])

        @pl.when(step == 3)
        def _():
            final = (total[...] + dot_tn(c_ref[...], w_ref[...])).astype(BF16)
            own = table_ref[52]
            out_ref[group_rows(own), :] = final[:rows]
            out_ref[group_rows(1 - own), :] = final[rows:]

    return pl.pallas_call(
        body,
        grid=(4,),
        in_specs=[SMEM] + [VMEM] * 4,
        out_specs=VMEM,
        out_shape=shape(2 * rows, width),
        scratch_shapes=[pltpu.VMEM((512, width), BF16), pltpu.VMEM((2 * rows, width), F32)],
        compiler_params=params(),
        cost_estimate=cost(2**23 + 2**22),
    )(table, *pre, weight)


def join(*sums):
    n, width = sums[0][0].shape
    h = n // 4

    def body(*refs):
        ins, outs = refs[: 3 * len(sums)], refs[3 * len(sums) :]
        outs[-1][...] = jnp.zeros_like(outs[-1])
        for k in range(len(sums)):
            sides_ref, from_next, from_prev = ins[3 * k : 3 * k + 3]
            up_ref, down_ref = outs[2 * k : 2 * k + 2]
            up_ref[:h, :] = sides_ref[:h, :]
            up_ref[h:, :] = add(sides_ref[h : 2 * h, :], from_prev[...]).astype(BF16)
            down_ref[:h, :] = add(sides_ref[2 * h : 3 * h, :], from_next[...]).astype(BF16)
            down_ref[h:, :] = sides_ref[3 * h :, :]

    return pl.pallas_call(
        body,
        out_shape=[shape(2 * h, width)] * (2 * len(sums)) + [MARK],
        in_specs=[VMEM] * (3 * len(sums)),
        out_specs=[VMEM] * (2 * len(sums) + 1),
        compiler_params=params(),
        cost_estimate=cost(4 * n * width),
    )(*[array for sides, arrived in sums for array in (sides, *arrived)])


def restore_order(place, rows):
    n, width = place.shape[1], rows.shape[1]

    def body(place_ref, rows_ref, out_ref):
        out_ref[...] = dot_tn(place_ref[...], rows_ref[...]).astype(BF16)

    return pl.pallas_call(
        body,
        out_shape=shape(n, width),
        in_specs=[VMEM] * 2,
        out_specs=VMEM,
        compiler_params=params(),
        cost_estimate=cost(2**21),
    )(place, rows)


def add(*terms):
    total = terms[0].astype(F32)
    for term in terms[1:]:
        total = total + term.astype(F32)
    return total


def first_hop(low, high, axis):
    return lax.ppermute(low, axis, ring(3)), lax.ppermute(high, axis, ring(1))


def second_hop(up, down, axis):
    return lax.ppermute(up, axis, ring(1)), lax.ppermute(down, axis, ring(3))


def cut(total, refs):
    keep_ref, sides_ref, low_ref, high_ref, mark_ref = refs
    n = total.shape[0]
    q = n // 4
    mark_ref[...] = jnp.zeros_like(mark_ref)
    total = total.astype(BF16)
    keep_ref[...] = total[:q]
    sides_ref[:q, :] = total[q : 2 * q]
    low_ref[...] = total[2 * q : 2 * q + q // 2]
    high_ref[...] = total[2 * q + q // 2 : 3 * q]
    sides_ref[q:, :] = total[3 * q :]


def cut_shapes(n, width):
    return [shape(n // k, width) for k in (4, 2, 8, 8)] + [MARK]


def combine(own, received):
    n, width = own.shape

    def body(own_ref, left, right, *refs):
        cut(add(own_ref[...], left[...], right[...]), refs)

    return pl.pallas_call(
        body,
        out_shape=cut_shapes(n, width),
        in_specs=[VMEM] * 3,
        out_specs=[VMEM] * 5,
        compiler_params=params(),
        cost_estimate=cost(8 * n * width),
    )(own, *received)


def in_hbm(array):
    return pltpu.with_memory_space_constraint(array, pltpu.HBM)


def sum_cores(terms):
    terms = lax.all_to_all(terms, "core", split_axis=0, concat_axis=0, tiled=True)
    n = terms.shape[0] // 2
    return add(terms[:n], terms[n:]).astype(BF16)


def local(tokens, out_grad, gate, region, w_in, w_out):
    expert = lax.axis_index("expert").astype(jnp.int32)
    x, y, core = (lax.axis_index(a).astype(jnp.int32) for a in ("x", "y", "core"))
    scale = 1.0 / math.sqrt(float(tokens.shape[0] * lax.axis_size(("y", "x", "core"))))
    order = jnp.array(ORDER, jnp.int32)
    every = jnp.arange(4, dtype=jnp.int32)
    by_x = ((((y + every[None, :]) % 4) * 4 + (x + order[:, None]) % 4) * 2 + core).reshape(16)
    by_y = ((((y + order[:, None]) % 4) * 4 + (x + every[None, :]) % 4) * 2 + core).reshape(16)
    same = jnp.array([INVERSE[q] * 4 + ORDER[p] for p in range(4) for q in range(4)], jnp.int32)
    table = jnp.concatenate([by_x, by_y, same, (expert - every) % 4, core[None]])
    weight_in, weight_out, mark = fetch_weights(table, in_hbm(w_in[0]), in_hbm(w_out[0]))

    place, *send_x = dispatch_tokens(
        expert[None], in_hbm(region.reshape(1, -1)), in_hbm(tokens)
    )
    send_d = dispatch_grads(expert[None], place, gate.reshape(1, -1), out_grad, ())

    def to_owner(parts):
        return [parts[0]] + [lax.ppermute(parts[r], "expert", ring(r)) for r in (1, 2, 3)]

    own_x = to_owner(send_x)
    own_d = to_owner(send_d)
    own_x[0] = after(own_x[0], mark, send_d[0])
    own_x[2] = after(own_x[2], own_d[1])
    both_x = own_x + [swap_core(p) for p in own_x]
    act, slope, rows_x, mark = forward(table, both_x, weight_in)
    own_d = [after(part, mark) for part in own_d]
    both_d = own_d + [swap_core(p) for p in own_d]

    out_low, out_high, rows_d, mark = outer_first(table, act, both_d)
    hop = first_hop(out_low, out_high, "x")
    pre_a, in_low, in_high, mark = backward(
        table, rows_d, rows_x, slope, weight_out, 0, 1, (mark,)
    )
    out_sides, out_own, mark = outer_rest(act, rows_d, (mark,))
    in_hop = first_hop(in_low, in_high, "y")
    pre_b, in_sides, mark = backward(table, rows_d, rows_x, slope, weight_out, 1, 2, (mark,))
    *pair, mark = join((after(out_sides, mark), hop))
    out_parts = second_hop(*pair, "x")
    *pair, mark = join((after(in_sides, mark), in_hop))
    in_parts = second_hop(*pair, "y")
    pre_c, in_own, mark = backward(table, rows_d, rows_x, slope, weight_out, 3, 1, (mark,))
    own = sum_cores(row_gradients(table, (pre_a, pre_b, pre_c), weight_in))
    back = lax.all_to_all(own, "expert", split_axis=0, concat_axis=0, tiled=True)

    out_keep, out_sides, low, high, mark = combine(out_own, out_parts)
    out_hop = first_hop(low, high, "y")
    in_keep, in_sides, low, high, mark = combine(after(in_own, mark), in_parts)
    in_hop = first_hop(low, high, "x")
    *pairs, _ = join((out_sides, out_hop), (in_sides, in_hop))
    out_parts = second_hop(*pairs[:2], "y")
    in_parts = second_hop(*pairs[2:], "x")
    grad_out = add(out_keep, *out_parts) * scale
    grad_in = add(in_keep, *in_parts) * scale
    token_grad = restore_order(place, back)
    return token_grad, grad_in[None], grad_out[None]


def solution(mesh):
    chips = Mesh(mesh.devices.reshape(4, 4, 2, 4), ("y", "x", "core", "expert"))
    rows = ("y", "x", "core", "expert")
    plane = ("y", "x", "core")
    return jax.shard_map(
        local,
        mesh=chips,
        in_specs=(
            P(rows, None),
            P(rows, None),
            P(rows),
            P(rows, None),
            P("expert", None, None),
            P("expert", None, None),
        ),
        out_specs=(P(rows, None), P("expert", plane, None), P("expert", plane, None)),
        check_vma=False,
    )
```

```python
import math

import jax
import jax.numpy as jnp
from jax import lax
from jax.experimental import pallas as pl
from jax.experimental.pallas import tpu as pltpu
from jax.sharding import Mesh, PartitionSpec as P

BF16 = jnp.bfloat16
F32 = jnp.float32
VMEM_LIMIT = 18 * 1024 * 1024
ORDER = (2, 1, 3, 0)
INVERSE = (3, 1, 0, 2)


def ring(step):
    return [(i, (i + step) % 4) for i in range(4)]


def swap_core(array):
    return lax.ppermute(array, "core", [(0, 1), (1, 0)])


def params():
    return pltpu.CompilerParams(vmem_limit_bytes=VMEM_LIMIT)


def cost(nbytes=1024):
    return pl.CostEstimate(flops=0, bytes_accessed=int(nbytes), transcendentals=0)


def shape(rows, cols, dtype=BF16):
    return jax.ShapeDtypeStruct((rows, cols), dtype)


def dot_nt(a, b):
    return lax.dot_general(a, b, (((1,), (1,)), ((), ())), preferred_element_type=F32)


def dot_nn(a, b):
    return lax.dot_general(a, b, (((1,), (0,)), ((), ())), preferred_element_type=F32)


def dot_tn(a, b):
    return lax.dot_general(a, b, (((0,), (0,)), ((), ())), preferred_element_type=F32)


def gelu_parts(pre_act):
    root_two_pi = 0.7978845608028654
    square = pre_act * pre_act
    inner = pre_act * (root_two_pi + root_two_pi * 0.044715 * square)
    halved = 0.5 + 0.5 * jnp.tanh(inner)
    value = pre_act * halved
    slope_of_inner = 2.0 * root_two_pi + 6.0 * root_two_pi * 0.044715 * square
    return value, halved + value * (1.0 - halved) * slope_of_inner


VMEM = pl.BlockSpec(memory_space=pltpu.VMEM)
SMEM = pl.BlockSpec(memory_space=pltpu.SMEM)
ANY = pl.BlockSpec(memory_space=pl.ANY)


def bucket(where_ref, r):
    return pl.ds(pl.multiple_of(jnp.bitwise_and(where_ref[0] + r, 3) * 128, 128), 128)


def dispatch_tokens(where, region, tokens):
    n, width = tokens.shape

    def body(where_ref, region_hbm, tok_hbm, place_ref, *refs):
        outs, (region_ref, tok_ref, sems) = refs[:4], refs[4:]
        copies = [
            pltpu.make_async_copy(region_hbm, region_ref, sems.at[0]),
            pltpu.make_async_copy(tok_hbm, tok_ref, sems.at[1]),
        ]
        for copy in copies:
            copy.start()
        upper = (
            lax.broadcasted_iota(jnp.int32, (n, n), 0) < lax.broadcasted_iota(jnp.int32, (n, n), 1)
        ).astype(F32)
        copies[0].wait()
        dest = region_ref[...]
        onehot = (dest == lax.broadcasted_iota(jnp.int32, (8, n), 0)).astype(F32)
        before = dot_nn(onehot.astype(BF16), upper.astype(BF16))
        rank = jnp.sum(before * onehot, axis=0, keepdims=True).astype(jnp.int32)
        slot = dest * 128 + rank
        place = (slot == lax.broadcasted_iota(jnp.int32, (512, n), 0)).astype(F32).astype(BF16)
        place_ref[...] = place
        copies[1].wait()
        for r, out in enumerate(outs):
            out[...] = dot_nn(place_ref[bucket(where_ref, r), :], tok_ref[...]).astype(BF16)

    return pl.pallas_call(
        body,
        out_shape=[shape(512, n)] + [shape(128, width)] * 4,
        in_specs=[SMEM] + [HBM] * 2,
        out_specs=[VMEM] * 5,
        scratch_shapes=[
            pltpu.VMEM((1, n), jnp.int32),
            pltpu.VMEM((n, width), BF16),
            pltpu.SemaphoreType.DMA((2,)),
        ],
        compiler_params=params(),
        cost_estimate=cost(4 * n * width * 2),
    )(where, region, tokens)


def dispatch_grads(where, place, gate, grads, deps):
    n, width = grads.shape

    def body(where_ref, place_ref, gate_ref, grad_ref, *refs):
        outs = refs[len(deps) :]
        column = jnp.transpose(jnp.broadcast_to(gate_ref[...], (128, n)))[:, :1]
        scaled = (column * grad_ref[...].astype(F32)).astype(BF16)
        for r, out in enumerate(outs):
            out[...] = dot_nn(place_ref[bucket(where_ref, r), :], scaled).astype(BF16)

    return pl.pallas_call(
        body,
        out_shape=[shape(128, width)] * 4,
        in_specs=[SMEM] + [VMEM] * 3 + [ANY] * len(deps),
        out_specs=[VMEM] * 4,
        compiler_params=params(),
        cost_estimate=cost(4 * n * width * 2),
    )(where, place, gate, grads, *deps)


HBM = pl.BlockSpec(memory_space=pltpu.HBM)


def fetch_weights(table, w_in, w_out):
    count, width = 16, w_in.shape[1]

    def body(table_ref, in_hbm_ref, out_hbm_ref, in_ref, out_ref, mark_ref, sems):
        mark_ref[...] = jnp.zeros_like(mark_ref)
        copies = []
        for k in range(count):
            for side, (source, target) in enumerate(((in_hbm_ref, in_ref), (out_hbm_ref, out_ref))):
                block = pl.multiple_of(table_ref[count * side + k] * 128, 128)
                copies.append(
                    pltpu.make_async_copy(
                        source.at[pl.ds(block, 128), :],
                        target.at[pl.ds(k * 128, 128), :],
                        sems.at[side, k],
                    )
                )
        for copy in copies:
            copy.start()
        for copy in copies:
            copy.wait()

    return pl.pallas_call(
        body,
        out_shape=[pltpu.VMEM((count * 128, width), BF16)] * 2 + [MARK],
        in_specs=[SMEM] + [HBM] * 2,
        out_specs=[VMEM] * 3,
        scratch_shapes=[pltpu.SemaphoreType.DMA((2, count))],
        compiler_params=params(),
        cost_estimate=cost(2**24),
    )(table, w_in, w_out)


def group_rows(index):
    return pl.ds(pl.multiple_of(index * 512, 512), 512)


def after(array, *others):
    def body(*refs):
        del refs

    return pl.pallas_call(
        body,
        in_specs=[ANY] * (1 + len(others)),
        out_specs=ANY,
        out_shape=jax.ShapeDtypeStruct(array.shape, array.dtype),
        input_output_aliases={0: 0},
        compiler_params=params(),
        cost_estimate=cost(),
    )(array, *others)


MARK = jax.ShapeDtypeStruct((8, 128), F32)


def merge(table_ref, part_refs, all_ref):
    for k, ref in enumerate(part_refs):
        begin = pl.multiple_of(k // 4 * 512 + table_ref[48 + k % 4] * 128, 128)
        all_ref[pl.ds(begin, 128), :] = ref[...]


def forward(table, parts, weight):
    width = weight.shape[1]
    tok = 128 * len(parts)

    def body(table_ref, *refs):
        part_refs, weight_ref = refs[: len(parts)], refs[len(parts)]
        act_ref, slope_ref, all_ref, mark_ref = refs[len(parts) + 1 :]
        step = pl.program_id(0)

        @pl.when(step == 0)
        def _():
            mark_ref[...] = jnp.zeros_like(mark_ref)
            merge(table_ref, part_refs, all_ref)

        group = group_rows(step)
        for begin in range(0, tok, 256):
            cols = slice(begin, begin + 256)
            act, slope = gelu_parts(dot_nt(weight_ref[group, :], all_ref[cols, :]))
            act_ref[group, cols] = act.astype(BF16)
            slope_ref[group, cols] = slope.astype(BF16)

    return pl.pallas_call(
        body,
        grid=(4,),
        in_specs=[SMEM] + [VMEM] * (len(parts) + 1),
        out_specs=[VMEM] * 4,
        out_shape=[pltpu.VMEM((2048, tok), BF16)] * 2 + [shape(tok, width), MARK],
        compiler_params=params(),
        cost_estimate=cost(2**24),
    )(table, *parts, weight)


def outer_first(table, act, parts):
    width = parts[0].shape[1]
    tok = 128 * len(parts)

    def body(table_ref, act_ref, *refs):
        part_refs, (low_ref, high_ref, all_ref, mark_ref) = refs[: len(parts)], refs[len(parts) :]
        mark_ref[...] = jnp.zeros_like(mark_ref)
        merge(table_ref, part_refs, all_ref)
        low_ref[...] = dot_nn(act_ref[:256, :], all_ref[...]).astype(BF16)
        high_ref[...] = dot_nn(act_ref[256:512, :], all_ref[...]).astype(BF16)

    return pl.pallas_call(
        body,
        in_specs=[SMEM] + [VMEM] * (len(parts) + 1),
        out_specs=[VMEM] * 4,
        out_shape=[shape(256, width)] * 2 + [shape(tok, width), MARK],
        compiler_params=params(),
        cost_estimate=cost(2**22),
    )(table, act, *parts)


def outer_rest(act, rows, deps):
    width = rows.shape[1]

    def body(act_ref, rows_ref, *refs):
        sides_ref, own_ref, mark_ref = refs[len(deps) :]
        mark_ref[...] = jnp.zeros_like(mark_ref)
        for k, out in enumerate((sides_ref.at[:512], sides_ref.at[512:], own_ref)):
            group = act_ref[(k + 1) * 512 : (k + 2) * 512, :]
            out[...] = dot_nn(group, rows_ref[...]).astype(BF16)

    return pl.pallas_call(
        body,
        in_specs=[VMEM] * 2 + [ANY] * len(deps),
        out_specs=[VMEM] * 3,
        out_shape=[shape(1024, width), shape(512, width), MARK],
        compiler_params=params(),
        cost_estimate=cost(2**23),
    )(act, rows, *deps)


def backward(table, grads, rows, slope, weight, first, count, deps):
    tok, width = rows.shape
    split = first == 0

    def body(table_ref, grads_ref, rows_ref, slope_ref, weight_ref, *refs):
        pre_ref, *outs, mark_ref = refs[len(deps) :]
        mark_ref[...] = jnp.zeros_like(mark_ref)
        step = pl.program_id(0)
        group = group_rows(step + first)
        for begin in range(0, tok, 256):
            cols = slice(begin, begin + 256)
            act_grad = dot_nt(weight_ref[group, :], grads_ref[cols, :])
            for q in range(4):
                block = pl.multiple_of(table_ref[32 + 4 * (step + first) + q] * 128, 128)
                place = pl.multiple_of(step * 512 + q * 128, 128)
                part = act_grad[q * 128 : (q + 1) * 128] * slope_ref[pl.ds(block, 128), cols].astype(F32)
                pre_ref[pl.ds(place, 128), cols] = part.astype(BF16)
        if split:
            for k, out in enumerate(outs):
                out[...] = dot_nn(pre_ref[k * 256 : (k + 1) * 256, :], rows_ref[...]).astype(BF16)
        else:
            product = dot_nn(pre_ref[group_rows(step), :], rows_ref[...])
            outs[0][group_rows(step), :] = product.astype(BF16)

    return pl.pallas_call(
        body,
        grid=(count,),
        in_specs=[SMEM] + [VMEM] * 4 + [ANY] * len(deps),
        out_specs=[VMEM] * (4 if split else 3),
        out_shape=[shape(512 * count, tok)]
        + ([shape(256, width)] * 2 if split else [shape(512 * count, width)])
        + [MARK],
        compiler_params=params(),
        cost_estimate=cost(2**20 * (2 + 4 * count)),
    )(table, grads, rows, slope, weight, *deps)


def row_gradients(table, pre, weight):
    width = weight.shape[1]
    rows = 512

    def body(table_ref, a_ref, b_ref, c_ref, weight_ref, out_ref, w_ref, total):
        step = pl.program_id(0)
        for q in range(4):
            block = pl.multiple_of(table_ref[32 + 4 * step + q] * 128, 128)
            w_ref[q * 128 : (q + 1) * 128, :] = weight_ref[pl.ds(block, 128), :]

        @pl.when(step == 0)
        def _():
            total[...] = dot_tn(a_ref[...], w_ref[...])

        @pl.when(jnp.logical_and(step > 0, step < 3))
        def _():
            total[...] += dot_tn(b_ref[group_rows(step - 1), :], w_ref[...])

        @pl.when(step == 3)
        def _():
            final = (total[...] + dot_tn(c_ref[...], w_ref[...])).astype(BF16)
            own = table_ref[52]
            out_ref[group_rows(own), :] = final[:rows]
            out_ref[group_rows(1 - own), :] = final[rows:]

    return pl.pallas_call(
        body,
        grid=(4,),
        in_specs=[SMEM] + [VMEM] * 4,
        out_specs=VMEM,
        out_shape=shape(2 * rows, width),
        scratch_shapes=[pltpu.VMEM((512, width), BF16), pltpu.VMEM((2 * rows, width), F32)],
        compiler_params=params(),
        cost_estimate=cost(2**23 + 2**22),
    )(table, *pre, weight)


def join(*sums):
    n, width = sums[0][0].shape
    h = n // 4

    def body(*refs):
        ins, outs = refs[: 3 * len(sums)], refs[3 * len(sums) :]
        outs[-1][...] = jnp.zeros_like(outs[-1])
        for k in range(len(sums)):
            sides_ref, from_next, from_prev = ins[3 * k : 3 * k + 3]
            up_ref, down_ref = outs[2 * k : 2 * k + 2]
            up_ref[:h, :] = sides_ref[:h, :]
            up_ref[h:, :] = add(sides_ref[h : 2 * h, :], from_prev[...]).astype(BF16)
            down_ref[:h, :] = add(sides_ref[2 * h : 3 * h, :], from_next[...]).astype(BF16)
            down_ref[h:, :] = sides_ref[3 * h :, :]

    return pl.pallas_call(
        body,
        out_shape=[shape(2 * h, width)] * (2 * len(sums)) + [MARK],
        in_specs=[VMEM] * (3 * len(sums)),
        out_specs=[VMEM] * (2 * len(sums) + 1),
        compiler_params=params(),
        cost_estimate=cost(4 * n * width),
    )(*[array for sides, arrived in sums for array in (sides, *arrived)])


def restore_order(place, rows):
    n, width = place.shape[1], rows.shape[1]

    def body(place_ref, rows_ref, out_ref):
        out_ref[...] = dot_tn(place_ref[...], rows_ref[...]).astype(BF16)

    return pl.pallas_call(
        body,
        out_shape=shape(n, width),
        in_specs=[VMEM] * 2,
        out_specs=VMEM,
        compiler_params=params(),
        cost_estimate=cost(2**21),
    )(place, rows)


def add(*terms):
    total = terms[0].astype(F32)
    for term in terms[1:]:
        total = total + term.astype(F32)
    return total


def first_hop(low, high, axis):
    return lax.ppermute(low, axis, ring(3)), lax.ppermute(high, axis, ring(1))


def second_hop(up, down, axis):
    return lax.ppermute(up, axis, ring(1)), lax.ppermute(down, axis, ring(3))


def cut(total, refs):
    keep_ref, sides_ref, low_ref, high_ref, mark_ref = refs
    n = total.shape[0]
    q = n // 4
    mark_ref[...] = jnp.zeros_like(mark_ref)
    total = total.astype(BF16)
    keep_ref[...] = total[:q]
    sides_ref[:q, :] = total[q : 2 * q]
    low_ref[...] = total[2 * q : 2 * q + q // 2]
    high_ref[...] = total[2 * q + q // 2 : 3 * q]
    sides_ref[q:, :] = total[3 * q :]


def cut_shapes(n, width):
    return [shape(n // k, width) for k in (4, 2, 8, 8)] + [MARK]


def combine(own, received):
    n, width = own.shape

    def body(own_ref, left, right, *refs):
        cut(add(own_ref[...], left[...], right[...]), refs)

    return pl.pallas_call(
        body,
        out_shape=cut_shapes(n, width),
        in_specs=[VMEM] * 3,
        out_specs=[VMEM] * 5,
        compiler_params=params(),
        cost_estimate=cost(8 * n * width),
    )(own, *received)


def in_hbm(array):
    return pltpu.with_memory_space_constraint(array, pltpu.HBM)


def sum_cores(terms):
    terms = lax.all_to_all(terms, "core", split_axis=0, concat_axis=0, tiled=True)
    n = terms.shape[0] // 2
    return add(terms[:n], terms[n:]).astype(BF16)


def local(tokens, out_grad, gate, region, w_in, w_out):
    expert = lax.axis_index("expert").astype(jnp.int32)
    x, y, core = (lax.axis_index(a).astype(jnp.int32) for a in ("x", "y", "core"))
    scale = 1.0 / math.sqrt(float(tokens.shape[0] * lax.axis_size(("y", "x", "core"))))
    order = jnp.array(ORDER, jnp.int32)
    every = jnp.arange(4, dtype=jnp.int32)
    by_x = ((((y + every[None, :]) % 4) * 4 + (x + order[:, None]) % 4) * 2 + core).reshape(16)
    by_y = ((((y + order[:, None]) % 4) * 4 + (x + every[None, :]) % 4) * 2 + core).reshape(16)
    same = jnp.array([INVERSE[q] * 4 + ORDER[p] for p in range(4) for q in range(4)], jnp.int32)
    table = jnp.concatenate([by_x, by_y, same, (expert - every) % 4, core[None]])
    weight_in, weight_out, mark = fetch_weights(table, in_hbm(w_in[0]), in_hbm(w_out[0]))

    place, *send_x = dispatch_tokens(
        expert[None], in_hbm(region.reshape(1, -1)), in_hbm(tokens)
    )
    send_d = dispatch_grads(expert[None], place, gate.reshape(1, -1), out_grad, ())

    def to_owner(parts):
        return [parts[0]] + [lax.ppermute(parts[r], "expert", ring(r)) for r in (1, 2, 3)]

    own_x = to_owner(send_x)
    own_d = to_owner(send_d)
    own_x[0] = after(own_x[0], mark, send_d[0])
    own_x[2] = after(own_x[2], own_d[2])
    both_x = own_x + [swap_core(p) for p in own_x]
    act, slope, rows_x, mark = forward(table, both_x, weight_in)
    own_d = [after(part, mark) for part in own_d]
    both_d = own_d + [swap_core(p) for p in own_d]

    out_low, out_high, rows_d, mark = outer_first(table, act, both_d)
    hop = first_hop(out_low, out_high, "x")
    pre_a, in_low, in_high, mark = backward(
        table, rows_d, rows_x, slope, weight_out, 0, 1, (mark,)
    )
    out_sides, out_own, mark = outer_rest(act, rows_d, (mark,))
    in_hop = first_hop(in_low, in_high, "y")
    pre_b, in_sides, mark = backward(table, rows_d, rows_x, slope, weight_out, 1, 2, (mark,))
    *pair, mark = join((after(out_sides, mark), hop))
    out_parts = second_hop(*pair, "x")
    *pair, mark = join((after(in_sides, mark), in_hop))
    in_parts = second_hop(*pair, "y")
    pre_c, in_own, mark = backward(table, rows_d, rows_x, slope, weight_out, 3, 1, (mark,))
    own = sum_cores(row_gradients(table, (pre_a, pre_b, pre_c), weight_in))
    out_keep, out_sides, low, high, mark = combine(out_own, out_parts)
    out_hop = first_hop(low, high, "y")
    back = lax.all_to_all(after(own, mark), "expert", split_axis=0, concat_axis=0, tiled=True)
    in_keep, in_sides, low, high, mark = combine(after(in_own, mark), in_parts)
    in_hop = first_hop(low, high, "x")
    *pairs, _ = join((out_sides, out_hop), (in_sides, in_hop))
    out_parts = second_hop(*pairs[:2], "y")
    in_parts = second_hop(*pairs[2:], "x")
    grad_out = add(out_keep, *out_parts) * scale
    grad_in = add(in_keep, *in_parts) * scale
    token_grad = restore_order(place, back)
    return token_grad, grad_in[None], grad_out[None]


def solution(mesh):
    chips = Mesh(mesh.devices.reshape(4, 4, 2, 4), ("y", "x", "core", "expert"))
    rows = ("y", "x", "core", "expert")
    plane = ("y", "x", "core")
    return jax.shard_map(
        local,
        mesh=chips,
        in_specs=(
            P(rows, None),
            P(rows, None),
            P(rows),
            P(rows, None),
            P("expert", None, None),
            P("expert", None, None),
        ),
        out_specs=(P(rows, None), P("expert", plane, None), P("expert", plane, None)),
        check_vma=False,
    )
```

```python
import math

import jax
import jax.numpy as jnp
from jax import lax
from jax.experimental import pallas as pl
from jax.experimental.pallas import tpu as pltpu
from jax.sharding import Mesh, PartitionSpec as P

BF16 = jnp.bfloat16
F32 = jnp.float32
VMEM_LIMIT = 18 * 1024 * 1024
ORDER = (2, 1, 3, 0)
INVERSE = (3, 1, 0, 2)


def ring(step):
    return [(i, (i + step) % 4) for i in range(4)]


def swap_core(array):
    return lax.ppermute(array, "core", [(0, 1), (1, 0)])


def params():
    return pltpu.CompilerParams(vmem_limit_bytes=VMEM_LIMIT)


def cost(nbytes=1024):
    return pl.CostEstimate(flops=0, bytes_accessed=int(nbytes), transcendentals=0)


def shape(rows, cols, dtype=BF16):
    return jax.ShapeDtypeStruct((rows, cols), dtype)


def dot_nt(a, b):
    return lax.dot_general(a, b, (((1,), (1,)), ((), ())), preferred_element_type=F32)


def dot_nn(a, b):
    return lax.dot_general(a, b, (((1,), (0,)), ((), ())), preferred_element_type=F32)


def dot_tn(a, b):
    return lax.dot_general(a, b, (((0,), (0,)), ((), ())), preferred_element_type=F32)


def gelu_parts(pre_act):
    root_two_pi = 0.7978845608028654
    square = pre_act * pre_act
    inner = pre_act * (root_two_pi + root_two_pi * 0.044715 * square)
    halved = 0.5 + 0.5 * jnp.tanh(inner)
    value = pre_act * halved
    slope_of_inner = 2.0 * root_two_pi + 6.0 * root_two_pi * 0.044715 * square
    return value, halved + value * (1.0 - halved) * slope_of_inner


VMEM = pl.BlockSpec(memory_space=pltpu.VMEM)
SMEM = pl.BlockSpec(memory_space=pltpu.SMEM)
ANY = pl.BlockSpec(memory_space=pl.ANY)


def bucket(where_ref, r):
    return pl.ds(pl.multiple_of(jnp.bitwise_and(where_ref[0] + r, 3) * 128, 128), 128)


def dispatch_tokens(where, region, tokens):
    n, width = tokens.shape

    def body(where_ref, region_hbm, tok_hbm, place_ref, *refs):
        outs, (region_ref, tok_ref, sems) = refs[:4], refs[4:]
        copies = [
            pltpu.make_async_copy(region_hbm, region_ref, sems.at[0]),
            pltpu.make_async_copy(tok_hbm, tok_ref, sems.at[1]),
        ]
        for copy in copies:
            copy.start()
        upper = (
            lax.broadcasted_iota(jnp.int32, (n, n), 0) < lax.broadcasted_iota(jnp.int32, (n, n), 1)
        ).astype(F32)
        copies[0].wait()
        dest = region_ref[...]
        onehot = (dest == lax.broadcasted_iota(jnp.int32, (8, n), 0)).astype(F32)
        before = dot_nn(onehot.astype(BF16), upper.astype(BF16))
        rank = jnp.sum(before * onehot, axis=0, keepdims=True).astype(jnp.int32)
        slot = dest * 128 + rank
        place = (slot == lax.broadcasted_iota(jnp.int32, (512, n), 0)).astype(F32).astype(BF16)
        place_ref[...] = place
        copies[1].wait()
        for r, out in enumerate(outs):
            out[...] = dot_nn(place_ref[bucket(where_ref, r), :], tok_ref[...]).astype(BF16)

    return pl.pallas_call(
        body,
        out_shape=[shape(512, n)] + [shape(128, width)] * 4,
        in_specs=[SMEM] + [HBM] * 2,
        out_specs=[VMEM] * 5,
        scratch_shapes=[
            pltpu.VMEM((1, n), jnp.int32),
            pltpu.VMEM((n, width), BF16),
            pltpu.SemaphoreType.DMA((2,)),
        ],
        compiler_params=params(),
        cost_estimate=cost(4 * n * width * 2),
    )(where, region, tokens)


def dispatch_grads(where, place, gate, grads, deps):
    n, width = grads.shape

    def body(where_ref, place_ref, gate_ref, grad_ref, *refs):
        outs = refs[len(deps) :]
        column = jnp.transpose(jnp.broadcast_to(gate_ref[...], (128, n)))[:, :1]
        scaled = (column * grad_ref[...].astype(F32)).astype(BF16)
        for r, out in enumerate(outs):
            out[...] = dot_nn(place_ref[bucket(where_ref, r), :], scaled).astype(BF16)

    return pl.pallas_call(
        body,
        out_shape=[shape(128, width)] * 4,
        in_specs=[SMEM] + [VMEM] * 3 + [ANY] * len(deps),
        out_specs=[VMEM] * 4,
        compiler_params=params(),
        cost_estimate=cost(4 * n * width * 2),
    )(where, place, gate, grads, *deps)


HBM = pl.BlockSpec(memory_space=pltpu.HBM)


def fetch_weights(table, w_in, w_out):
    count, width = 16, w_in.shape[1]

    def body(table_ref, in_hbm_ref, out_hbm_ref, in_ref, out_ref, mark_ref, sems):
        mark_ref[...] = jnp.zeros_like(mark_ref)
        copies = []
        for k in range(count):
            for side, (source, target) in enumerate(((in_hbm_ref, in_ref), (out_hbm_ref, out_ref))):
                block = pl.multiple_of(table_ref[count * side + k] * 128, 128)
                copies.append(
                    pltpu.make_async_copy(
                        source.at[pl.ds(block, 128), :],
                        target.at[pl.ds(k * 128, 128), :],
                        sems.at[side, k],
                    )
                )
        for copy in copies:
            copy.start()
        for copy in copies:
            copy.wait()

    return pl.pallas_call(
        body,
        out_shape=[pltpu.VMEM((count * 128, width), BF16)] * 2 + [MARK],
        in_specs=[SMEM] + [HBM] * 2,
        out_specs=[VMEM] * 3,
        scratch_shapes=[pltpu.SemaphoreType.DMA((2, count))],
        compiler_params=params(),
        cost_estimate=cost(2**24),
    )(table, w_in, w_out)


def group_rows(index):
    return pl.ds(pl.multiple_of(index * 512, 512), 512)


def after(array, *others):
    def body(*refs):
        del refs

    return pl.pallas_call(
        body,
        in_specs=[ANY] * (1 + len(others)),
        out_specs=ANY,
        out_shape=jax.ShapeDtypeStruct(array.shape, array.dtype),
        input_output_aliases={0: 0},
        compiler_params=params(),
        cost_estimate=cost(),
    )(array, *others)


MARK = jax.ShapeDtypeStruct((8, 128), F32)


def merge(table_ref, part_refs, all_ref):
    for k, ref in enumerate(part_refs):
        begin = pl.multiple_of(k // 4 * 512 + table_ref[48 + k % 4] * 128, 128)
        all_ref[pl.ds(begin, 128), :] = ref[...]


def forward(table, parts, weight):
    width = weight.shape[1]
    tok = 128 * len(parts)

    def body(table_ref, *refs):
        part_refs, weight_ref = refs[: len(parts)], refs[len(parts)]
        act_ref, slope_ref, all_ref, mark_ref = refs[len(parts) + 1 :]
        step = pl.program_id(0)

        @pl.when(step == 0)
        def _():
            mark_ref[...] = jnp.zeros_like(mark_ref)
            merge(table_ref, part_refs, all_ref)

        group = group_rows(step)
        for begin in range(0, tok, 256):
            cols = slice(begin, begin + 256)
            act, slope = gelu_parts(dot_nt(weight_ref[group, :], all_ref[cols, :]))
            act_ref[group, cols] = act.astype(BF16)
            slope_ref[group, cols] = slope.astype(BF16)

    return pl.pallas_call(
        body,
        grid=(4,),
        in_specs=[SMEM] + [VMEM] * (len(parts) + 1),
        out_specs=[VMEM] * 4,
        out_shape=[pltpu.VMEM((2048, tok), BF16)] * 2 + [shape(tok, width), MARK],
        compiler_params=params(),
        cost_estimate=cost(2**24),
    )(table, *parts, weight)


def outer_first(table, act, parts):
    width = parts[0].shape[1]
    tok = 128 * len(parts)

    def body(table_ref, act_ref, *refs):
        part_refs, (low_ref, high_ref, all_ref, mark_ref) = refs[: len(parts)], refs[len(parts) :]
        mark_ref[...] = jnp.zeros_like(mark_ref)
        merge(table_ref, part_refs, all_ref)
        low_ref[...] = dot_nn(act_ref[:256, :], all_ref[...]).astype(BF16)
        high_ref[...] = dot_nn(act_ref[256:512, :], all_ref[...]).astype(BF16)

    return pl.pallas_call(
        body,
        in_specs=[SMEM] + [VMEM] * (len(parts) + 1),
        out_specs=[VMEM] * 4,
        out_shape=[shape(256, width)] * 2 + [shape(tok, width), MARK],
        compiler_params=params(),
        cost_estimate=cost(2**22),
    )(table, act, *parts)


def outer_rest(act, rows, deps):
    width = rows.shape[1]

    def body(act_ref, rows_ref, *refs):
        sides_ref, own_ref, mark_ref = refs[len(deps) :]
        mark_ref[...] = jnp.zeros_like(mark_ref)
        for k, out in enumerate((sides_ref.at[:512], sides_ref.at[512:], own_ref)):
            group = act_ref[(k + 1) * 512 : (k + 2) * 512, :]
            out[...] = dot_nn(group, rows_ref[...]).astype(BF16)

    return pl.pallas_call(
        body,
        in_specs=[VMEM] * 2 + [ANY] * len(deps),
        out_specs=[VMEM] * 3,
        out_shape=[shape(1024, width), shape(512, width), MARK],
        compiler_params=params(),
        cost_estimate=cost(2**23),
    )(act, rows, *deps)


def backward(table, grads, rows, slope, weight, first, count, deps):
    tok, width = rows.shape
    split = first == 0

    def body(table_ref, grads_ref, rows_ref, slope_ref, weight_ref, *refs):
        pre_ref, *outs, mark_ref = refs[len(deps) :]
        mark_ref[...] = jnp.zeros_like(mark_ref)
        step = pl.program_id(0)
        group = group_rows(step + first)
        for begin in range(0, tok, 256):
            cols = slice(begin, begin + 256)
            act_grad = dot_nt(weight_ref[group, :], grads_ref[cols, :])
            for q in range(4):
                block = pl.multiple_of(table_ref[32 + 4 * (step + first) + q] * 128, 128)
                place = pl.multiple_of(step * 512 + q * 128, 128)
                part = act_grad[q * 128 : (q + 1) * 128] * slope_ref[pl.ds(block, 128), cols].astype(F32)
                pre_ref[pl.ds(place, 128), cols] = part.astype(BF16)
        if split:
            for k, out in enumerate(outs):
                out[...] = dot_nn(pre_ref[k * 256 : (k + 1) * 256, :], rows_ref[...]).astype(BF16)
        else:
            product = dot_nn(pre_ref[group_rows(step), :], rows_ref[...])
            outs[0][group_rows(step), :] = product.astype(BF16)

    return pl.pallas_call(
        body,
        grid=(count,),
        in_specs=[SMEM] + [VMEM] * 4 + [ANY] * len(deps),
        out_specs=[VMEM] * (4 if split else 3),
        out_shape=[shape(512 * count, tok)]
        + ([shape(256, width)] * 2 if split else [shape(512 * count, width)])
        + [MARK],
        compiler_params=params(),
        cost_estimate=cost(2**20 * (2 + 4 * count)),
    )(table, grads, rows, slope, weight, *deps)


def row_gradients(table, pre, weight):
    width = weight.shape[1]
    rows = 512

    def body(table_ref, a_ref, b_ref, c_ref, weight_ref, out_ref, w_ref, total):
        step = pl.program_id(0)
        for q in range(4):
            block = pl.multiple_of(table_ref[32 + 4 * step + q] * 128, 128)
            w_ref[q * 128 : (q + 1) * 128, :] = weight_ref[pl.ds(block, 128), :]

        @pl.when(step == 0)
        def _():
            total[...] = dot_tn(a_ref[...], w_ref[...])

        @pl.when(jnp.logical_and(step > 0, step < 3))
        def _():
            total[...] += dot_tn(b_ref[group_rows(step - 1), :], w_ref[...])

        @pl.when(step == 3)
        def _():
            final = (total[...] + dot_tn(c_ref[...], w_ref[...])).astype(BF16)
            own = table_ref[52]
            out_ref[group_rows(own), :] = final[:rows]
            out_ref[group_rows(1 - own), :] = final[rows:]

    return pl.pallas_call(
        body,
        grid=(4,),
        in_specs=[SMEM] + [VMEM] * 4,
        out_specs=VMEM,
        out_shape=shape(2 * rows, width),
        scratch_shapes=[pltpu.VMEM((512, width), BF16), pltpu.VMEM((2 * rows, width), F32)],
        compiler_params=params(),
        cost_estimate=cost(2**23 + 2**22),
    )(table, *pre, weight)


def join(*sums):
    n, width = sums[0][0].shape
    h = n // 4

    def body(*refs):
        ins, outs = refs[: 3 * len(sums)], refs[3 * len(sums) :]
        outs[-1][...] = jnp.zeros_like(outs[-1])
        for k in range(len(sums)):
            sides_ref, from_next, from_prev = ins[3 * k : 3 * k + 3]
            up_ref, down_ref = outs[2 * k : 2 * k + 2]
            up_ref[:h, :] = sides_ref[:h, :]
            up_ref[h:, :] = add(sides_ref[h : 2 * h, :], from_prev[...]).astype(BF16)
            down_ref[:h, :] = add(sides_ref[2 * h : 3 * h, :], from_next[...]).astype(BF16)
            down_ref[h:, :] = sides_ref[3 * h :, :]

    return pl.pallas_call(
        body,
        out_shape=[shape(2 * h, width)] * (2 * len(sums)) + [MARK],
        in_specs=[VMEM] * (3 * len(sums)),
        out_specs=[VMEM] * (2 * len(sums) + 1),
        compiler_params=params(),
        cost_estimate=cost(4 * n * width),
    )(*[array for sides, arrived in sums for array in (sides, *arrived)])


def restore_order(place, rows):
    n, width = place.shape[1], rows.shape[1]

    def body(place_ref, rows_ref, out_ref):
        out_ref[...] = dot_tn(place_ref[...], rows_ref[...]).astype(BF16)

    return pl.pallas_call(
        body,
        out_shape=shape(n, width),
        in_specs=[VMEM] * 2,
        out_specs=VMEM,
        compiler_params=params(),
        cost_estimate=cost(2**21),
    )(place, rows)


def add(*terms):
    total = terms[0].astype(F32)
    for term in terms[1:]:
        total = total + term.astype(F32)
    return total


def first_hop(low, high, axis):
    return lax.ppermute(low, axis, ring(3)), lax.ppermute(high, axis, ring(1))


def second_hop(up, down, axis):
    return lax.ppermute(up, axis, ring(1)), lax.ppermute(down, axis, ring(3))


def cut(total, refs):
    keep_ref, sides_ref, low_ref, high_ref, mark_ref = refs
    n = total.shape[0]
    q = n // 4
    mark_ref[...] = jnp.zeros_like(mark_ref)
    total = total.astype(BF16)
    keep_ref[...] = total[:q]
    sides_ref[:q, :] = total[q : 2 * q]
    low_ref[...] = total[2 * q : 2 * q + q // 2]
    high_ref[...] = total[2 * q + q // 2 : 3 * q]
    sides_ref[q:, :] = total[3 * q :]


def cut_shapes(n, width):
    return [shape(n // k, width) for k in (4, 2, 8, 8)] + [MARK]


def combine(own, received):
    n, width = own.shape

    def body(own_ref, left, right, *refs):
        cut(add(own_ref[...], left[...], right[...]), refs)

    return pl.pallas_call(
        body,
        out_shape=cut_shapes(n, width),
        in_specs=[VMEM] * 3,
        out_specs=[VMEM] * 5,
        compiler_params=params(),
        cost_estimate=cost(8 * n * width),
    )(own, *received)


def in_hbm(array):
    return pltpu.with_memory_space_constraint(array, pltpu.HBM)


def sum_cores(terms):
    terms = lax.all_to_all(terms, "core", split_axis=0, concat_axis=0, tiled=True)
    n = terms.shape[0] // 2
    return add(terms[:n], terms[n:]).astype(BF16)


def local(tokens, out_grad, gate, region, w_in, w_out):
    expert = lax.axis_index("expert").astype(jnp.int32)
    x, y, core = (lax.axis_index(a).astype(jnp.int32) for a in ("x", "y", "core"))
    scale = 1.0 / math.sqrt(float(tokens.shape[0] * lax.axis_size(("y", "x", "core"))))
    order = jnp.array(ORDER, jnp.int32)
    every = jnp.arange(4, dtype=jnp.int32)
    by_x = ((((y + every[None, :]) % 4) * 4 + (x + order[:, None]) % 4) * 2 + core).reshape(16)
    by_y = ((((y + order[:, None]) % 4) * 4 + (x + every[None, :]) % 4) * 2 + core).reshape(16)
    same = jnp.array([INVERSE[q] * 4 + ORDER[p] for p in range(4) for q in range(4)], jnp.int32)
    table = jnp.concatenate([by_x, by_y, same, (expert - every) % 4, core[None]])
    weight_in, weight_out, mark = fetch_weights(table, in_hbm(w_in[0]), in_hbm(w_out[0]))

    place, *send_x = dispatch_tokens(
        expert[None], in_hbm(region.reshape(1, -1)), in_hbm(tokens)
    )
    send_d = dispatch_grads(expert[None], place, gate.reshape(1, -1), out_grad, ())

    def to_owner(parts):
        return [parts[0]] + [lax.ppermute(parts[r], "expert", ring(r)) for r in (1, 2, 3)]

    own_x = to_owner(send_x)
    own_d = to_owner(send_d)
    own_x[0] = after(own_x[0], mark, send_d[0])
    both_x = own_x + [swap_core(p) for p in own_x]
    act, slope, rows_x, mark = forward(table, both_x, weight_in)
    own_d = [after(part, mark) for part in own_d]
    both_d = own_d + [swap_core(p) for p in own_d]

    out_low, out_high, rows_d, mark = outer_first(table, act, both_d)
    hop = first_hop(out_low, out_high, "x")
    pre_a, in_low, in_high, mark = backward(
        table, rows_d, rows_x, slope, weight_out, 0, 1, (mark,)
    )
    out_sides, out_own, mark = outer_rest(act, rows_d, (mark,))
    in_hop = first_hop(in_low, in_high, "y")
    pre_b, in_sides, mark = backward(table, rows_d, rows_x, slope, weight_out, 1, 2, (mark,))
    *pair, mark = join((after(out_sides, mark), hop))
    out_parts = second_hop(*pair, "x")
    *pair, mark = join((after(in_sides, mark), in_hop))
    in_parts = second_hop(*pair, "y")
    pre_c, in_own, mark = backward(table, rows_d, rows_x, slope, weight_out, 3, 1, (mark,))
    own = sum_cores(row_gradients(table, (pre_a, pre_b, pre_c), weight_in))
    out_keep, out_sides, low, high, mark = combine(out_own, out_parts)
    out_hop = first_hop(low, high, "y")
    back = lax.all_to_all(after(own, mark), "expert", split_axis=0, concat_axis=0, tiled=True)
    in_keep, in_sides, low, high, mark = combine(after(in_own, mark), in_parts)
    in_hop = first_hop(low, high, "x")
    *pairs, _ = join((out_sides, out_hop), (in_sides, in_hop))
    out_parts = second_hop(*pairs[:2], "y")
    in_parts = second_hop(*pairs[2:], "x")
    grad_out = add(out_keep, *out_parts) * scale
    grad_in = add(in_keep, *in_parts) * scale
    token_grad = restore_order(place, back)
    return token_grad, grad_in[None], grad_out[None]


def solution(mesh):
    chips = Mesh(mesh.devices.reshape(4, 4, 2, 4), ("y", "x", "core", "expert"))
    rows = ("y", "x", "core", "expert")
    plane = ("y", "x", "core")
    return jax.shard_map(
        local,
        mesh=chips,
        in_specs=(
            P(rows, None),
            P(rows, None),
            P(rows),
            P(rows, None),
            P("expert", None, None),
            P("expert", None, None),
        ),
        out_specs=(P(rows, None), P("expert", plane, None), P("expert", plane, None)),
        check_vma=False,
    )
```

```python
import math

import jax
import jax.numpy as jnp
from jax import lax
from jax.experimental import pallas as pl
from jax.experimental.pallas import tpu as pltpu
from jax.sharding import Mesh, PartitionSpec as P

BF16 = jnp.bfloat16
F32 = jnp.float32
VMEM_LIMIT = 18 * 1024 * 1024
ORDER = (2, 1, 3, 0)
INVERSE = (3, 1, 0, 2)


def ring(step):
    return [(i, (i + step) % 4) for i in range(4)]


def swap_core(array):
    return lax.ppermute(array, "core", [(0, 1), (1, 0)])


def params():
    return pltpu.CompilerParams(vmem_limit_bytes=VMEM_LIMIT)


def cost(nbytes=1024):
    return pl.CostEstimate(flops=0, bytes_accessed=int(nbytes), transcendentals=0)


def shape(rows, cols, dtype=BF16):
    return jax.ShapeDtypeStruct((rows, cols), dtype)


def dot_nt(a, b):
    return lax.dot_general(a, b, (((1,), (1,)), ((), ())), preferred_element_type=F32)


def dot_nn(a, b):
    return lax.dot_general(a, b, (((1,), (0,)), ((), ())), preferred_element_type=F32)


def dot_tn(a, b):
    return lax.dot_general(a, b, (((0,), (0,)), ((), ())), preferred_element_type=F32)


def gelu_parts(pre_act):
    root_two_pi = 0.7978845608028654
    square = pre_act * pre_act
    inner = pre_act * (root_two_pi + root_two_pi * 0.044715 * square)
    halved = 0.5 + 0.5 * jnp.tanh(inner)
    value = pre_act * halved
    slope_of_inner = 2.0 * root_two_pi + 6.0 * root_two_pi * 0.044715 * square
    return value, halved + value * (1.0 - halved) * slope_of_inner


VMEM = pl.BlockSpec(memory_space=pltpu.VMEM)
SMEM = pl.BlockSpec(memory_space=pltpu.SMEM)
ANY = pl.BlockSpec(memory_space=pl.ANY)


def bucket(where_ref, r):
    return pl.ds(pl.multiple_of(jnp.bitwise_and(where_ref[0] + r, 3) * 128, 128), 128)


def dispatch_tokens(where, region, tokens):
    n, width = tokens.shape

    def body(where_ref, region_hbm, tok_hbm, place_ref, *refs):
        outs, (region_ref, tok_ref, sems) = refs[:4], refs[4:]
        copies = [
            pltpu.make_async_copy(region_hbm, region_ref, sems.at[0]),
            pltpu.make_async_copy(tok_hbm, tok_ref, sems.at[1]),
        ]
        for copy in copies:
            copy.start()
        upper = (
            lax.broadcasted_iota(jnp.int32, (n, n), 0) < lax.broadcasted_iota(jnp.int32, (n, n), 1)
        ).astype(F32)
        copies[0].wait()
        dest = region_ref[...]
        onehot = (dest == lax.broadcasted_iota(jnp.int32, (8, n), 0)).astype(F32)
        before = dot_nn(onehot.astype(BF16), upper.astype(BF16))
        rank = jnp.sum(before * onehot, axis=0, keepdims=True).astype(jnp.int32)
        slot = dest * 128 + rank
        place = (slot == lax.broadcasted_iota(jnp.int32, (512, n), 0)).astype(F32).astype(BF16)
        place_ref[...] = place
        copies[1].wait()
        for r, out in enumerate(outs):
            out[...] = dot_nn(place_ref[bucket(where_ref, r), :], tok_ref[...]).astype(BF16)

    return pl.pallas_call(
        body,
        out_shape=[shape(512, n)] + [shape(128, width)] * 4,
        in_specs=[SMEM] + [HBM] * 2,
        out_specs=[VMEM] * 5,
        scratch_shapes=[
            pltpu.VMEM((1, n), jnp.int32),
            pltpu.VMEM((n, width), BF16),
            pltpu.SemaphoreType.DMA((2,)),
        ],
        compiler_params=params(),
        cost_estimate=cost(4 * n * width * 2),
    )(where, region, tokens)


def dispatch_grads(where, place, gate, grads, deps):
    n, width = grads.shape

    def body(where_ref, place_ref, gate_ref, grad_ref, *refs):
        outs = refs[len(deps) :]
        column = jnp.transpose(jnp.broadcast_to(gate_ref[...], (128, n)))[:, :1]
        scaled = (column * grad_ref[...].astype(F32)).astype(BF16)
        for r, out in enumerate(outs):
            out[...] = dot_nn(place_ref[bucket(where_ref, r), :], scaled).astype(BF16)

    return pl.pallas_call(
        body,
        out_shape=[shape(128, width)] * 4,
        in_specs=[SMEM] + [VMEM] * 3 + [ANY] * len(deps),
        out_specs=[VMEM] * 4,
        compiler_params=params(),
        cost_estimate=cost(4 * n * width * 2),
    )(where, place, gate, grads, *deps)


HBM = pl.BlockSpec(memory_space=pltpu.HBM)


def fetch_weights(table, w_in, w_out):
    count, width = 16, w_in.shape[1]

    def body(table_ref, in_hbm_ref, out_hbm_ref, in_ref, out_ref, mark_ref, sems):
        mark_ref[...] = jnp.zeros_like(mark_ref)
        copies = []
        for k in range(count):
            for side, (source, target) in enumerate(((in_hbm_ref, in_ref), (out_hbm_ref, out_ref))):
                block = pl.multiple_of(table_ref[count * side + k] * 128, 128)
                copies.append(
                    pltpu.make_async_copy(
                        source.at[pl.ds(block, 128), :],
                        target.at[pl.ds(k * 128, 128), :],
                        sems.at[side, k],
                    )
                )
        for copy in copies:
            copy.start()
        for copy in copies:
            copy.wait()

    return pl.pallas_call(
        body,
        out_shape=[pltpu.VMEM((count * 128, width), BF16)] * 2 + [MARK],
        in_specs=[SMEM] + [HBM] * 2,
        out_specs=[VMEM] * 3,
        scratch_shapes=[pltpu.SemaphoreType.DMA((2, count))],
        compiler_params=params(),
        cost_estimate=cost(2**24),
    )(table, w_in, w_out)


def group_rows(index):
    return pl.ds(pl.multiple_of(index * 512, 512), 512)


def after(array, *others):
    def body(*refs):
        del refs

    return pl.pallas_call(
        body,
        in_specs=[ANY] * (1 + len(others)),
        out_specs=ANY,
        out_shape=jax.ShapeDtypeStruct(array.shape, array.dtype),
        input_output_aliases={0: 0},
        compiler_params=params(),
        cost_estimate=cost(),
    )(array, *others)


MARK = jax.ShapeDtypeStruct((8, 128), F32)


def merge(table_ref, part_refs, all_ref):
    for k, ref in enumerate(part_refs):
        begin = pl.multiple_of(k // 4 * 512 + table_ref[48 + k % 4] * 128, 128)
        all_ref[pl.ds(begin, 128), :] = ref[...]


def forward(table, parts, weight):
    width = weight.shape[1]
    tok = 128 * len(parts)

    def body(table_ref, *refs):
        part_refs, weight_ref = refs[: len(parts)], refs[len(parts)]
        act_ref, slope_ref, all_ref, mark_ref = refs[len(parts) + 1 :]
        step = pl.program_id(0)

        @pl.when(step == 0)
        def _():
            mark_ref[...] = jnp.zeros_like(mark_ref)
            merge(table_ref, part_refs, all_ref)

        group = group_rows(step)
        for begin in range(0, tok, 256):
            cols = slice(begin, begin + 256)
            act, slope = gelu_parts(dot_nt(weight_ref[group, :], all_ref[cols, :]))
            act_ref[group, cols] = act.astype(BF16)
            slope_ref[group, cols] = slope.astype(BF16)

    return pl.pallas_call(
        body,
        grid=(4,),
        in_specs=[SMEM] + [VMEM] * (len(parts) + 1),
        out_specs=[VMEM] * 4,
        out_shape=[pltpu.VMEM((2048, tok), BF16)] * 2 + [shape(tok, width), MARK],
        compiler_params=params(),
        cost_estimate=cost(2**24),
    )(table, *parts, weight)


def outer_first(table, act, parts):
    width = parts[0].shape[1]
    tok = 128 * len(parts)

    def body(table_ref, act_ref, *refs):
        part_refs, (low_ref, high_ref, all_ref, mark_ref) = refs[: len(parts)], refs[len(parts) :]
        mark_ref[...] = jnp.zeros_like(mark_ref)
        merge(table_ref, part_refs, all_ref)
        low_ref[...] = dot_nn(act_ref[:256, :], all_ref[...]).astype(BF16)
        high_ref[...] = dot_nn(act_ref[256:512, :], all_ref[...]).astype(BF16)

    return pl.pallas_call(
        body,
        in_specs=[SMEM] + [VMEM] * (len(parts) + 1),
        out_specs=[VMEM] * 4,
        out_shape=[shape(256, width)] * 2 + [shape(tok, width), MARK],
        compiler_params=params(),
        cost_estimate=cost(2**22),
    )(table, act, *parts)


def outer_rest(act, rows, deps):
    width = rows.shape[1]

    def body(act_ref, rows_ref, *refs):
        sides_ref, own_ref, mark_ref = refs[len(deps) :]
        mark_ref[...] = jnp.zeros_like(mark_ref)
        for k, out in enumerate((sides_ref.at[:512], sides_ref.at[512:], own_ref)):
            group = act_ref[(k + 1) * 512 : (k + 2) * 512, :]
            out[...] = dot_nn(group, rows_ref[...]).astype(BF16)

    return pl.pallas_call(
        body,
        in_specs=[VMEM] * 2 + [ANY] * len(deps),
        out_specs=[VMEM] * 3,
        out_shape=[shape(1024, width), shape(512, width), MARK],
        compiler_params=params(),
        cost_estimate=cost(2**23),
    )(act, rows, *deps)


def backward(table, grads, rows, slope, weight, first, count, deps):
    tok, width = rows.shape
    split = first == 0

    def body(table_ref, grads_ref, rows_ref, slope_ref, weight_ref, *refs):
        pre_ref, *outs, mark_ref = refs[len(deps) :]
        mark_ref[...] = jnp.zeros_like(mark_ref)
        step = pl.program_id(0)
        group = group_rows(step + first)
        for begin in range(0, tok, 256):
            cols = slice(begin, begin + 256)
            act_grad = dot_nt(weight_ref[group, :], grads_ref[cols, :])
            for q in range(4):
                block = pl.multiple_of(table_ref[32 + 4 * (step + first) + q] * 128, 128)
                place = pl.multiple_of(step * 512 + q * 128, 128)
                part = act_grad[q * 128 : (q + 1) * 128] * slope_ref[pl.ds(block, 128), cols].astype(F32)
                pre_ref[pl.ds(place, 128), cols] = part.astype(BF16)
        if split:
            for k, out in enumerate(outs):
                out[...] = dot_nn(pre_ref[k * 256 : (k + 1) * 256, :], rows_ref[...]).astype(BF16)
        else:
            product = dot_nn(pre_ref[group_rows(step), :], rows_ref[...])
            outs[0][group_rows(step), :] = product.astype(BF16)

    return pl.pallas_call(
        body,
        grid=(count,),
        in_specs=[SMEM] + [VMEM] * 4 + [ANY] * len(deps),
        out_specs=[VMEM] * (4 if split else 3),
        out_shape=[shape(512 * count, tok)]
        + ([shape(256, width)] * 2 if split else [shape(512 * count, width)])
        + [MARK],
        compiler_params=params(),
        cost_estimate=cost(2**20 * (2 + 4 * count)),
    )(table, grads, rows, slope, weight, *deps)


def row_gradients(table, pre, weight):
    width = weight.shape[1]
    rows = 512

    def body(table_ref, a_ref, b_ref, c_ref, weight_ref, out_ref, w_ref, total):
        step = pl.program_id(0)
        for q in range(4):
            block = pl.multiple_of(table_ref[32 + 4 * step + q] * 128, 128)
            w_ref[q * 128 : (q + 1) * 128, :] = weight_ref[pl.ds(block, 128), :]

        @pl.when(step == 0)
        def _():
            total[...] = dot_tn(a_ref[...], w_ref[...])

        @pl.when(jnp.logical_and(step > 0, step < 3))
        def _():
            total[...] += dot_tn(b_ref[group_rows(step - 1), :], w_ref[...])

        @pl.when(step == 3)
        def _():
            final = (total[...] + dot_tn(c_ref[...], w_ref[...])).astype(BF16)
            own = table_ref[52]
            out_ref[group_rows(own), :] = final[:rows]
            out_ref[group_rows(1 - own), :] = final[rows:]

    return pl.pallas_call(
        body,
        grid=(4,),
        in_specs=[SMEM] + [VMEM] * 4,
        out_specs=VMEM,
        out_shape=shape(2 * rows, width),
        scratch_shapes=[pltpu.VMEM((512, width), BF16), pltpu.VMEM((2 * rows, width), F32)],
        compiler_params=params(),
        cost_estimate=cost(2**23 + 2**22),
    )(table, *pre, weight)


def join(*sums):
    n, width = sums[0][0].shape
    h = n // 4

    def body(*refs):
        ins, outs = refs[: 3 * len(sums)], refs[3 * len(sums) :]
        outs[-1][...] = jnp.zeros_like(outs[-1])
        for k in range(len(sums)):
            sides_ref, from_next, from_prev = ins[3 * k : 3 * k + 3]
            up_ref, down_ref = outs[2 * k : 2 * k + 2]
            up_ref[:h, :] = sides_ref[:h, :]
            up_ref[h:, :] = add(sides_ref[h : 2 * h, :], from_prev[...]).astype(BF16)
            down_ref[:h, :] = add(sides_ref[2 * h : 3 * h, :], from_next[...]).astype(BF16)
            down_ref[h:, :] = sides_ref[3 * h :, :]

    return pl.pallas_call(
        body,
        out_shape=[shape(2 * h, width)] * (2 * len(sums)) + [MARK],
        in_specs=[VMEM] * (3 * len(sums)),
        out_specs=[VMEM] * (2 * len(sums) + 1),
        compiler_params=params(),
        cost_estimate=cost(4 * n * width),
    )(*[array for sides, arrived in sums for array in (sides, *arrived)])


def restore_order(place, rows):
    n, width = place.shape[1], rows.shape[1]

    def body(place_ref, rows_ref, out_ref):
        out_ref[...] = dot_tn(place_ref[...], rows_ref[...]).astype(BF16)

    return pl.pallas_call(
        body,
        out_shape=shape(n, width),
        in_specs=[VMEM] * 2,
        out_specs=VMEM,
        compiler_params=params(),
        cost_estimate=cost(2**21),
    )(place, rows)


def add(*terms):
    total = terms[0].astype(F32)
    for term in terms[1:]:
        total = total + term.astype(F32)
    return total


def first_hop(low, high, axis):
    return lax.ppermute(low, axis, ring(3)), lax.ppermute(high, axis, ring(1))


def second_hop(up, down, axis):
    return lax.ppermute(up, axis, ring(1)), lax.ppermute(down, axis, ring(3))


def cut(total, refs):
    keep_ref, sides_ref, low_ref, high_ref, mark_ref = refs
    n = total.shape[0]
    q = n // 4
    mark_ref[...] = jnp.zeros_like(mark_ref)
    total = total.astype(BF16)
    keep_ref[...] = total[:q]
    sides_ref[:q, :] = total[q : 2 * q]
    low_ref[...] = total[2 * q : 2 * q + q // 2]
    high_ref[...] = total[2 * q + q // 2 : 3 * q]
    sides_ref[q:, :] = total[3 * q :]


def cut_shapes(n, width):
    return [shape(n // k, width) for k in (4, 2, 8, 8)] + [MARK]


def combine(own, received):
    n, width = own.shape

    def body(own_ref, left, right, *refs):
        cut(add(own_ref[...], left[...], right[...]), refs)

    return pl.pallas_call(
        body,
        out_shape=cut_shapes(n, width),
        in_specs=[VMEM] * 3,
        out_specs=[VMEM] * 5,
        compiler_params=params(),
        cost_estimate=cost(8 * n * width),
    )(own, *received)


def in_hbm(array):
    return pltpu.with_memory_space_constraint(array, pltpu.HBM)


def sum_cores(terms):
    terms = lax.all_to_all(terms, "core", split_axis=0, concat_axis=0, tiled=True)
    n = terms.shape[0] // 2
    return add(terms[:n], terms[n:]).astype(BF16)


def local(tokens, out_grad, gate, region, w_in, w_out):
    expert = lax.axis_index("expert").astype(jnp.int32)
    x, y, core = (lax.axis_index(a).astype(jnp.int32) for a in ("x", "y", "core"))
    scale = 1.0 / math.sqrt(float(tokens.shape[0] * lax.axis_size(("y", "x", "core"))))
    order = jnp.array(ORDER, jnp.int32)
    every = jnp.arange(4, dtype=jnp.int32)
    by_x = ((((y + every[None, :]) % 4) * 4 + (x + order[:, None]) % 4) * 2 + core).reshape(16)
    by_y = ((((y + order[:, None]) % 4) * 4 + (x + every[None, :]) % 4) * 2 + core).reshape(16)
    same = jnp.array([INVERSE[q] * 4 + ORDER[p] for p in range(4) for q in range(4)], jnp.int32)
    table = jnp.concatenate([by_x, by_y, same, (expert - every) % 4, core[None]])
    weight_in, weight_out, mark = fetch_weights(table, in_hbm(w_in[0]), in_hbm(w_out[0]))

    place, *send_x = dispatch_tokens(
        expert[None], in_hbm(region.reshape(1, -1)), in_hbm(tokens)
    )
    send_d = dispatch_grads(expert[None], place, gate.reshape(1, -1), out_grad, ())

    def to_owner(parts):
        return [parts[0]] + [lax.ppermute(parts[r], "expert", ring(r)) for r in (1, 2, 3)]

    own_x = to_owner(send_x)
    own_d = to_owner(send_d)
    own_x[0] = after(own_x[0], mark, send_d[0])
    both_x = own_x + [swap_core(p) for p in own_x]
    act, slope, rows_x, mark = forward(table, both_x, weight_in)
    own_d = [after(part, mark) for part in own_d]
    both_d = own_d + [swap_core(p) for p in own_d]

    out_low, out_high, rows_d, mark = outer_first(table, act, both_d)
    hop = first_hop(out_low, out_high, "x")
    pre_a, in_low, in_high, mark = backward(
        table, rows_d, rows_x, slope, weight_out, 0, 1, (mark,)
    )
    out_sides, out_own, mark = outer_rest(act, rows_d, (mark,))
    in_hop = first_hop(in_low, in_high, "y")
    pre_b, in_sides, mark = backward(table, rows_d, rows_x, slope, weight_out, 1, 2, (mark,))
    *pair, mark = join((after(out_sides, mark), hop))
    out_parts = second_hop(*pair, "x")
    *pair, mark = join((after(in_sides, mark), in_hop))
    in_parts = second_hop(*pair, "y")
    pre_c, in_own, mark = backward(table, rows_d, rows_x, slope, weight_out, 3, 1, (mark,))
    own = sum_cores(row_gradients(table, (pre_a, pre_b, pre_c), weight_in))
    out_keep, out_sides, low, high, mark = combine(out_own, out_parts)
    out_hop = first_hop(low, high, "y")
    back = lax.all_to_all(after(own, mark), "expert", split_axis=0, concat_axis=0, tiled=True)
    in_keep, in_sides, low, high, mark = combine(after(in_own, mark), in_parts)
    in_hop = first_hop(low, high, "x")
    *pair, mark = join((out_sides, out_hop))
    out_parts = second_hop(*pair, "y")
    *pair, _ = join((in_sides, in_hop))
    in_parts = second_hop(*pair, "x")
    grad_out = add(out_keep, *out_parts) * scale
    grad_in = add(in_keep, *in_parts) * scale
    token_grad = restore_order(place, back)
    return token_grad, grad_in[None], grad_out[None]


def solution(mesh):
    chips = Mesh(mesh.devices.reshape(4, 4, 2, 4), ("y", "x", "core", "expert"))
    rows = ("y", "x", "core", "expert")
    plane = ("y", "x", "core")
    return jax.shard_map(
        local,
        mesh=chips,
        in_specs=(
            P(rows, None),
            P(rows, None),
            P(rows),
            P(rows, None),
            P("expert", None, None),
            P("expert", None, None),
        ),
        out_specs=(P(rows, None), P("expert", plane, None), P("expert", plane, None)),
        check_vma=False,
    )
```
